512 devices in a mesh: user: 32 (over z_lo, x, core), item: 16 (over z_hi, y).
Axes of the slice: x: 4, y: 8, z: 8 (z_hi: 2, z_lo: 4; z = z_hi * 4 + z_lo), core: 2. Of those that a mesh axis runs over, the one named last changes fastest.
Arguments:
- user_x: bfloat16 [131072, 512], P(('user', 'item')), may hold values from -120 to 120
- item_x: bfloat16 [131072, 512], P(('user', 'item')), may hold values from -6 to 6
- lin_proj: bfloat16 [131072, 256], P(('user', 'item')), may hold values from -0.015625 to 0.015625
- tile_lists: int32 [512, 16], P('user'), may hold values from 0 to 2, as said below
- w_q: bfloat16 [512, 512], replicated, may hold values from -0.25 to 0.25
- w_k: bfloat16 [512, 512], replicated, may hold values from -0.25 to 0.25
- w_v: bfloat16 [512, 512], replicated, may hold values from -0.25 to 0.25
- w_o: bfloat16 [512, 512], replicated, may hold values from -1 to 1
- cotangent: bfloat16 [131072, 512], P(('user', 'item')), may hold values from -6 to 6
Outputs:
- updated: bfloat16 [131072, 512], P(('user', 'item'))
- user_grad: bfloat16 [131072, 512], P(('user', 'item'))
- item_grad: bfloat16 [131072, 512], P(('user', 'item'))
The draws below stay inside these ranges and needn't reach their ends.
Inputs may be any that keep to these rules, and one draw needn't show every extreme that they name: `tile_lists`: A value below 2 names a tile of item device j of block b's group; 2 means no tile from it. Every block takes at least one tile, and in every group of 16 blocks some block takes a tile from every item device of the group.
All inputs are finite; a program needn't handle non-finite values.
Results may differ from the reference program's by a relative error of at most 0.009.
Values may be sent and summed in bfloat16 or wider, within the bound.
A program may use at most 128 MiB of HBM per device.

```python
import jax
import jax.numpy as jnp
from jax import lax

D = 512
HEADS = 8
HEAD = 64
RANK = 256
TILE = 128
UDEV = 256
TDEV = 2
IDEV = 256
OWNERS = 16
BLOCKS = 512
USERS = 131072
ITEMS = 131072


def item_rows(key):
    noise_key = jax.random.fold_in(key, 11)
    return jnp.clip(jax.random.normal(noise_key, (ITEMS, D), jnp.float32), -6.0, 6.0)


def key_weight(key):
    noise_key = jax.random.fold_in(key, 13)
    return jnp.clip(jax.random.normal(noise_key, (D, D), jnp.float32) * D ** (-0.5), -0.25, 0.25)


def tile_table(key):
    table_key = jax.random.fold_in(key, 17)
    first_key, second_key, order_key, tile_key = jax.random.split(table_key, 4)
    first = jax.random.randint(first_key, (BLOCKS, 1), 0, OWNERS + 1)
    second = jax.random.randint(second_key, (BLOCKS, 1), 0, OWNERS + 1)
    counts = jnp.maximum(OWNERS - first * second // OWNERS, 1)
    block_ids = jnp.arange(BLOCKS)[:, None]
    full_block = block_ids % OWNERS == block_ids // OWNERS * 5 % OWNERS
    counts = jnp.where(full_block, OWNERS, counts)
    ranking = jax.random.randint(order_key, (BLOCKS, OWNERS), 0, 1 << 20) * OWNERS + jnp.arange(OWNERS)[None, :]
    order = jnp.argsort(ranking, axis=1)
    place = jnp.argsort(order, axis=1)
    tiles = jax.random.randint(tile_key, (BLOCKS, OWNERS), 0, TDEV)
    return jnp.where(place < counts, tiles, TDEV).astype(jnp.int32)


def draw_tile_lists(key, part):
    return tile_table(key)


def draw_item_x(key, part):
    values = item_rows(key)
    return values.astype(jnp.bfloat16)


def draw_w_k(key, part):
    values = key_weight(key)
    return values.astype(jnp.bfloat16)


def draw_w_q(key, part):
    key = jax.random.fold_in(key, 2)
    own = jax.random.normal(key, (D, D), jnp.float32) * D ** (-0.5)
    return jnp.clip(own, -0.25, 0.25).astype(jnp.bfloat16)


def draw_user_x(key, part):
    key = jax.random.fold_in(key, 3)
    values = jnp.clip(jax.random.normal(key, (USERS, D), jnp.float32), -6.0, 6.0)
    return values.astype(jnp.bfloat16)


def block_scale(rng, extent, cuts, least, top_value):
    factor_of, own = 1.0, jax.random.fold_in(rng, 6)
    for position, shards_of in cuts:
        heights = jnp.exp(jax.random.uniform(jax.random.fold_in(own, position), (shards_of,), jnp.float32, least / len(cuts), top_value / len(cuts)))
        factor_of = factor_of * jnp.repeat(heights, extent[position] // shards_of).reshape([-1 if axis == position else 1 for axis in range(len(extent))])
    return factor_of


def normal_values(key, shape, scale, reach, cuts=(), kind=jnp.bfloat16):
    values = jax.random.normal(key, shape, jnp.float32) * scale
    if len(cuts) > 0:
        values = block_scale(key, shape, cuts, -0.22, 0.18) * values
    return jnp.clip(values, min=-reach, max=reach).astype(kind)


def setup_inputs(seed: int = 0) -> dict:
    splits = jax.random.split(jax.random.key(seed), 10)
    return {
        "user_x": draw_user_x(jax.random.fold_in(splits[9], 71), 0),
        "item_x": draw_item_x(jax.random.fold_in(splits[9], 71), 0),
        "lin_proj": normal_values(splits[2], (ITEMS, RANK), ITEMS ** -0.5, 0.015625, ((0, 512),)),
        "tile_lists": draw_tile_lists(jax.random.fold_in(splits[9], 71), 0),
        "w_q": draw_w_q(jax.random.fold_in(splits[9], 71), 0),
        "w_k": draw_w_k(jax.random.fold_in(splits[9], 71), 0),
        "w_v": normal_values(splits[6], (D, D), D ** -0.5, 0.25),
        "w_o": normal_values(splits[7], (D, D), (D // 16) ** -0.5, 1.0),
        "cotangent": normal_values(splits[8], (USERS, D), 1.0, 6.0, ((0, 512),)),
    }


def head_split(matrix):
    return matrix.reshape(matrix.shape[0], HEADS, HEAD).astype(jnp.float32)


def reference(user_x, item_x, lin_proj, tile_lists, w_q, w_k, w_v, w_o, cotangent):
    both_weights = jnp.concatenate([w_k, w_v], axis=1)
    item_kv = jnp.dot(item_x, both_weights, preferred_element_type=jnp.float32).astype(jnp.bfloat16)
    lin_kv = jnp.dot(lin_proj.T, item_kv, preferred_element_type=jnp.float32).astype(jnp.bfloat16)
    tiled = item_kv.reshape(BLOCKS, TDEV, TILE, 2 * D)
    factor = HEAD ** -0.5

    def block_step(totals, inputs):
        grad_kv, grad_lin = totals
        block_id, user_rows, cot_rows, chosen = inputs
        owner_dev = ((block_id // OWNERS) * OWNERS + jnp.arange(OWNERS)).astype(jnp.int32)
        live_slot = chosen < TDEV
        safe_tile = jnp.minimum(chosen, TDEV - 1).astype(jnp.int32)
        gathered = tiled[owner_dev, safe_tile].reshape(OWNERS * TILE, 2 * D)
        keys_all = jnp.concatenate([gathered[:, :D], lin_kv[:, :D]], axis=0)
        values_all = jnp.concatenate([gathered[:, D:], lin_kv[:, D:]], axis=0)
        keep_key = jnp.concatenate([jnp.repeat(live_slot, TILE), jnp.ones((RANK,), dtype=bool)])
        queries = jnp.dot(user_rows, w_q, preferred_element_type=jnp.float32).astype(jnp.bfloat16)
        query_heads = head_split(queries)
        key_heads = head_split(keys_all)
        value_heads = head_split(values_all)
        scores = jnp.einsum('uhe,she->hus', query_heads, key_heads) * factor
        scores = jnp.where(keep_key[None, None, :], scores, -1e30)
        attn_probs = jax.nn.softmax(scores, axis=-1)
        probs_b = lax.optimization_barrier(attn_probs.astype(jnp.bfloat16)).astype(jnp.float32)
        attended = jnp.einsum('hus,she->uhe', probs_b, value_heads).reshape(UDEV, D).astype(jnp.bfloat16)
        updated = jnp.dot(attended, w_o, preferred_element_type=jnp.float32).astype(jnp.bfloat16)
        d_attended = jnp.dot(cot_rows, w_o.T, preferred_element_type=jnp.float32).astype(jnp.bfloat16)
        grad_heads = head_split(d_attended)
        d_probs = jnp.einsum('uhe,she->hus', grad_heads, value_heads)
        row_delta = jnp.sum(attn_probs * d_probs, axis=-1, keepdims=True)
        d_scores = (attn_probs * (d_probs - row_delta) * factor).astype(jnp.bfloat16)
        d_scores = lax.optimization_barrier(d_scores).astype(jnp.float32)
        d_queries = jnp.einsum('hus,she->uhe', d_scores, key_heads).reshape(UDEV, D).astype(jnp.bfloat16)
        user_grad = jnp.dot(d_queries, w_q.T, preferred_element_type=jnp.float32).astype(jnp.bfloat16)
        d_keys = jnp.einsum('hus,uhe->she', d_scores, query_heads).reshape(-1, D)
        d_values = jnp.einsum('hus,uhe->she', probs_b, grad_heads).reshape(-1, D)
        d_both = jnp.concatenate([d_keys, d_values], axis=1)
        tile_grad = lax.optimization_barrier(d_both[:OWNERS * TILE].astype(jnp.bfloat16)).astype(jnp.float32)
        item_index = ((owner_dev * IDEV)[:, None] + (safe_tile * TILE)[:, None] + jnp.arange(TILE)[None, :]).reshape(-1).astype(jnp.int32)
        grad_kv = grad_kv.at[item_index].add(tile_grad)
        grad_lin = grad_lin + d_both[OWNERS * TILE:]
        return (grad_kv, grad_lin), (updated, user_grad)

    start = (jnp.zeros((ITEMS, 2 * D), jnp.float32), jnp.zeros((RANK, 2 * D), jnp.float32))
    inputs = (jnp.arange(BLOCKS).astype(jnp.int32), user_x.reshape(BLOCKS, UDEV, D), cotangent.reshape(BLOCKS, UDEV, D), tile_lists)
    (grad_kv, grad_lin), (updated, user_grad) = lax.scan(block_step, start, inputs)
    kv_grad = grad_kv + jnp.dot(lin_proj.astype(jnp.float32), grad_lin, precision=lax.Precision.HIGHEST)
    item_grad = jnp.dot(kv_grad, both_weights.T.astype(jnp.float32), precision=lax.Precision.HIGHEST).astype(jnp.bfloat16)
    return updated.reshape(USERS, D), user_grad.reshape(USERS, D), item_grad
```

```python
import functools

import jax
import jax.numpy as jnp
from jax import lax
from jax.experimental import pallas as pl
from jax.experimental.pallas import tpu as pltpu
from jax.sharding import PartitionSpec as P

F32, BF16 = jnp.float32, jnp.bfloat16
HEADS, HEAD, WIDTH, TILE, RANK = 8, 64, 512, 128, 256
ROWS = 256
OWNERS = 16
KEYS = OWNERS * TILE + RANK
CHUNK = 256
CHUNKS = KEYS // CHUNK
VMEM_BYTES = 60 * 1024 * 1024
MESH = pl.DeviceIdType.MESH


def dot(a, b):
    return lax.dot_general(a, b, (((1,), (0,)), ((), ())), preferred_element_type=F32)


def dot_t(a, b):
    return lax.dot_general(a, b, (((1,), (1,)), ((), ())), preferred_element_type=F32)


def split(a):
    high = a.astype(BF16)
    return high, (a - high.astype(F32)).astype(BF16)


class Place:
    def __init__(self):
        self.user, self.item = lax.axis_index("user"), lax.axis_index("item")
        self.near = lax.rem(self.user, 8)
        self.z_lo = lax.div(self.user, 8)
        self.y = lax.rem(self.item, 8)
        self.z_hi = lax.div(self.item, 8)
        self.z = self.z_hi * 4 + self.z_lo
        self.member = (self.near, self.z, self.y)

    def peer(self, group, k):
        if group == 0:
            return (self.z_lo * 8 + k, self.item)
        if group == 1:
            return (lax.rem(k, 4) * 8 + self.near, lax.div(k, 4) * 8 + self.y)
        return (self.user, self.z_hi * 8 + k)

    def along_y(self, step):
        return lax.rem(self.y + step + 8, 8)

    def partner(self):
        return (self.user, lax.rem(self.item + 8, 16))


def greet(place):
    barrier = pltpu.get_barrier_semaphore()
    for group in range(3):
        for r in range(1, 8):
            k = lax.rem(place.member[group] + r, 8)
            pl.semaphore_signal(barrier, inc=1, device_id=place.peer(group, k), device_id_type=MESH)
    pl.semaphore_wait(barrier, 21)


class Total:
    scratch = [
        pltpu.VMEM((8, 32, WIDTH), F32),
        pltpu.VMEM((8, 8, 256), F32),
        pltpu.VMEM((8, 8, 256), F32),
        pltpu.VMEM((8, 256), F32),
        pltpu.VMEM((8, 8, 256), F32),
        pltpu.VMEM((8, 256), F32),
        pltpu.VMEM((8, 8, 256), F32),
        pltpu.VMEM((32, WIDTH), F32),
        pltpu.SemaphoreType.DMA((5, 8)),
        pltpu.SemaphoreType.DMA((5, 8)),
    ]

    def __init__(self, place, part, out, scratch):
        self.place, self.part, self.out = place, part, out
        (self.land1, self.s1, self.land2, self.s2, self.land3, self.s3, self.land4, self.s4) = scratch[:8]
        self.send_sem, self.recv_sem = scratch[8:]
        self.started = [[] for _ in range(5)]

    def start(self, phase, group, source, land):
        me = self.place.member[group]
        for r in range(1, 8):
            k = lax.rem(me + r, 8)
            copy = pltpu.make_async_remote_copy(
                src_ref=source(k),
                dst_ref=land.at[me],
                send_sem=self.send_sem.at[phase, r],
                recv_sem=self.recv_sem.at[phase, r],
                device_id=self.place.peer(group, k),
                device_id_type=MESH,
            )
            copy.start()
            self.started[phase].append(copy)

    def arrive(self, phase):
        for copy in self.started[phase]:
            copy.wait_recv()

    def step(self, phase):
        near, z, y = self.place.member
        if phase == 0:
            self.start(0, 0, lambda k: self.part.at[k], self.land1)
            self.land1[near] = self.part[near]
            return
        self.arrive(phase - 1)
        if phase == 1:
            total = self.land1[0]
            for k in range(1, 8):
                total = total + self.land1[k]
            for p in range(8):
                self.s1[p] = total[p // 2 * 8 : p // 2 * 8 + 8, p % 2 * 256 : p % 2 * 256 + 256]
            self.start(1, 1, lambda k: self.s1.at[k], self.land2)
            self.land2[z] = self.s1[z]
        elif phase == 2:
            total = self.land2[0]
            for k in range(1, 8):
                total = total + self.land2[k]
            self.s2[...] = total
            self.start(2, 2, lambda k: self.s2, self.land3)
            self.land3[y] = total
        elif phase == 3:
            total = self.land3[0]
            for k in range(1, 8):
                total = total + self.land3[k]
            self.s3[...] = total
            self.start(3, 1, lambda k: self.s3, self.land4)
            self.land4[z] = total
        elif phase == 4:
            for p in range(8):
                self.s4[p // 2 * 8 : p // 2 * 8 + 8, p % 2 * 256 : p % 2 * 256 + 256] = self.land4[p]
            self.start(4, 0, lambda k: self.s4, self.out)
            self.out[near] = self.s4[...]

    def finish(self):
        for copies in self.started:
            for copy in copies:
                copy.wait_send()


def gather_kernel(x_ref, proj_ref, all_ref, lin_ref, part, own_sem, zs, zr, ring_send, ring_recv, *scratch):
    place = Place()
    greet(place)
    item, y = place.item, place.y
    keep = pltpu.make_async_copy(x_ref, all_ref.at[item], own_sem)
    keep.start()
    across = pltpu.make_async_remote_copy(
        src_ref=x_ref, dst_ref=all_ref.at[item], send_sem=zs, recv_sem=zr,
        device_id=place.partner(), device_id_type=MESH,
    )
    across.start()
    ring = {}

    def send(chain, way, d):
        column = place.z_hi if chain == 0 else 1 - place.z_hi
        step = 1 if way == 0 else -1
        index = column * 8 + place.along_y(-step * (d - 1))
        source = x_ref if (chain == 0 and d == 1) else all_ref.at[index]
        target = all_ref.at[index]
        if d == 4:
            source, target = source.at[pl.ds(way * TILE, TILE)], target.at[pl.ds(way * TILE, TILE)]
        copy = pltpu.make_async_remote_copy(
            src_ref=source, dst_ref=target,
            send_sem=ring_send.at[chain, way, d], recv_sem=ring_recv.at[chain, way, d],
            device_id=(place.user, place.z_hi * 8 + place.along_y(step)), device_id_type=MESH,
        )
        copy.start()
        ring[chain, way, d] = copy

    def forward(chain, d):
        for way in range(2):
            ring[chain, way, d].wait_recv()
            if d < 4:
                send(chain, way, d + 1)

    for way in range(2):
        send(0, way, 1)
    total = lax.dot_general(
        proj_ref[...], x_ref[...], (((0,), (0,)), ((), ())), preferred_element_type=F32
    )
    for k in range(8):
        part[k] = total[k * 32 : k * 32 + 32]
    lin = Total(place, part, lin_ref, scratch)
    lin.step(0)
    lin.step(1)
    forward(0, 1)
    lin.step(2)
    across.wait_recv()
    for way in range(2):
        send(1, way, 1)
    lin.step(3)
    forward(0, 2)
    lin.step(4)
    forward(1, 1)
    forward(0, 3)
    forward(1, 2)
    lin.arrive(4)
    forward(0, 4)
    forward(1, 3)
    forward(1, 4)
    lin.finish()
    keep.wait()
    across.wait_send()
    for copy in ring.values():
        copy.wait_send()


def attention_kernel(
    row_ref, x_ref, lin_ref, user_ref, cot_ref, wq_ref, wk_ref, wv_ref, wo_ref,
    upd_ref, ug_ref, g_ref, dl_ref,
    xg, k_s, v_s, kt_s, vt_s, qt_m, at_m, q_m, a_m, at_s, s_s, dkv, dlin, o_t, dq_t,
):
    q = dot(user_ref[...], wq_ref[...]).astype(BF16).astype(F32) * (HEAD**-0.5)
    a = dot_t(cot_ref[...], wo_ref[...]).astype(BF16).astype(F32)
    qt, at = q.T, a.T
    at_s[...] = at.reshape(HEADS, HEAD, ROWS)
    low_lane = lax.broadcasted_iota(jnp.int32, (ROWS, 128), 1) < HEAD
    low_row = lax.broadcasted_iota(jnp.int32, (128, ROWS), 0) < HEAD
    for p in range(4):
        cut = slice(p * 128, p * 128 + 128)
        for hh in range(2):
            lane, row = (low_lane, low_row) if hh == 0 else (~low_lane, ~low_row)
            q_m[p, hh * ROWS : hh * ROWS + ROWS] = jnp.where(lane, q[:, cut], 0.0).astype(BF16)
            a_m[p, hh * ROWS : hh * ROWS + ROWS] = jnp.where(lane, a[:, cut], 0.0).astype(BF16)
            qt_m[2 * p + hh] = jnp.where(row, qt[cut], 0.0).astype(BF16)
            at_m[2 * p + hh] = jnp.where(row, at[cut], 0.0).astype(BF16)
    wk_t = wk_ref[...].astype(F32).T.astype(BF16)
    wv_t = wv_ref[...].astype(F32).T.astype(BF16)

    for j in range(OWNERS):
        tile = jnp.minimum(row_ref[j], 1)
        xg[j * TILE : j * TILE + TILE] = x_ref[j, pl.ds(pl.multiple_of(tile * TILE, TILE), TILE), :]
    for c in range(CHUNKS):
        at_rows = slice(c * CHUNK, c * CHUNK + CHUNK)
        if c < CHUNKS - 1:
            pieces = (xg[at_rows],)
        else:
            pieces = split(lin_ref[...])
        k = sum(dot(piece, wk_ref[...]) for piece in pieces).astype(BF16)
        v = sum(dot(piece, wv_ref[...]) for piece in pieces).astype(BF16)
        for p in range(4):
            k_s[p, at_rows] = k[:, p * 128 : p * 128 + 128]
            v_s[p, at_rows] = v[:, p * 128 : p * 128 + 128]
        kt = sum(dot_t(wk_t, piece) for piece in pieces).astype(BF16)
        vt = sum(dot_t(wv_t, piece) for piece in pieces).astype(BF16)
        kt_s[:, :, at_rows] = kt.reshape(HEADS, HEAD, CHUNK)
        vt_s[:, :, at_rows] = vt.reshape(HEADS, HEAD, CHUNK)

    def pair(p, carry):
        inverse, delta = [], []
        for hh in range(2):
            h = 2 * p + hh
            top = jnp.full((1, ROWS), -jnp.inf, F32)
            for c in range(CHUNKS):
                at_rows = slice(c * CHUNK, c * CHUNK + CHUNK)
                s = dot(k_s[p, at_rows], qt_m[h])
                if c < CHUNKS - 1:
                    s = jnp.concatenate(
                        [
                            jnp.where(row_ref[2 * c] < 2, s[:TILE], -1e30),
                            jnp.where(row_ref[2 * c + 1] < 2, s[TILE:], -1e30),
                        ],
                        axis=0,
                    )
                s_s[hh, at_rows] = s
                top = jnp.maximum(top, jnp.max(s, axis=0, keepdims=True))
            denom = jnp.zeros((1, ROWS), F32)
            o = jnp.zeros((HEAD, ROWS), F32)
            for c in range(CHUNKS):
                at_rows = slice(c * CHUNK, c * CHUNK + CHUNK)
                e = jnp.exp(s_s[hh, at_rows] - top)
                denom = denom + jnp.sum(e, axis=0, keepdims=True)
                s_s[hh, at_rows] = e
                o = o + dot(vt_s[h, :, at_rows], e.astype(BF16))
            inv = 1.0 / denom
            o = o * inv
            o_t[h] = o
            inverse.append(inv)
            delta.append(jnp.sum(o * at_s[h], axis=0, keepdims=True))
        dq = [jnp.zeros((HEAD, ROWS), F32) for _ in range(2)]
        lanes_k = pl.ds(pl.multiple_of(p * 128, 128), 128)
        lanes_v = pl.ds(pl.multiple_of(WIDTH + p * 128, 128), 128)
        for c in range(CHUNKS):
            at_rows = slice(c * CHUNK, c * CHUNK + CHUNK)
            ds, pb = [], []
            for hh in range(2):
                h = 2 * p + hh
                dp = dot(v_s[p, at_rows], at_m[h])
                prob = s_s[hh, at_rows] * inverse[hh]
                pb.append(prob.astype(BF16))
                ds.append((prob * (dp - delta[hh])).astype(BF16))
                dq[hh] = dq[hh] + dot(kt_s[h, :, at_rows], ds[hh])
            dk = dot(jnp.concatenate(ds, axis=1), q_m[p])
            dv = dot(jnp.concatenate(pb, axis=1), a_m[p])
            if c < CHUNKS - 1:
                dkv[at_rows, lanes_k] = dk.astype(BF16)
                dkv[at_rows, lanes_v] = dv.astype(BF16)
            else:
                dlin[:, lanes_k] = dk
                dlin[:, lanes_v] = dv
        for hh in range(2):
            dq_t[2 * p + hh] = dq[hh] * (HEAD**-0.5)
        return carry

    lax.fori_loop(0, 4, pair, 0)

    attended = o_t[...].reshape(WIDTH, ROWS).T.astype(BF16)
    upd_ref[...] = dot(attended, wo_ref[...]).astype(BF16)
    d_query = dq_t[...].reshape(WIDTH, ROWS).T.astype(BF16)
    ug_ref[...] = dot_t(d_query, wq_ref[...]).astype(BF16)
    for c in range(CHUNKS - 1):
        at_rows = slice(c * CHUNK, c * CHUNK + CHUNK)
        g = dot_t(dkv[at_rows, :WIDTH], wk_ref[...]) + dot_t(dkv[at_rows, WIDTH:], wv_ref[...])
        g_ref[2 * c] = g[:TILE].astype(BF16)
        g_ref[2 * c + 1] = g[TILE:].astype(BF16)
    g = jnp.zeros((RANK, WIDTH), F32)
    for piece in split(dlin[...]):
        g = g + dot_t(piece[:, :WIDTH], wk_ref[...]) + dot_t(piece[:, WIDTH:], wv_ref[...])
    for k in range(8):
        dl_ref[k] = g[k * 32 : k * 32 + 32]


def scatter_kernel(
    row_ref, g_ref, part, proj_ref, out_ref, lin_out, leave, land, z_buf, z_land, zs, zr, ring_send, ring_recv, *scratch
):
    place = Place()
    greet(place)
    lin = Total(place, part, lin_out, scratch)
    lin.step(0)
    ring = {}

    def own(index, tile):
        return jnp.where(row_ref[index] == tile, g_ref[index].astype(F32), 0.0)

    def send(chain, way, d):
        column = place.z_hi if chain == 0 else 1 - place.z_hi
        step = 1 if way == 0 else -1
        index = column * 8 + place.along_y(step * d)
        buf = leave.at[chain, way, d - 1]
        if d < 4:
            ring[chain, way, d + 1].wait_recv()
        for tile in range(2):
            if d == 4 and tile != way:
                continue
            rows = slice(tile * TILE, tile * TILE + TILE)
            value = own(index, tile)
            if d < 3 or (d == 3 and tile == way):
                value = value + land[chain, way, d, rows].astype(F32)
            leave[chain, way, d - 1, rows] = value.astype(BF16)
        target = land.at[chain, way, d - 1]
        if d == 4:
            buf, target = buf.at[pl.ds(way * TILE, TILE)], target.at[pl.ds(way * TILE, TILE)]
        copy = pltpu.make_async_remote_copy(
            src_ref=buf, dst_ref=target,
            send_sem=ring_send.at[chain, way, d], recv_sem=ring_recv.at[chain, way, d],
            device_id=(place.user, place.z_hi * 8 + place.along_y(step)), device_id_type=MESH,
        )
        copy.start()
        ring[chain, way, d] = copy

    def total(chain, tile):
        column = place.z_hi if chain == 0 else 1 - place.z_hi
        rows = slice(tile * TILE, tile * TILE + TILE)
        value = own(column * 8 + place.y, tile)
        return value + land[chain, 0, 0, rows].astype(F32) + land[chain, 1, 0, rows].astype(F32)

    for d in (4, 3, 2, 1):
        for chain in (1, 0):
            for way in range(2):
                send(chain, way, d)
        lin.step(5 - d)
    for way in range(2):
        ring[1, way, 1].wait_recv()
    for tile in range(2):
        z_buf[tile * TILE : tile * TILE + TILE] = total(1, tile).astype(BF16)
    across = pltpu.make_async_remote_copy(
        src_ref=z_buf, dst_ref=z_land, send_sem=zs, recv_sem=zr,
        device_id=place.partner(), device_id_type=MESH,
    )
    across.start()
    lin.arrive(4)
    back = jnp.zeros((ROWS, WIDTH), F32)
    for piece in split(lin_out[...].reshape(RANK, WIDTH)):
        back = back + dot(proj_ref[...], piece)
    for way in range(2):
        ring[0, way, 1].wait_recv()
    across.wait_recv()
    for tile in range(2):
        rows = slice(tile * TILE, tile * TILE + TILE)
        value = back[rows] + total(0, tile) + z_land[rows].astype(F32)
        out_ref[rows] = value.astype(BF16)
    lin.finish()
    across.wait_send()
    for copy in ring.values():
        copy.wait_send()


def in_vmem(count):
    return [pl.BlockSpec(memory_space=pltpu.VMEM)] * count


def in_smem():
    return pl.BlockSpec(memory_space=pltpu.SMEM)


def per_device(user_x, item_x, lin_proj, tile_lists, w_q, w_k, w_v, w_o, cotangent):
    position = lax.axis_index("item")
    own_row = lax.dynamic_slice_in_dim(tile_lists, position, 1, 0)[0]
    shape = jax.ShapeDtypeStruct
    all_x, lin = pl.pallas_call(
        gather_kernel,
        out_shape=(shape((OWNERS, ROWS, WIDTH), BF16), shape((8, 32, WIDTH), F32)),
        in_specs=in_vmem(2),
        out_specs=in_vmem(2),
        scratch_shapes=[
            pltpu.VMEM((8, 32, WIDTH), F32),
            pltpu.SemaphoreType.DMA,
            pltpu.SemaphoreType.DMA,
            pltpu.SemaphoreType.DMA,
            pltpu.SemaphoreType.DMA((2, 2, 5)),
            pltpu.SemaphoreType.DMA((2, 2, 5)),
        ] + Total.scratch,
        compiler_params=pltpu.CompilerParams(
            collective_id=0, has_side_effects=True, vmem_limit_bytes=VMEM_BYTES
        ),
        name="gather_items",
    )(item_x, lin_proj)
    updated, user_grad, grads, d_lin = pl.pallas_call(
        attention_kernel,
        out_shape=(
            shape((ROWS, WIDTH), BF16),
            shape((ROWS, WIDTH), BF16),
            shape((OWNERS, TILE, WIDTH), BF16),
            shape((8, 32, WIDTH), F32),
        ),
        in_specs=[in_smem()] + in_vmem(8),
        out_specs=in_vmem(4),
        scratch_shapes=[
            pltpu.VMEM((OWNERS * TILE, WIDTH), BF16),
            pltpu.VMEM((4, KEYS, 128), BF16),
            pltpu.VMEM((4, KEYS, 128), BF16),
            pltpu.VMEM((HEADS, HEAD, KEYS), BF16),
            pltpu.VMEM((HEADS, HEAD, KEYS), BF16),
            pltpu.VMEM((HEADS, 128, ROWS), BF16),
            pltpu.VMEM((HEADS, 128, ROWS), BF16),
            pltpu.VMEM((4, 2 * ROWS, 128), BF16),
            pltpu.VMEM((4, 2 * ROWS, 128), BF16),
            pltpu.VMEM((HEADS, HEAD, ROWS), F32),
            pltpu.VMEM((2, KEYS, ROWS), F32),
            pltpu.VMEM((OWNERS * TILE, 2 * WIDTH), BF16),
            pltpu.VMEM((RANK, 2 * WIDTH), F32),
            pltpu.VMEM((HEADS, HEAD, ROWS), F32),
            pltpu.VMEM((HEADS, HEAD, ROWS), F32),
        ],
        compiler_params=pltpu.CompilerParams(vmem_limit_bytes=VMEM_BYTES),
        name="attend",
    )(own_row, all_x, lin.reshape(RANK, WIDTH), user_x, cotangent, w_q, w_k, w_v, w_o)
    item_grad, _ = pl.pallas_call(
        scatter_kernel,
        out_shape=(shape((ROWS, WIDTH), BF16), shape((8, 32, WIDTH), F32)),
        in_specs=[in_smem()] + in_vmem(3),
        out_specs=in_vmem(2),
        scratch_shapes=[
            pltpu.VMEM((2, 2, 4, ROWS, WIDTH), BF16),
            pltpu.VMEM((2, 2, 4, ROWS, WIDTH), BF16),
            pltpu.VMEM((ROWS, WIDTH), BF16),
            pltpu.VMEM((ROWS, WIDTH), BF16),
            pltpu.SemaphoreType.DMA,
            pltpu.SemaphoreType.DMA,
            pltpu.SemaphoreType.DMA((2, 2, 5)),
            pltpu.SemaphoreType.DMA((2, 2, 5)),
        ] + Total.scratch,
        compiler_params=pltpu.CompilerParams(
            collective_id=1, has_side_effects=True, vmem_limit_bytes=VMEM_BYTES
        ),
        name="scatter_grads",
    )(own_row, grads, d_lin, lin_proj)
    return updated, user_grad, item_grad


def solution(mesh):
    rows = P(("user", "item"), None)
    return jax.shard_map(
        per_device,
        mesh=mesh,
        in_specs=(rows, rows, rows, P("user", None), P(), P(), P(), P(), rows),
        out_specs=(rows, rows, rows),
        check_vma=False,
    )
```

```python
import functools

import jax
import jax.numpy as jnp
from jax import lax
from jax.experimental import pallas as pl
from jax.experimental.pallas import tpu as pltpu
from jax.sharding import PartitionSpec as P

F32, BF16 = jnp.float32, jnp.bfloat16
HEADS, HEAD, WIDTH, TILE, RANK = 8, 64, 512, 128, 256
ROWS = 256
OWNERS = 16
KEYS = OWNERS * TILE + RANK
CHUNK = 256
CHUNKS = KEYS // CHUNK
VMEM_BYTES = 60 * 1024 * 1024
MESH = pl.DeviceIdType.MESH


def dot(a, b):
    return lax.dot_general(a, b, (((1,), (0,)), ((), ())), preferred_element_type=F32)


def dot_t(a, b):
    return lax.dot_general(a, b, (((1,), (1,)), ((), ())), preferred_element_type=F32)


def split(a):
    high = a.astype(BF16)
    return high, (a - high.astype(F32)).astype(BF16)


class Place:
    def __init__(self):
        self.user, self.item = lax.axis_index("user"), lax.axis_index("item")
        self.near = lax.rem(self.user, 8)
        self.z_lo = lax.div(self.user, 8)
        self.y = lax.rem(self.item, 8)
        self.z_hi = lax.div(self.item, 8)
        self.z = self.z_hi * 4 + self.z_lo
        self.member = (self.near, self.z, self.y)

    def peer(self, group, k):
        if group == 0:
            return (self.z_lo * 8 + k, self.item)
        if group == 1:
            return (lax.rem(k, 4) * 8 + self.near, lax.div(k, 4) * 8 + self.y)
        return (self.user, self.z_hi * 8 + k)

    def along_y(self, step):
        return lax.rem(self.y + step + 8, 8)

    def partner(self):
        return (self.user, lax.rem(self.item + 8, 16))


def greet(place):
    barrier = pltpu.get_barrier_semaphore()
    for group in range(3):
        for r in range(1, 8):
            k = lax.rem(place.member[group] + r, 8)
            pl.semaphore_signal(barrier, inc=1, device_id=place.peer(group, k), device_id_type=MESH)
    pl.semaphore_wait(barrier, 21)


class Total:
    scratch = [
        pltpu.VMEM((8, 32, WIDTH), F32),
        pltpu.VMEM((8, 8, 256), F32),
        pltpu.VMEM((8, 8, 256), F32),
        pltpu.VMEM((8, 256), F32),
        pltpu.VMEM((8, 8, 256), F32),
        pltpu.VMEM((8, 256), F32),
        pltpu.VMEM((8, 8, 256), F32),
        pltpu.VMEM((32, WIDTH), F32),
        pltpu.SemaphoreType.DMA((5, 8)),
        pltpu.SemaphoreType.DMA((5, 8)),
    ]

    def __init__(self, place, part, out, scratch):
        self.place, self.part, self.out = place, part, out
        (self.land1, self.s1, self.land2, self.s2, self.land3, self.s3, self.land4, self.s4) = scratch[:8]
        self.send_sem, self.recv_sem = scratch[8:]
        self.started = [[] for _ in range(5)]

    def start(self, phase, group, source, land):
        me = self.place.member[group]
        for r in range(1, 8):
            k = lax.rem(me + r, 8)
            copy = pltpu.make_async_remote_copy(
                src_ref=source(k),
                dst_ref=land.at[me],
                send_sem=self.send_sem.at[phase, r],
                recv_sem=self.recv_sem.at[phase, r],
                device_id=self.place.peer(group, k),
                device_id_type=MESH,
            )
            copy.start()
            self.started[phase].append(copy)

    def arrive(self, phase):
        for copy in self.started[phase]:
            copy.wait_recv()

    def step(self, phase):
        near, z, y = self.place.member
        if phase == 0:
            self.start(0, 0, lambda k: self.part.at[k], self.land1)
            self.land1[near] = self.part[near]
            return
        self.arrive(phase - 1)
        if phase == 1:
            total = self.land1[0]
            for k in range(1, 8):
                total = total + self.land1[k]
            for p in range(8):
                self.s1[p] = total[p // 2 * 8 : p // 2 * 8 + 8, p % 2 * 256 : p % 2 * 256 + 256]
            self.start(1, 1, lambda k: self.s1.at[k], self.land2)
            self.land2[z] = self.s1[z]
        elif phase == 2:
            total = self.land2[0]
            for k in range(1, 8):
                total = total + self.land2[k]
            self.s2[...] = total
            self.start(2, 2, lambda k: self.s2, self.land3)
            self.land3[y] = total
        elif phase == 3:
            total = self.land3[0]
            for k in range(1, 8):
                total = total + self.land3[k]
            self.s3[...] = total
            self.start(3, 1, lambda k: self.s3, self.land4)
            self.land4[z] = total
        elif phase == 4:
            for p in range(8):
                self.s4[p // 2 * 8 : p // 2 * 8 + 8, p % 2 * 256 : p % 2 * 256 + 256] = self.land4[p]
            self.start(4, 0, lambda k: self.s4, self.out)
            self.out[near] = self.s4[...]

    def finish(self):
        for copies in self.started:
            for copy in copies:
                copy.wait_send()


class Attention:
    scratch = [
        pltpu.VMEM((4, KEYS, 128), BF16),
        pltpu.VMEM((4, KEYS, 128), BF16),
        pltpu.VMEM((HEADS, HEAD, KEYS), BF16),
        pltpu.VMEM((HEADS, HEAD, CHUNK), BF16),
        pltpu.VMEM((HEADS, 128, ROWS), BF16),
        pltpu.VMEM((HEADS, 128, ROWS), BF16),
        pltpu.VMEM((4, 2 * ROWS, 128), BF16),
        pltpu.VMEM((4, 2 * ROWS, 128), BF16),
        pltpu.VMEM((HEADS, HEAD, ROWS), F32),
        pltpu.VMEM((HEADS, KEYS, ROWS), F32),
        pltpu.VMEM((CHUNK, 2 * WIDTH), F32),
        pltpu.VMEM((HEADS, HEAD, ROWS), F32),
        pltpu.VMEM((HEADS, HEAD, ROWS), F32),
        pltpu.VMEM((HEADS, 1, ROWS), F32),
        pltpu.VMEM((HEADS, 1, ROWS), F32),
        pltpu.VMEM((HEADS, 1, ROWS), F32),
        pltpu.VMEM((CHUNKS, HEADS, 1, ROWS), F32),
        pltpu.VMEM((WIDTH, WIDTH), BF16),
        pltpu.VMEM((WIDTH, WIDTH), BF16),
    ]

    def __init__(self, weights, scratch):
        self.wq, self.wk, self.wv, self.wo = weights
        (self.k_s, self.v_s, self.kt_s, self.vt_s, self.qt_m, self.at_m, self.q_m, self.a_m, self.at_s,
         self.e_s, self.dkv, self.o_t, self.dq_t, self.top, self.den, self.delta, self.tops,
         self.wk_t, self.wv_t) = scratch

    def prepare(self, user_ref, cot_ref):
        q = dot(user_ref[...], self.wq[...]).astype(BF16).astype(F32) * (HEAD**-0.5)
        a = dot_t(cot_ref[...], self.wo[...]).astype(BF16).astype(F32)
        qt, at = q.T, a.T
        self.at_s[...] = at.reshape(HEADS, HEAD, ROWS)
        low_lane = lax.broadcasted_iota(jnp.int32, (ROWS, 128), 1) < HEAD
        low_row = lax.broadcasted_iota(jnp.int32, (128, ROWS), 0) < HEAD
        for p in range(4):
            cut = slice(p * 128, p * 128 + 128)
            for hh in range(2):
                lane, row = (low_lane, low_row) if hh == 0 else (~low_lane, ~low_row)
                half = slice(hh * ROWS, hh * ROWS + ROWS)
                self.q_m[p, half] = jnp.where(lane, q[:, cut], 0.0).astype(BF16)
                self.a_m[p, half] = jnp.where(lane, a[:, cut], 0.0).astype(BF16)
                self.qt_m[2 * p + hh] = jnp.where(row, qt[cut], 0.0).astype(BF16)
                self.at_m[2 * p + hh] = jnp.where(row, at[cut], 0.0).astype(BF16)
        self.wk_t[...] = self.wk[...].astype(F32).T.astype(BF16)
        self.wv_t[...] = self.wv[...].astype(F32).T.astype(BF16)
        self.top[...] = jnp.full(self.top.shape, -1e30, F32)
        self.den[...] = jnp.zeros(self.den.shape, F32)
        self.o_t[...] = jnp.zeros(self.o_t.shape, F32)
        self.dq_t[...] = jnp.zeros(self.dq_t.shape, F32)

    def forward(self, c, pieces, live):
        at_rows = slice(c * CHUNK, c * CHUNK + CHUNK)
        k = sum(dot(piece, self.wk[...]) for piece in pieces).astype(BF16)
        v = sum(dot(piece, self.wv[...]) for piece in pieces).astype(BF16)
        for p in range(4):
            self.k_s[p, at_rows] = k[:, p * 128 : p * 128 + 128]
            self.v_s[p, at_rows] = v[:, p * 128 : p * 128 + 128]
        kt = sum(dot_t(self.wk_t[...], piece) for piece in pieces).astype(BF16)
        vt = sum(dot_t(self.wv_t[...], piece) for piece in pieces).astype(BF16)
        self.kt_s[:, :, at_rows] = kt.reshape(HEADS, HEAD, CHUNK)
        self.vt_s[...] = vt.reshape(HEADS, HEAD, CHUNK)

        def pair(p, carry):
            for hh in range(2):
                h = 2 * p + hh
                s = dot(self.k_s[p, at_rows], self.qt_m[h])
                if live is not None:
                    s = jnp.concatenate(
                        [jnp.where(live[0], s[:TILE], -1e30), jnp.where(live[1], s[TILE:], -1e30)], axis=0
                    )
                before = self.top[h]
                top = jnp.maximum(before, jnp.max(s, axis=0, keepdims=True))
                e = jnp.exp(s - top)
                scale = jnp.exp(before - top)
                self.top[h] = top
                self.tops[c, h] = top
                self.e_s[h, at_rows] = e
                self.den[h] = self.den[h] * scale + jnp.sum(e, axis=0, keepdims=True)
                self.o_t[h] = self.o_t[h] * scale + dot(self.vt_s[h], e.astype(BF16))
            return carry

        lax.fori_loop(0, 4, pair, 0)

    def settle(self):
        for h in range(HEADS):
            inverse = 1.0 / self.den[h]
            o = self.o_t[h] * inverse
            self.o_t[h] = o
            self.den[h] = inverse
            self.delta[h] = jnp.sum(o * self.at_s[h], axis=0, keepdims=True)

    def backward(self, c):
        at_rows = slice(c * CHUNK, c * CHUNK + CHUNK)

        def pair(p, carry):
            ds, pb = [], []
            for hh in range(2):
                h = 2 * p + hh
                dp = dot(self.v_s[p, at_rows], self.at_m[h])
                prob = self.e_s[h, at_rows] * (jnp.exp(self.tops[c, h] - self.top[h]) * self.den[h])
                pb.append(prob.astype(BF16))
                ds.append((prob * (dp - self.delta[h])).astype(BF16))
                self.dq_t[h] = self.dq_t[h] + dot(self.kt_s[h, :, at_rows], ds[hh])
            self.dkv[:, pl.ds(pl.multiple_of(p * 128, 128), 128)] = dot(
                jnp.concatenate(ds, axis=1), self.q_m[p]
            )
            self.dkv[:, pl.ds(pl.multiple_of(WIDTH + p * 128, 128), 128)] = dot(
                jnp.concatenate(pb, axis=1), self.a_m[p]
            )
            return carry

        lax.fori_loop(0, 4, pair, 0)
        if c < CHUNKS - 1:
            pieces = (self.dkv[...].astype(BF16),)
        else:
            pieces = split(self.dkv[...])
        return sum(
            dot_t(piece[:, :WIDTH], self.wk[...]) + dot_t(piece[:, WIDTH:], self.wv[...]) for piece in pieces
        )

    def updated(self):
        attended = self.o_t[...].reshape(WIDTH, ROWS).T.astype(BF16)
        return dot(attended, self.wo[...]).astype(BF16)

    def user_grad(self):
        d_query = (self.dq_t[...] * (HEAD**-0.5)).reshape(WIDTH, ROWS).T.astype(BF16)
        return dot_t(d_query, self.wq[...]).astype(BF16)


RING = [
    pltpu.SemaphoreType.DMA,
    pltpu.SemaphoreType.DMA,
    pltpu.SemaphoreType.DMA((2, 2, 5)),
    pltpu.SemaphoreType.DMA((2, 2, 5)),
]


class Gather:
    def __init__(self, place, x_ref, all_ref, sems):
        self.place, self.x, self.all = place, x_ref, all_ref
        self.zs, self.zr, self.send_sem, self.recv_sem = sems
        self.ring = {}

    def column(self, chain):
        return (self.place.z_hi if chain == 0 else 1 - self.place.z_hi) * 8

    def start_across(self):
        self.across = pltpu.make_async_remote_copy(
            src_ref=self.x, dst_ref=self.all.at[self.place.item], send_sem=self.zs, recv_sem=self.zr,
            device_id=self.place.partner(), device_id_type=MESH,
        )
        self.across.start()

    def send(self, chain, way, d):
        step = 1 if way == 0 else -1
        index = self.column(chain) + self.place.along_y(-step * (d - 1))
        source = self.x if (chain == 0 and d == 1) else self.all.at[index]
        target = self.all.at[index]
        if d == 4:
            source, target = source.at[pl.ds(way * TILE, TILE)], target.at[pl.ds(way * TILE, TILE)]
        copy = pltpu.make_async_remote_copy(
            src_ref=source, dst_ref=target,
            send_sem=self.send_sem.at[chain, way, d], recv_sem=self.recv_sem.at[chain, way, d],
            device_id=(self.place.user, self.place.z_hi * 8 + self.place.along_y(step)), device_id_type=MESH,
        )
        copy.start()
        self.ring[chain, way, d] = copy

    def forward(self, chain, d):
        for way in range(2):
            self.ring[chain, way, d].wait_recv()
            if d < 4:
                self.send(chain, way, d + 1)

    def finish(self):
        self.across.wait_send()
        for copy in self.ring.values():
            copy.wait_send()


class Scatter:
    scratch = [
        pltpu.VMEM((2, 2, 4, ROWS, WIDTH), BF16),
        pltpu.VMEM((2, 2, 4, ROWS, WIDTH), BF16),
        pltpu.VMEM((ROWS, WIDTH), BF16),
        pltpu.VMEM((ROWS, WIDTH), BF16),
    ] + RING

    def __init__(self, place, listed, scratch):
        self.place, self.listed = place, listed
        (self.leave, self.land, self.z_buf, self.z_land, self.zs, self.zr, self.send_sem, self.recv_sem) = scratch
        self.ring = {}

    def send(self, chain, way, d, own):
        step = 1 if way == 0 else -1
        buf, target = self.leave.at[chain, way, d - 1], self.land.at[chain, way, d - 1]
        if d < 4:
            self.ring[chain, way, d + 1].wait_recv()
        for tile in range(2):
            if d == 4 and tile != way:
                continue
            rows = slice(tile * TILE, tile * TILE + TILE)
            value = own(tile)
            if d < 3 or (d == 3 and tile == way):
                value = value + self.land[chain, way, d, rows].astype(F32)
            self.leave[chain, way, d - 1, rows] = value.astype(BF16)
        if d == 4:
            buf, target = buf.at[pl.ds(way * TILE, TILE)], target.at[pl.ds(way * TILE, TILE)]
        copy = pltpu.make_async_remote_copy(
            src_ref=buf, dst_ref=target,
            send_sem=self.send_sem.at[chain, way, d], recv_sem=self.recv_sem.at[chain, way, d],
            device_id=(self.place.user, self.place.z_hi * 8 + self.place.along_y(step)), device_id_type=MESH,
        )
        copy.start()
        self.ring[chain, way, d] = copy

    def total(self, chain, own, tile):
        rows = slice(tile * TILE, tile * TILE + TILE)
        value = own(tile)
        return value + self.land[chain, 0, 0, rows].astype(F32) + self.land[chain, 1, 0, rows].astype(F32)

    def arrive(self, chain):
        for way in range(2):
            self.ring[chain, way, 1].wait_recv()

    def start_across(self, own):
        for tile in range(2):
            self.z_buf[tile * TILE : tile * TILE + TILE] = self.total(1, own, tile).astype(BF16)
        self.across = pltpu.make_async_remote_copy(
            src_ref=self.z_buf, dst_ref=self.z_land, send_sem=self.zs, recv_sem=self.zr,
            device_id=self.place.partner(), device_id_type=MESH,
        )
        self.across.start()

    def finish(self):
        self.across.wait_send()
        for copy in self.ring.values():
            copy.wait_send()


def take(scratch, count):
    taken = scratch[:count]
    del scratch[:count]
    return taken


def kernel(
    row_ref, user_ref, x_ref, proj_ref, wq_ref, wk_ref, wv_ref, wo_ref, cot_ref,
    upd_ref, ug_ref, out_ref, all_x, part, lin_sum, lin_total, grads, own_part, *scratch
):
    scratch = list(scratch)
    place = Place()
    gather = Gather(place, x_ref, all_x, take(scratch, 4))
    scatter = Scatter(place, row_ref, take(scratch, len(Scatter.scratch)))
    lin = Total(place, part, lin_sum, take(scratch, len(Total.scratch)))
    d_lin = Total(place, own_part, lin_total, take(scratch, len(Total.scratch)))
    attention = Attention((wq_ref, wk_ref, wv_ref, wo_ref), scratch)

    greet(place)
    gather.start_across()
    for way in range(2):
        gather.send(0, way, 1)
    total = lax.dot_general(
        proj_ref[...], x_ref[...], (((0,), (0,)), ((), ())), preferred_element_type=F32
    )
    for k in range(8):
        part[k] = total[k * 32 : k * 32 + 32]
    lin.step(0)
    attention.prepare(user_ref, cot_ref)
    lin.step(1)
    gather.forward(0, 1)
    lin.step(2)
    gather.across.wait_recv()
    for way in range(2):
        gather.send(1, way, 1)
    lin.step(3)

    def listed(chain, dy):
        return row_ref[gather.column(chain) + place.along_y(dy)]

    def chunk_forward(dy):
        rows, live = [], []
        for chain in range(2):
            tile = listed(chain, dy)
            block = x_ref if (chain == 0 and dy == 0) else all_x.at[gather.column(chain) + place.along_y(dy)]
            rows.append(jnp.where(tile == 1, block[TILE:], block[:TILE]))
            live.append(tile < 2)
        attention.forward(dy, (jnp.concatenate(rows, axis=0),), live)

    chunk_forward(0)
    gather.forward(0, 2)
    lin.step(4)
    gather.forward(1, 1)
    chunk_forward(7)
    gather.forward(0, 3)
    chunk_forward(1)
    gather.forward(1, 2)
    chunk_forward(6)
    chunk_forward(2)
    gather.forward(1, 3)
    chunk_forward(5)
    chunk_forward(3)
    lin.arrive(4)
    attention.forward(8, split(lin_sum[...].reshape(RANK, WIDTH)), None)
    gather.forward(0, 4)
    gather.forward(1, 4)
    chunk_forward(4)
    attention.settle()

    g = attention.backward(8)
    for k in range(8):
        own_part[k] = g[k * 32 : k * 32 + 32]
    d_lin.step(0)

    def chunk_backward(dy):
        grads[...] = attention.backward(dy)

    def own(chain, dy):
        def term(tile):
            return jnp.where(listed(chain, dy) == tile, grads[chain * TILE : chain * TILE + TILE], 0.0)

        return term

    chunk_backward(4)
    for chain in (1, 0):
        for way in range(2):
            scatter.send(chain, way, 4, own(chain, 4))
    d_lin.step(1)
    for d in (3, 2, 1):
        for way in range(2):
            dy = d if way == 0 else 8 - d
            chunk_backward(dy)
            for chain in (1, 0):
                scatter.send(chain, way, d, own(chain, dy))
        d_lin.step(5 - d)
    chunk_backward(0)
    upd_ref[...] = attention.updated()
    ug_ref[...] = attention.user_grad()
    scatter.arrive(1)
    scatter.start_across(own(1, 0))
    d_lin.arrive(4)
    back = jnp.zeros((ROWS, WIDTH), F32)
    for piece in split(lin_total[...].reshape(RANK, WIDTH)):
        back = back + dot(proj_ref[...], piece)
    scatter.arrive(0)
    scatter.across.wait_recv()
    for tile in range(2):
        rows = slice(tile * TILE, tile * TILE + TILE)
        value = back[rows] + scatter.total(0, own(0, 0), tile) + scatter.z_land[rows].astype(F32)
        out_ref[rows] = value.astype(BF16)
    lin.finish()
    d_lin.finish()
    gather.finish()
    scatter.finish()


def in_vmem(count):
    return [pl.BlockSpec(memory_space=pltpu.VMEM)] * count


def per_device(user_x, item_x, lin_proj, tile_lists, w_q, w_k, w_v, w_o, cotangent):
    position = lax.axis_index("item")
    own_row = lax.dynamic_slice_in_dim(tile_lists, position, 1, 0)[0]
    shape = jax.ShapeDtypeStruct
    sums = pltpu.VMEM((8, 32, WIDTH), F32)
    return pl.pallas_call(
        kernel,
        out_shape=[shape((ROWS, WIDTH), BF16)] * 3,
        in_specs=[pl.BlockSpec(memory_space=pltpu.SMEM)] + in_vmem(8),
        out_specs=in_vmem(3),
        scratch_shapes=[
            pltpu.VMEM((OWNERS, ROWS, WIDTH), BF16),
            sums, sums, sums,
            pltpu.VMEM((CHUNK, WIDTH), F32),
            sums,
        ] + RING + Scatter.scratch + Total.scratch + Total.scratch + Attention.scratch,
        compiler_params=pltpu.CompilerParams(
            collective_id=0, has_side_effects=True, vmem_limit_bytes=VMEM_BYTES
        ),
        name="attend_and_exchange",
    )(own_row, user_x, item_x, lin_proj, w_q, w_k, w_v, w_o, cotangent)


def solution(mesh):
    rows = P(("user", "item"), None)
    return jax.shard_map(
        per_device,
        mesh=mesh,
        in_specs=(rows, rows, rows, P("user", None), P(), P(), P(), P(), rows),
        out_specs=(rows, rows, rows),
        check_vma=False,
    )
```

```python
import functools

import jax
import jax.numpy as jnp
from jax import lax
from jax.experimental import pallas as pl
from jax.experimental.pallas import tpu as pltpu
from jax.sharding import PartitionSpec as P

F32, BF16 = jnp.float32, jnp.bfloat16
HEADS, HEAD, WIDTH, TILE, RANK = 8, 64, 512, 128, 256
ROWS = 256
OWNERS = 16
KEYS = OWNERS * TILE + RANK
CHUNK = 256
CHUNKS = KEYS // CHUNK
VMEM_BYTES = 60 * 1024 * 1024
MESH = pl.DeviceIdType.MESH


def dot(a, b):
    return lax.dot_general(a, b, (((1,), (0,)), ((), ())), preferred_element_type=F32)


def dot_t(a, b):
    return lax.dot_general(a, b, (((1,), (1,)), ((), ())), preferred_element_type=F32)


def split(a):
    high = a.astype(BF16)
    return high, (a - high.astype(F32)).astype(BF16)


class Place:
    def __init__(self):
        self.user, self.item = lax.axis_index("user"), lax.axis_index("item")
        self.near = lax.rem(self.user, 8)
        self.z_lo = lax.div(self.user, 8)
        self.y = lax.rem(self.item, 8)
        self.z_hi = lax.div(self.item, 8)
        self.z = self.z_hi * 4 + self.z_lo
        self.member = (self.near, self.z, self.y)

    def peer(self, group, k):
        if group == 0:
            return (self.z_lo * 8 + k, self.item)
        if group == 1:
            return (lax.rem(k, 4) * 8 + self.near, lax.div(k, 4) * 8 + self.y)
        return (self.user, self.z_hi * 8 + k)

    def along_y(self, step):
        return lax.rem(self.y + step + 8, 8)

    def partner(self):
        return (self.user, lax.rem(self.item + 8, 16))


def greet(place):
    barrier = pltpu.get_barrier_semaphore()
    for group in range(3):
        for r in range(1, 8):
            k = lax.rem(place.member[group] + r, 8)
            pl.semaphore_signal(barrier, inc=1, device_id=place.peer(group, k), device_id_type=MESH)
    pl.semaphore_wait(barrier, 21)


class Total:
    scratch = [
        pltpu.VMEM((8, 32, WIDTH), F32),
        pltpu.VMEM((8, 8, 256), F32),
        pltpu.VMEM((8, 8, 256), F32),
        pltpu.VMEM((8, 256), F32),
        pltpu.VMEM((8, 8, 256), F32),
        pltpu.VMEM((8, 256), F32),
        pltpu.VMEM((8, 8, 256), F32),
        pltpu.VMEM((32, WIDTH), F32),
        pltpu.SemaphoreType.DMA((5, 8)),
        pltpu.SemaphoreType.DMA((5, 8)),
    ]

    def __init__(self, place, part, out, scratch):
        self.place, self.part, self.out = place, part, out
        (self.land1, self.s1, self.land2, self.s2, self.land3, self.s3, self.land4, self.s4) = scratch[:8]
        self.send_sem, self.recv_sem = scratch[8:]
        self.started = [[] for _ in range(5)]

    def start(self, phase, group, source, land):
        me = self.place.member[group]
        for r in range(1, 8):
            k = lax.rem(me + r, 8)
            copy = pltpu.make_async_remote_copy(
                src_ref=source(k),
                dst_ref=land.at[me],
                send_sem=self.send_sem.at[phase, r],
                recv_sem=self.recv_sem.at[phase, r],
                device_id=self.place.peer(group, k),
                device_id_type=MESH,
            )
            copy.start()
            self.started[phase].append(copy)

    def arrive(self, phase):
        for copy in self.started[phase]:
            copy.wait_recv()

    def step(self, phase):
        near, z, y = self.place.member
        if phase == 0:
            self.start(0, 0, lambda k: self.part.at[k], self.land1)
            self.land1[near] = self.part[near]
            return
        self.arrive(phase - 1)
        if phase == 1:
            total = self.land1[0]
            for k in range(1, 8):
                total = total + self.land1[k]
            for p in range(8):
                self.s1[p] = total[p // 2 * 8 : p // 2 * 8 + 8, p % 2 * 256 : p % 2 * 256 + 256]
            self.start(1, 1, lambda k: self.s1.at[k], self.land2)
            self.land2[z] = self.s1[z]
        elif phase == 2:
            total = self.land2[0]
            for k in range(1, 8):
                total = total + self.land2[k]
            self.s2[...] = total
            self.start(2, 2, lambda k: self.s2, self.land3)
            self.land3[y] = total
        elif phase == 3:
            total = self.land3[0]
            for k in range(1, 8):
                total = total + self.land3[k]
            self.s3[...] = total
            self.start(3, 1, lambda k: self.s3, self.land4)
            self.land4[z] = total
        elif phase == 4:
            for p in range(8):
                self.s4[p // 2 * 8 : p // 2 * 8 + 8, p % 2 * 256 : p % 2 * 256 + 256] = self.land4[p]
            self.start(4, 0, lambda k: self.s4, self.out)
            self.out[near] = self.s4[...]

    def finish(self):
        for copies in self.started:
            for copy in copies:
                copy.wait_send()


class Attention:
    scratch = [
        pltpu.VMEM((4, KEYS, 128), BF16),
        pltpu.VMEM((4, KEYS, 128), BF16),
        pltpu.VMEM((HEADS, HEAD, KEYS), BF16),
        pltpu.VMEM((HEADS, HEAD, CHUNK), BF16),
        pltpu.VMEM((HEADS, 128, ROWS), BF16),
        pltpu.VMEM((HEADS, 128, ROWS), BF16),
        pltpu.VMEM((4, 2 * ROWS, 128), BF16),
        pltpu.VMEM((4, 2 * ROWS, 128), BF16),
        pltpu.VMEM((HEADS, HEAD, ROWS), F32),
        pltpu.VMEM((HEADS, KEYS, ROWS), F32),
        pltpu.VMEM((CHUNK, 2 * WIDTH), F32),
        pltpu.VMEM((HEADS, HEAD, ROWS), F32),
        pltpu.VMEM((HEADS, HEAD, ROWS), F32),
        pltpu.VMEM((HEADS, 1, ROWS), F32),
        pltpu.VMEM((HEADS, 1, ROWS), F32),
        pltpu.VMEM((HEADS, 1, ROWS), F32),
        pltpu.VMEM((CHUNKS, HEADS, 1, ROWS), F32),
        pltpu.VMEM((WIDTH, WIDTH), BF16),
        pltpu.VMEM((WIDTH, WIDTH), BF16),
    ]

    def __init__(self, weights, scratch):
        self.wq, self.wk, self.wv, self.wo = weights
        (self.k_s, self.v_s, self.kt_s, self.vt_s, self.qt_m, self.at_m, self.q_m, self.a_m, self.at_s,
         self.e_s, self.dkv, self.o_t, self.dq_t, self.top, self.den, self.delta, self.tops,
         self.wk_t, self.wv_t) = scratch

    def prepare(self, user_ref, cot_ref):
        q = dot(user_ref[...], self.wq[...]).astype(BF16).astype(F32) * (HEAD**-0.5)
        a = dot_t(cot_ref[...], self.wo[...]).astype(BF16).astype(F32)
        qt, at = q.T, a.T
        self.at_s[...] = at.reshape(HEADS, HEAD, ROWS)
        low_lane = lax.broadcasted_iota(jnp.int32, (ROWS, 128), 1) < HEAD
        low_row = lax.broadcasted_iota(jnp.int32, (128, ROWS), 0) < HEAD
        for p in range(4):
            cut = slice(p * 128, p * 128 + 128)
            for hh in range(2):
                lane, row = (low_lane, low_row) if hh == 0 else (~low_lane, ~low_row)
                half = slice(hh * ROWS, hh * ROWS + ROWS)
                self.q_m[p, half] = jnp.where(lane, q[:, cut], 0.0).astype(BF16)
                self.a_m[p, half] = jnp.where(lane, a[:, cut], 0.0).astype(BF16)
                self.qt_m[2 * p + hh] = jnp.where(row, qt[cut], 0.0).astype(BF16)
                self.at_m[2 * p + hh] = jnp.where(row, at[cut], 0.0).astype(BF16)
        self.wk_t[...] = self.wk[...].astype(F32).T.astype(BF16)
        self.wv_t[...] = self.wv[...].astype(F32).T.astype(BF16)
        self.top[...] = jnp.full(self.top.shape, -1e30, F32)
        self.den[...] = jnp.zeros(self.den.shape, F32)
        self.o_t[...] = jnp.zeros(self.o_t.shape, F32)
        self.dq_t[...] = jnp.zeros(self.dq_t.shape, F32)

    def forward(self, c, pieces, live):
        at_rows = slice(c * CHUNK, c * CHUNK + CHUNK)
        k = sum(dot(piece, self.wk[...]) for piece in pieces).astype(BF16)
        v = sum(dot(piece, self.wv[...]) for piece in pieces).astype(BF16)
        for p in range(4):
            self.k_s[p, at_rows] = k[:, p * 128 : p * 128 + 128]
            self.v_s[p, at_rows] = v[:, p * 128 : p * 128 + 128]
        kt = sum(dot_t(self.wk_t[...], piece) for piece in pieces).astype(BF16)
        vt = sum(dot_t(self.wv_t[...], piece) for piece in pieces).astype(BF16)
        self.kt_s[:, :, at_rows] = kt.reshape(HEADS, HEAD, CHUNK)
        self.vt_s[...] = vt.reshape(HEADS, HEAD, CHUNK)

        def pair(p, carry):
            for hh in range(2):
                h = 2 * p + hh
                s = dot(self.k_s[p, at_rows], self.qt_m[h])
                if live is not None:
                    s = jnp.concatenate(
                        [jnp.where(live[0], s[:TILE], -1e30), jnp.where(live[1], s[TILE:], -1e30)], axis=0
                    )
                before = self.top[h]
                top = jnp.maximum(before, jnp.max(s, axis=0, keepdims=True))
                e = jnp.exp(s - top)
                scale = jnp.exp(before - top)
                self.top[h] = top
                self.tops[c, h] = top
                self.e_s[h, at_rows] = e
                self.den[h] = self.den[h] * scale + jnp.sum(e, axis=0, keepdims=True)
                self.o_t[h] = self.o_t[h] * scale + dot(self.vt_s[h], e.astype(BF16))
            return carry

        lax.fori_loop(0, 4, pair, 0)

    def settle(self):
        for h in range(HEADS):
            inverse = 1.0 / self.den[h]
            o = self.o_t[h] * inverse
            self.o_t[h] = o
            self.den[h] = inverse
            self.delta[h] = jnp.sum(o * self.at_s[h], axis=0, keepdims=True)

    def backward(self, c):
        at_rows = slice(c * CHUNK, c * CHUNK + CHUNK)

        def pair(p, carry):
            ds, pb = [], []
            for hh in range(2):
                h = 2 * p + hh
                dp = dot(self.v_s[p, at_rows], self.at_m[h])
                prob = self.e_s[h, at_rows] * (jnp.exp(self.tops[c, h] - self.top[h]) * self.den[h])
                pb.append(prob.astype(BF16))
                ds.append((prob * (dp - self.delta[h])).astype(BF16))
                self.dq_t[h] = self.dq_t[h] + dot(self.kt_s[h, :, at_rows], ds[hh])
            self.dkv[:, pl.ds(pl.multiple_of(p * 128, 128), 128)] = dot(
                jnp.concatenate(ds, axis=1), self.q_m[p]
            )
            self.dkv[:, pl.ds(pl.multiple_of(WIDTH + p * 128, 128), 128)] = dot(
                jnp.concatenate(pb, axis=1), self.a_m[p]
            )
            return carry

        lax.fori_loop(0, 4, pair, 0)
        if c < CHUNKS - 1:
            pieces = (self.dkv[...].astype(BF16),)
        else:
            pieces = split(self.dkv[...])
        return sum(
            dot_t(piece[:, :WIDTH], self.wk[...]) + dot_t(piece[:, WIDTH:], self.wv[...]) for piece in pieces
        )

    def updated(self):
        attended = self.o_t[...].reshape(WIDTH, ROWS).T.astype(BF16)
        return dot(attended, self.wo[...]).astype(BF16)

    def user_grad(self):
        d_query = (self.dq_t[...] * (HEAD**-0.5)).reshape(WIDTH, ROWS).T.astype(BF16)
        return dot_t(d_query, self.wq[...]).astype(BF16)


def ring_peer(place, way, hops=1):
    return place.z_hi * 8 + place.along_y(hops if way == 0 else -hops)


class Ring:
    semaphores = [
        pltpu.SemaphoreType.DMA((2, 2, 8)),
        pltpu.SemaphoreType.DMA((2, 2, 8)),
        pltpu.SemaphoreType.DMA((2,)),
        pltpu.SemaphoreType.DMA((2,)),
    ]

    def __init__(self, place, sems):
        self.place = place
        self.send_sem, self.recv_sem, self.zs, self.zr = sems
        self.copies, self.across = {}, {}

    def column(self, chain):
        return (self.place.z_hi if chain == 0 else 1 - self.place.z_hi) * 8

    def push(self, chain, way, number, source, target):
        copy = pltpu.make_async_remote_copy(
            src_ref=source, dst_ref=target,
            send_sem=self.send_sem.at[chain, way, number], recv_sem=self.recv_sem.at[chain, way, number],
            device_id=(self.place.user, ring_peer(self.place, way)), device_id_type=MESH,
        )
        copy.start()
        self.copies[chain, way, number] = copy

    def wait(self, chain, way, number):
        self.copies[chain, way, number].wait_recv()

    def cross(self, tile, source, target):
        copy = pltpu.make_async_remote_copy(
            src_ref=source, dst_ref=target, send_sem=self.zs.at[tile], recv_sem=self.zr.at[tile],
            device_id=self.place.partner(), device_id_type=MESH,
        )
        copy.start()
        self.across[tile] = copy

    def finish(self):
        for copy in list(self.across.values()) + list(self.copies.values()):
            copy.wait_send()


def tile_rows(tile):
    return pl.ds(tile * TILE, TILE)


class Gather(Ring):
    scratch = [
        pltpu.VMEM((2, 2, TILE, WIDTH), BF16),
        pltpu.VMEM((2, 2, TILE // 2, WIDTH), BF16),
        pltpu.VMEM((2, 2, TILE, WIDTH), BF16),
        pltpu.VMEM((2, 2, TILE // 2, WIDTH), BF16),
        pltpu.VMEM((2, 2, TILE // 2, WIDTH), BF16),
    ] + Ring.semaphores

    def __init__(self, place, lists, x_ref, all_ref, scratch):
        self.lists, self.x, self.all = lists, x_ref, all_ref
        self.out3, self.out4, self.in3, self.via3, self.in4 = scratch[:5]
        super().__init__(place, scratch[5:])

    def source(self, chain, way, hops):
        return self.column(chain) + self.place.along_y(-hops if way == 0 else hops)

    def block(self, chain, index, own):
        return self.x if own and chain == 0 else self.all.at[index]

    def cross_tile(self, tile):
        self.cross(tile, self.x.at[tile_rows(tile)], self.all.at[self.place.item, tile_rows(tile)])

    def first(self, chain, tile):
        index = self.source(chain, 0, 0)
        for way in range(2):
            source = self.block(chain, index, True).at[tile_rows(tile)]
            self.push(chain, way, tile, source, self.all.at[index, tile_rows(tile)])

    def second(self, chain):
        for tile in range(2):
            for way in range(2):
                self.wait(chain, way, tile)
                part = self.all.at[self.source(chain, way, 1), tile_rows(tile)]
                self.push(chain, way, 2 + tile, part, part)

    def third(self, chain):
        for way in range(2):
            index = self.source(chain, way, 2)
            for tile in range(2):
                self.wait(chain, way, 2 + tile)
            far = self.lists[ring_peer(self.place, way, 2), index] == 1
            low = way * (TILE // 2)
            self.out4[chain, way] = jnp.where(
                far,
                self.all[index, TILE + low : TILE + low + TILE // 2],
                self.all[index, low : low + TILE // 2],
            )
            self.push(chain, way, 4, self.out4.at[chain, way], self.via3.at[chain, way])
            near = self.lists[ring_peer(self.place, way, 1), index] == 1
            self.out3[chain, way] = jnp.where(near, self.all[index, TILE:], self.all[index, :TILE])
            self.push(chain, way, 5, self.out3.at[chain, way], self.in3.at[chain, way])

    def fourth(self, chain):
        for way in range(2):
            self.wait(chain, way, 4)
            self.push(chain, way, 6, self.via3.at[chain, way], self.in4.at[chain, way])

    def tiles(self, chain, e):
        found, live = [], []
        for way in ((1, 0) if e else (None, 4)):
            hops = 4 if way == 4 else e
            index = self.source(chain, 0 if way in (None, 4) else way, hops)
            tile = self.lists[self.place.item, index]
            live.append(tile < 2)
            if way == 4:
                for way in range(2):
                    self.wait(chain, way, 6)
                    found.append(self.in4[chain, way])
            elif e == 3:
                self.wait(chain, way, 5)
                found.append(self.in3[chain, way])
            else:
                block = self.block(chain, index, e == 0)
                found.append(jnp.where(tile == 1, block[TILE:], block[:TILE]))
        return jnp.concatenate(found, axis=0), live


class Scatter(Ring):
    scratch = [
        pltpu.VMEM((2, 2, TILE // 2, WIDTH), BF16),
        pltpu.VMEM((2, 2, TILE // 2, WIDTH), BF16),
        pltpu.VMEM((2, 2, TILE // 2, WIDTH), BF16),
        pltpu.VMEM((2, 2, TILE, WIDTH), BF16),
        pltpu.VMEM((2, 2, TILE, WIDTH), BF16),
        pltpu.VMEM((2, 2, 2, TILE, WIDTH), BF16),
        pltpu.VMEM((2, 2, 2, TILE, WIDTH), BF16),
        pltpu.VMEM((2, 2, 2, TILE, WIDTH), BF16),
        pltpu.VMEM((2, 2, 2, TILE, WIDTH), BF16),
        pltpu.VMEM((2, TILE, WIDTH), BF16),
        pltpu.VMEM((2, TILE, WIDTH), BF16),
        pltpu.VMEM((8, CHUNK, WIDTH), F32),
    ] + Ring.semaphores

    def __init__(self, place, lists, scratch):
        self.lists = lists
        (self.out4, self.via3, self.in4, self.out3, self.in3, self.out2, self.in2, self.out1, self.in1,
         self.z_out, self.z_in, self.grads) = scratch[:12]
        super().__init__(place, scratch[12:])

    def owner(self, chain, way, hops):
        return self.column(chain) + self.place.along_y(hops if way == 0 else -hops)

    def own(self, chain, way, e):
        return self.grads[chain * 4 + e, tile_rows(0 if way == 0 else 1)]

    def lists_here(self, index, tile):
        return self.lists[self.place.item, index] == tile

    def send4(self, chain):
        for way in range(2):
            low = TILE + way * (TILE // 2)
            self.out4[chain, way] = self.grads[chain * 4, low : low + TILE // 2].astype(BF16)
            self.push(chain, way, 0, self.out4.at[chain, way], self.via3.at[chain, way])

    def send3(self, chain):
        for way in range(2):
            self.out3[chain, way] = self.own(chain, way, 3).astype(BF16)
            self.wait(chain, way, 0)
            self.push(chain, way, 1, self.via3.at[chain, way], self.in4.at[chain, way])
            self.push(chain, way, 2, self.out3.at[chain, way], self.in3.at[chain, way])

    def send2(self, chain):
        for way in range(2):
            index = self.owner(chain, way, 2)
            one, two = ring_peer(self.place, way, -1), ring_peer(self.place, way, -2)
            self.wait(chain, way, 1)
            self.wait(chain, way, 2)
            half = slice(way * (TILE // 2), way * (TILE // 2) + TILE // 2)
            other = slice((1 - way) * (TILE // 2), (1 - way) * (TILE // 2) + TILE // 2)
            for tile in range(2):
                value = jnp.where(self.lists_here(index, tile), self.own(chain, way, 2), 0.0)
                value = value + jnp.where(
                    self.lists[one, index] == tile, self.in3[chain, way].astype(F32), 0.0
                )
                far = jnp.where(self.lists[two, index] == tile, self.in4[chain, way].astype(F32), 0.0)
                self.out2[chain, way, tile, half] = (value[half] + far).astype(BF16)
                self.out2[chain, way, tile, other] = value[other].astype(BF16)
                self.push(chain, way, 3 + tile, self.out2.at[chain, way, tile], self.in2.at[chain, way, tile])

    def send1(self, chain):
        for tile in range(2):
            for way in range(2):
                index = self.owner(chain, way, 1)
                self.wait(chain, way, 3 + tile)
                value = jnp.where(self.lists_here(index, tile), self.own(chain, way, 1), 0.0)
                value = value + self.in2[chain, way, tile].astype(F32)
                self.out1[chain, way, tile] = value.astype(BF16)
                self.push(chain, way, 5 + tile, self.out1.at[chain, way, tile], self.in1.at[chain, way, tile])

    def total(self, chain, tile):
        for way in range(2):
            self.wait(chain, way, 5 + tile)
        value = jnp.where(self.lists_here(self.owner(chain, 0, 0), tile), self.own(chain, 0, 0), 0.0)
        return value + self.in1[chain, 0, tile].astype(F32) + self.in1[chain, 1, tile].astype(F32)

    def send_across(self):
        for tile in range(2):
            self.z_out[tile] = self.total(1, tile).astype(BF16)
            self.cross(tile, self.z_out.at[tile], self.z_in.at[tile])


def take(scratch, count):
    taken = scratch[:count]
    del scratch[:count]
    return taken


def kernel(
    lists_ref, user_ref, x_ref, proj_ref, wq_ref, wk_ref, wv_ref, wo_ref, cot_ref,
    upd_ref, ug_ref, out_ref, all_x, part, lin_sum, lin_total, own_part, *scratch
):
    scratch = list(scratch)
    place = Place()
    gather = Gather(place, lists_ref, x_ref, all_x, take(scratch, len(Gather.scratch)))
    scatter = Scatter(place, lists_ref, take(scratch, len(Scatter.scratch)))
    lin = Total(place, part, lin_sum, take(scratch, len(Total.scratch)))
    d_lin = Total(place, own_part, lin_total, take(scratch, len(Total.scratch)))
    attention = Attention((wq_ref, wk_ref, wv_ref, wo_ref), scratch)

    def chunk_forward(chain, e):
        rows, live = gather.tiles(chain, e)
        attention.forward(chain * 4 + e, (rows,), live)

    def chunk_backward(chain, e):
        scatter.grads[chain * 4 + e] = attention.backward(chain * 4 + e)

    greet(place)
    for tile in range(2):
        gather.first(0, tile)
        gather.cross_tile(tile)
    total = lax.dot_general(
        proj_ref[...], x_ref[...], (((0,), (0,)), ((), ())), preferred_element_type=F32
    )
    for k in range(8):
        part[k] = total[k * 32 : k * 32 + 32]
    lin.step(0)
    attention.prepare(user_ref, cot_ref)
    gather.second(0)
    chunk_forward(0, 1)
    lin.step(1)
    gather.third(0)
    for tile in range(2):
        gather.across[tile].wait_recv()
        gather.first(1, tile)
    chunk_forward(0, 2)
    lin.step(2)
    gather.fourth(0)
    chunk_forward(0, 3)
    lin.step(3)
    gather.second(1)
    chunk_forward(0, 0)
    chunk_forward(1, 1)
    lin.step(4)
    gather.third(1)
    chunk_forward(1, 2)
    gather.fourth(1)
    lin.arrive(4)
    attention.forward(8, split(lin_sum[...].reshape(RANK, WIDTH)), None)
    chunk_forward(1, 3)
    chunk_forward(1, 0)
    attention.settle()

    chunk_backward(1, 0)
    scatter.send4(1)
    chunk_backward(1, 3)
    scatter.send3(1)
    chunk_backward(0, 0)
    scatter.send4(0)
    g = attention.backward(8)
    for k in range(8):
        own_part[k] = g[k * 32 : k * 32 + 32]
    d_lin.step(0)
    chunk_backward(1, 2)
    scatter.send2(1)
    chunk_backward(0, 3)
    scatter.send3(0)
    d_lin.step(1)
    chunk_backward(1, 1)
    scatter.send1(1)
    chunk_backward(0, 2)
    scatter.send2(0)
    d_lin.step(2)
    chunk_backward(0, 1)
    scatter.send_across()
    d_lin.step(3)
    scatter.send1(0)
    upd_ref[...] = attention.updated()
    ug_ref[...] = attention.user_grad()
    d_lin.step(4)
    d_lin.arrive(4)
    back = jnp.zeros((ROWS, WIDTH), F32)
    for piece in split(lin_total[...].reshape(RANK, WIDTH)):
        back = back + dot(proj_ref[...], piece)
    for tile in range(2):
        value = back[tile * TILE : tile * TILE + TILE] + scatter.total(0, tile)
        scatter.across[tile].wait_recv()
        out_ref[tile * TILE : tile * TILE + TILE] = (value + scatter.z_in[tile].astype(F32)).astype(BF16)
    lin.finish()
    d_lin.finish()
    gather.finish()
    scatter.finish()


def in_vmem(count):
    return [pl.BlockSpec(memory_space=pltpu.VMEM)] * count


def per_device(user_x, item_x, lin_proj, tile_lists, w_q, w_k, w_v, w_o, cotangent):
    shape = jax.ShapeDtypeStruct
    sums = pltpu.VMEM((8, 32, WIDTH), F32)
    return pl.pallas_call(
        kernel,
        out_shape=[shape((ROWS, WIDTH), BF16)] * 3,
        in_specs=[pl.BlockSpec(memory_space=pltpu.SMEM)] + in_vmem(8),
        out_specs=in_vmem(3),
        scratch_shapes=[
            pltpu.VMEM((OWNERS, ROWS, WIDTH), BF16),
            sums, sums, sums, sums,
        ] + Gather.scratch + Scatter.scratch + Total.scratch + Total.scratch + Attention.scratch,
        compiler_params=pltpu.CompilerParams(
            collective_id=0, has_side_effects=True, vmem_limit_bytes=VMEM_BYTES
        ),
        name="attend_and_exchange",
    )(tile_lists, user_x, item_x, lin_proj, w_q, w_k, w_v, w_o, cotangent)


def solution(mesh):
    rows = P(("user", "item"), None)
    return jax.shard_map(
        per_device,
        mesh=mesh,
        in_specs=(rows, rows, rows, P("user", None), P(), P(), P(), P(), rows),
        out_specs=(rows, rows, rows),
        check_vma=False,
    )
```

```python
import functools

import jax
import jax.numpy as jnp
from jax import lax
from jax.experimental import pallas as pl
from jax.experimental.pallas import tpu as pltpu
from jax.sharding import PartitionSpec as P

F32, BF16 = jnp.float32, jnp.bfloat16
HEADS, HEAD, WIDTH, TILE, RANK = 8, 64, 512, 128, 256
ROWS = 256
OWNERS = 16
KEYS = OWNERS * TILE + RANK
CHUNK = 256
CHUNKS = KEYS // CHUNK
VMEM_BYTES = 60 * 1024 * 1024
MESH = pl.DeviceIdType.MESH


def dot(a, b):
    return lax.dot_general(a, b, (((1,), (0,)), ((), ())), preferred_element_type=F32)


def dot_t(a, b):
    return lax.dot_general(a, b, (((1,), (1,)), ((), ())), preferred_element_type=F32)


def split(a):
    high = a.astype(BF16)
    return high, (a - high.astype(F32)).astype(BF16)


class Place:
    def __init__(self):
        self.user, self.item = lax.axis_index("user"), lax.axis_index("item")
        self.near = lax.rem(self.user, 8)
        self.z_lo = lax.div(self.user, 8)
        self.y = lax.rem(self.item, 8)
        self.z_hi = lax.div(self.item, 8)
        self.z = self.z_hi * 4 + self.z_lo
        self.member = (self.near, self.z, self.y)

    def peer(self, group, k):
        if group == 0:
            return (self.z_lo * 8 + k, self.item)
        if group == 1:
            return (lax.rem(k, 4) * 8 + self.near, lax.div(k, 4) * 8 + self.y)
        return (self.user, self.z_hi * 8 + k)

    def along_y(self, step):
        return lax.rem(self.y + step + 8, 8)

    def partner(self):
        return (self.user, lax.rem(self.item + 8, 16))


def greet(place):
    barrier = pltpu.get_barrier_semaphore()
    for group in range(3):
        for r in range(1, 8):
            k = lax.rem(place.member[group] + r, 8)
            pl.semaphore_signal(barrier, inc=1, device_id=place.peer(group, k), device_id_type=MESH)
    pl.semaphore_wait(barrier, 21)


class Total:
    scratch = [
        pltpu.VMEM((8, 32, WIDTH), F32),
        pltpu.VMEM((8, 8, 256), F32),
        pltpu.VMEM((8, 8, 256), F32),
        pltpu.VMEM((8, 256), F32),
        pltpu.VMEM((8, 8, 256), F32),
        pltpu.VMEM((8, 256), F32),
        pltpu.VMEM((8, 8, 256), F32),
        pltpu.VMEM((32, WIDTH), F32),
        pltpu.SemaphoreType.DMA((5, 8)),
        pltpu.SemaphoreType.DMA((5, 8)),
    ]

    def __init__(self, place, part, out, scratch):
        self.place, self.part, self.out = place, part, out
        (self.land1, self.s1, self.land2, self.s2, self.land3, self.s3, self.land4, self.s4) = scratch[:8]
        self.send_sem, self.recv_sem = scratch[8:]
        self.started = [[] for _ in range(5)]

    def start(self, phase, group, source, land):
        me = self.place.member[group]
        for r in range(1, 8):
            k = lax.rem(me + r, 8)
            copy = pltpu.make_async_remote_copy(
                src_ref=source(k),
                dst_ref=land.at[me],
                send_sem=self.send_sem.at[phase, r],
                recv_sem=self.recv_sem.at[phase, r],
                device_id=self.place.peer(group, k),
                device_id_type=MESH,
            )
            copy.start()
            self.started[phase].append(copy)

    def arrive(self, phase):
        for copy in self.started[phase]:
            copy.wait_recv()

    def step(self, phase):
        near, z, y = self.place.member
        if phase == 0:
            self.start(0, 0, lambda k: self.part.at[k], self.land1)
            self.land1[near] = self.part[near]
            return
        self.arrive(phase - 1)
        if phase == 1:
            total = self.land1[0]
            for k in range(1, 8):
                total = total + self.land1[k]
            for p in range(8):
                self.s1[p] = total[p // 2 * 8 : p // 2 * 8 + 8, p % 2 * 256 : p % 2 * 256 + 256]
            self.start(1, 1, lambda k: self.s1.at[k], self.land2)
            self.land2[z] = self.s1[z]
        elif phase == 2:
            total = self.land2[0]
            for k in range(1, 8):
                total = total + self.land2[k]
            self.s2[...] = total
            self.start(2, 2, lambda k: self.s2, self.land3)
            self.land3[y] = total
        elif phase == 3:
            total = self.land3[0]
            for k in range(1, 8):
                total = total + self.land3[k]
            self.s3[...] = total
            self.start(3, 1, lambda k: self.s3, self.land4)
            self.land4[z] = total
        elif phase == 4:
            for p in range(8):
                self.s4[p // 2 * 8 : p // 2 * 8 + 8, p % 2 * 256 : p % 2 * 256 + 256] = self.land4[p]
            self.start(4, 0, lambda k: self.s4, self.out)
            self.out[near] = self.s4[...]

    def finish(self):
        for copies in self.started:
            for copy in copies:
                copy.wait_send()


class Attention:
    scratch = [
        pltpu.VMEM((4, KEYS, 128), BF16),
        pltpu.VMEM((4, KEYS, 128), BF16),
        pltpu.VMEM((HEADS, HEAD, KEYS), BF16),
        pltpu.VMEM((HEADS, HEAD, CHUNK), BF16),
        pltpu.VMEM((HEADS, 128, ROWS), BF16),
        pltpu.VMEM((HEADS, 128, ROWS), BF16),
        pltpu.VMEM((4, 2 * ROWS, 128), BF16),
        pltpu.VMEM((4, 2 * ROWS, 128), BF16),
        pltpu.VMEM((HEADS, HEAD, ROWS), F32),
        pltpu.VMEM((HEADS, KEYS, ROWS), F32),
        pltpu.VMEM((CHUNK, 2 * WIDTH), F32),
        pltpu.VMEM((HEADS, HEAD, ROWS), F32),
        pltpu.VMEM((HEADS, HEAD, ROWS), F32),
        pltpu.VMEM((HEADS, 1, ROWS), F32),
        pltpu.VMEM((HEADS, 1, ROWS), F32),
        pltpu.VMEM((HEADS, 1, ROWS), F32),
        pltpu.VMEM((CHUNKS, HEADS, 1, ROWS), F32),
        pltpu.VMEM((WIDTH, WIDTH), BF16),
        pltpu.VMEM((WIDTH, WIDTH), BF16),
    ]

    def __init__(self, weights, scratch):
        self.wq, self.wk, self.wv, self.wo = weights
        (self.k_s, self.v_s, self.kt_s, self.vt_s, self.qt_m, self.at_m, self.q_m, self.a_m, self.at_s,
         self.e_s, self.dkv, self.o_t, self.dq_t, self.top, self.den, self.delta, self.tops,
         self.wk_t, self.wv_t) = scratch

    def prepare(self, user_ref, cot_ref):
        q = dot(user_ref[...], self.wq[...]).astype(BF16).astype(F32) * (HEAD**-0.5)
        a = dot_t(cot_ref[...], self.wo[...]).astype(BF16).astype(F32)
        qt, at = q.T, a.T
        self.at_s[...] = at.reshape(HEADS, HEAD, ROWS)
        low_lane = lax.broadcasted_iota(jnp.int32, (ROWS, 128), 1) < HEAD
        low_row = lax.broadcasted_iota(jnp.int32, (128, ROWS), 0) < HEAD
        for p in range(4):
            cut = slice(p * 128, p * 128 + 128)
            for hh in range(2):
                lane, row = (low_lane, low_row) if hh == 0 else (~low_lane, ~low_row)
                half = slice(hh * ROWS, hh * ROWS + ROWS)
                self.q_m[p, half] = jnp.where(lane, q[:, cut], 0.0).astype(BF16)
                self.a_m[p, half] = jnp.where(lane, a[:, cut], 0.0).astype(BF16)
                self.qt_m[2 * p + hh] = jnp.where(row, qt[cut], 0.0).astype(BF16)
                self.at_m[2 * p + hh] = jnp.where(row, at[cut], 0.0).astype(BF16)
        self.wk_t[...] = self.wk[...].astype(F32).T.astype(BF16)
        self.wv_t[...] = self.wv[...].astype(F32).T.astype(BF16)
        self.top[...] = jnp.full(self.top.shape, -1e30, F32)
        self.den[...] = jnp.zeros(self.den.shape, F32)
        self.o_t[...] = jnp.zeros(self.o_t.shape, F32)
        self.dq_t[...] = jnp.zeros(self.dq_t.shape, F32)

    def forward(self, c, pieces, live):
        at_rows = slice(c * CHUNK, c * CHUNK + CHUNK)
        k = sum(dot(piece, self.wk[...]) for piece in pieces).astype(BF16)
        v = sum(dot(piece, self.wv[...]) for piece in pieces).astype(BF16)
        for p in range(4):
            self.k_s[p, at_rows] = k[:, p * 128 : p * 128 + 128]
            self.v_s[p, at_rows] = v[:, p * 128 : p * 128 + 128]
        kt = sum(dot_t(self.wk_t[...], piece) for piece in pieces).astype(BF16)
        vt = sum(dot_t(self.wv_t[...], piece) for piece in pieces).astype(BF16)
        self.kt_s[:, :, at_rows] = kt.reshape(HEADS, HEAD, CHUNK)
        self.vt_s[...] = vt.reshape(HEADS, HEAD, CHUNK)

        def pair(p, carry):
            for hh in range(2):
                h = 2 * p + hh
                s = dot(self.k_s[p, at_rows], self.qt_m[h])
                if live is not None:
                    s = jnp.concatenate(
                        [jnp.where(live[0], s[:TILE], -1e30), jnp.where(live[1], s[TILE:], -1e30)], axis=0
                    )
                before = self.top[h]
                top = jnp.maximum(before, jnp.max(s, axis=0, keepdims=True))
                e = jnp.exp(s - top)
                scale = jnp.exp(before - top)
                self.top[h] = top
                self.tops[c, h] = top
                self.e_s[h, at_rows] = e
                self.den[h] = self.den[h] * scale + jnp.sum(e, axis=0, keepdims=True)
                self.o_t[h] = self.o_t[h] * scale + dot(self.vt_s[h], e.astype(BF16))
            return carry

        lax.fori_loop(0, 4, pair, 0)

    def settle(self):
        for h in range(HEADS):
            inverse = 1.0 / self.den[h]
            o = self.o_t[h] * inverse
            self.o_t[h] = o
            self.den[h] = inverse
            self.delta[h] = jnp.sum(o * self.at_s[h], axis=0, keepdims=True)

    def backward(self, c):
        at_rows = slice(c * CHUNK, c * CHUNK + CHUNK)

        def pair(p, carry):
            ds, pb = [], []
            for hh in range(2):
                h = 2 * p + hh
                dp = dot(self.v_s[p, at_rows], self.at_m[h])
                prob = self.e_s[h, at_rows] * (jnp.exp(self.tops[c, h] - self.top[h]) * self.den[h])
                pb.append(prob.astype(BF16))
                ds.append((prob * (dp - self.delta[h])).astype(BF16))
                self.dq_t[h] = self.dq_t[h] + dot(self.kt_s[h, :, at_rows], ds[hh])
            self.dkv[:, pl.ds(pl.multiple_of(p * 128, 128), 128)] = dot(
                jnp.concatenate(ds, axis=1), self.q_m[p]
            )
            self.dkv[:, pl.ds(pl.multiple_of(WIDTH + p * 128, 128), 128)] = dot(
                jnp.concatenate(pb, axis=1), self.a_m[p]
            )
            return carry

        lax.fori_loop(0, 4, pair, 0)
        if c < CHUNKS - 1:
            pieces = (self.dkv[...].astype(BF16),)
        else:
            pieces = split(self.dkv[...])
        return sum(
            dot_t(piece[:, :WIDTH], self.wk[...]) + dot_t(piece[:, WIDTH:], self.wv[...]) for piece in pieces
        )

    def attended(self):
        return self.o_t[...].reshape(WIDTH, ROWS).T.astype(BF16)

    def d_query(self):
        return (self.dq_t[...] * (HEAD**-0.5)).reshape(WIDTH, ROWS).T.astype(BF16)


def ring_peer(place, way, hops=1):
    return place.z_hi * 8 + place.along_y(hops if way == 0 else -hops)


class Ring:
    semaphores = [
        pltpu.SemaphoreType.DMA((2, 2, 8)),
        pltpu.SemaphoreType.DMA((2, 2, 8)),
        pltpu.SemaphoreType.DMA((4,)),
        pltpu.SemaphoreType.DMA((4,)),
        pltpu.VMEM((2, TILE, WIDTH), BF16),
    ]

    def __init__(self, place, sems):
        self.place = place
        self.send_sem, self.recv_sem, self.zs, self.zr, self.relay_buf = sems
        self.copies, self.across = {}, {}

    def column(self, chain):
        return (self.place.z_hi if chain == 0 else 1 - self.place.z_hi) * 8

    def push(self, chain, way, number, source, target):
        copy = pltpu.make_async_remote_copy(
            src_ref=source, dst_ref=target,
            send_sem=self.send_sem.at[chain, way, number], recv_sem=self.recv_sem.at[chain, way, number],
            device_id=(self.place.user, ring_peer(self.place, way)), device_id_type=MESH,
        )
        copy.start()
        self.copies[chain, way, number] = copy

    def wait(self, chain, way, number):
        self.copies[chain, way, number].wait_recv()

    def leap(self, number, tile, source, target):
        z = lax.rem(self.place.z + (2 if tile == 0 else 6), 8)
        copy = pltpu.make_async_remote_copy(
            src_ref=source, dst_ref=target, send_sem=self.zs.at[number], recv_sem=self.zr.at[number],
            device_id=self.place.peer(1, z), device_id_type=MESH,
        )
        copy.start()
        self.across[number] = copy

    def cross(self, tile, source):
        self.leap(tile, tile, source, self.relay_buf.at[tile])

    def relay(self, tile, target):
        self.across[tile].wait_recv()
        self.leap(2 + tile, tile, self.relay_buf.at[tile], target)

    def wait_cross(self, tile):
        self.across[2 + tile].wait_recv()

    def finish(self):
        for copy in list(self.across.values()) + list(self.copies.values()):
            copy.wait_send()


def tile_rows(tile):
    return pl.ds(tile * TILE, TILE)


class Gather(Ring):
    scratch = [
        pltpu.VMEM((2, 2, TILE, WIDTH), BF16),
        pltpu.VMEM((2, 2, TILE // 2, WIDTH), BF16),
        pltpu.VMEM((2, 2, TILE, WIDTH), BF16),
        pltpu.VMEM((2, 2, TILE // 2, WIDTH), BF16),
        pltpu.VMEM((2, 2, TILE // 2, WIDTH), BF16),
    ] + Ring.semaphores

    def __init__(self, place, lists, x_ref, all_ref, scratch):
        self.lists, self.x, self.all = lists, x_ref, all_ref
        self.out3, self.out4, self.in3, self.via3, self.in4 = scratch[:5]
        super().__init__(place, scratch[5:])

    def source(self, chain, way, hops):
        return self.column(chain) + self.place.along_y(-hops if way == 0 else hops)

    def block(self, chain, index, own):
        return self.x if own and chain == 0 else self.all.at[index]

    def cross_tile(self, tile):
        self.cross(tile, self.x.at[tile_rows(tile)])

    def relay_tile(self, tile):
        z = lax.rem(self.place.z + (6 if tile == 0 else 2), 8)
        self.relay(tile, self.all.at[lax.div(z, 4) * 8 + self.place.y, tile_rows(tile)])

    def first(self, chain, tile):
        index = self.source(chain, 0, 0)
        for way in range(2):
            source = self.block(chain, index, True).at[tile_rows(tile)]
            self.push(chain, way, tile, source, self.all.at[index, tile_rows(tile)])

    def second(self, chain):
        for tile in range(2):
            for way in range(2):
                self.wait(chain, way, tile)
                part = self.all.at[self.source(chain, way, 1), tile_rows(tile)]
                self.push(chain, way, 2 + tile, part, part)

    def third(self, chain):
        for way in range(2):
            index = self.source(chain, way, 2)
            for tile in range(2):
                self.wait(chain, way, 2 + tile)
            far = self.lists[ring_peer(self.place, way, 2), index] == 1
            low = way * (TILE // 2)
            self.out4[chain, way] = jnp.where(
                far,
                self.all[index, TILE + low : TILE + low + TILE // 2],
                self.all[index, low : low + TILE // 2],
            )
            self.push(chain, way, 4, self.out4.at[chain, way], self.via3.at[chain, way])
            near = self.lists[ring_peer(self.place, way, 1), index] == 1
            self.out3[chain, way] = jnp.where(near, self.all[index, TILE:], self.all[index, :TILE])
            self.push(chain, way, 5, self.out3.at[chain, way], self.in3.at[chain, way])

    def fourth(self, chain):
        for way in range(2):
            self.wait(chain, way, 4)
            self.push(chain, way, 6, self.via3.at[chain, way], self.in4.at[chain, way])

    def tiles(self, chain, e):
        found, live = [], []
        for way in ((1, 0) if e else (None, 4)):
            hops = 4 if way == 4 else e
            index = self.source(chain, 0 if way in (None, 4) else way, hops)
            tile = self.lists[self.place.item, index]
            live.append(tile < 2)
            if way == 4:
                for way in range(2):
                    self.wait(chain, way, 6)
                    found.append(self.in4[chain, way])
            elif e == 3:
                self.wait(chain, way, 5)
                found.append(self.in3[chain, way])
            else:
                block = self.block(chain, index, e == 0)
                found.append(jnp.where(tile == 1, block[TILE:], block[:TILE]))
        return jnp.concatenate(found, axis=0), live


class Scatter(Ring):
    scratch = [
        pltpu.VMEM((2, 2, TILE // 2, WIDTH), BF16),
        pltpu.VMEM((2, 2, TILE // 2, WIDTH), BF16),
        pltpu.VMEM((2, 2, TILE // 2, WIDTH), BF16),
        pltpu.VMEM((2, 2, TILE, WIDTH), BF16),
        pltpu.VMEM((2, 2, TILE, WIDTH), BF16),
        pltpu.VMEM((2, 2, 2, TILE, WIDTH), BF16),
        pltpu.VMEM((2, 2, 2, TILE, WIDTH), BF16),
        pltpu.VMEM((2, 2, 2, TILE, WIDTH), BF16),
        pltpu.VMEM((2, 2, 2, TILE, WIDTH), BF16),
        pltpu.VMEM((2, TILE, WIDTH), BF16),
        pltpu.VMEM((2, TILE, WIDTH), BF16),
        pltpu.VMEM((8, CHUNK, WIDTH), F32),
    ] + Ring.semaphores

    def __init__(self, place, lists, scratch):
        self.lists = lists
        (self.out4, self.via3, self.in4, self.out3, self.in3, self.out2, self.in2, self.out1, self.in1,
         self.z_out, self.z_in, self.grads) = scratch[:12]
        super().__init__(place, scratch[12:])

    def owner(self, chain, way, hops):
        return self.column(chain) + self.place.along_y(hops if way == 0 else -hops)

    def own(self, chain, way, e):
        return self.grads[chain * 4 + e, tile_rows(0 if way == 0 else 1)]

    def lists_here(self, index, tile):
        return self.lists[self.place.item, index] == tile

    def send4(self, chain):
        for way in range(2):
            low = TILE + way * (TILE // 2)
            self.out4[chain, way] = self.grads[chain * 4, low : low + TILE // 2].astype(BF16)
            self.push(chain, way, 0, self.out4.at[chain, way], self.via3.at[chain, way])

    def send3(self, chain):
        for way in range(2):
            self.out3[chain, way] = self.own(chain, way, 3).astype(BF16)
            self.wait(chain, way, 0)
            self.push(chain, way, 1, self.via3.at[chain, way], self.in4.at[chain, way])
            self.push(chain, way, 2, self.out3.at[chain, way], self.in3.at[chain, way])

    def send2(self, chain):
        for way in range(2):
            index = self.owner(chain, way, 2)
            one, two = ring_peer(self.place, way, -1), ring_peer(self.place, way, -2)
            self.wait(chain, way, 1)
            self.wait(chain, way, 2)
            half = slice(way * (TILE // 2), way * (TILE // 2) + TILE // 2)
            other = slice((1 - way) * (TILE // 2), (1 - way) * (TILE // 2) + TILE // 2)
            for tile in range(2):
                value = jnp.where(self.lists_here(index, tile), self.own(chain, way, 2), 0.0)
                value = value + jnp.where(
                    self.lists[one, index] == tile, self.in3[chain, way].astype(F32), 0.0
                )
                far = jnp.where(self.lists[two, index] == tile, self.in4[chain, way].astype(F32), 0.0)
                self.out2[chain, way, tile, half] = (value[half] + far).astype(BF16)
                self.out2[chain, way, tile, other] = value[other].astype(BF16)
                self.push(chain, way, 3 + tile, self.out2.at[chain, way, tile], self.in2.at[chain, way, tile])

    def send1(self, chain):
        for tile in range(2):
            for way in range(2):
                index = self.owner(chain, way, 1)
                self.wait(chain, way, 3 + tile)
                value = jnp.where(self.lists_here(index, tile), self.own(chain, way, 1), 0.0)
                value = value + self.in2[chain, way, tile].astype(F32)
                self.out1[chain, way, tile] = value.astype(BF16)
                self.push(chain, way, 5 + tile, self.out1.at[chain, way, tile], self.in1.at[chain, way, tile])

    def total(self, chain, tile):
        for way in range(2):
            self.wait(chain, way, 5 + tile)
        value = jnp.where(self.lists_here(self.owner(chain, 0, 0), tile), self.own(chain, 0, 0), 0.0)
        return value + self.in1[chain, 0, tile].astype(F32) + self.in1[chain, 1, tile].astype(F32)

    def send_across(self):
        for tile in range(2):
            self.z_out[tile] = self.total(1, tile).astype(BF16)
            self.cross(tile, self.z_out.at[tile])

    def relay_total(self):
        for tile in range(2):
            self.relay(tile, self.z_in.at[tile])


def take(scratch, count):
    taken = scratch[:count]
    del scratch[:count]
    return taken


def kernel(
    lists_ref, user_ref, x_ref, proj_ref, wq_ref, wk_ref, wv_ref, wo_ref, cot_ref,
    att_ref, dq_ref, out_ref, all_x, part, lin_sum, lin_total, own_part, *scratch
):
    scratch = list(scratch)
    place = Place()
    gather = Gather(place, lists_ref, x_ref, all_x, take(scratch, len(Gather.scratch)))
    scatter = Scatter(place, lists_ref, take(scratch, len(Scatter.scratch)))
    lin = Total(place, part, lin_sum, take(scratch, len(Total.scratch)))
    d_lin = Total(place, own_part, lin_total, take(scratch, len(Total.scratch)))
    attention = Attention((wq_ref, wk_ref, wv_ref, wo_ref), scratch)

    def chunk_forward(chain, e):
        rows, live = gather.tiles(chain, e)
        attention.forward(chain * 4 + e, (rows,), live)

    def chunk_backward(chain, e):
        scatter.grads[chain * 4 + e] = attention.backward(chain * 4 + e)

    greet(place)
    for tile in range(2):
        gather.first(0, tile)
        gather.cross_tile(tile)
    total = lax.dot_general(
        proj_ref[...], x_ref[...], (((0,), (0,)), ((), ())), preferred_element_type=F32
    )
    for k in range(8):
        part[k] = total[k * 32 : k * 32 + 32]
    lin.step(0)
    attention.prepare(user_ref, cot_ref)
    gather.second(0)
    for tile in range(2):
        gather.relay_tile(tile)
    chunk_forward(0, 1)
    lin.step(1)
    gather.third(0)
    for tile in range(2):
        gather.wait_cross(tile)
        gather.first(1, tile)
    chunk_forward(0, 2)
    lin.step(2)
    gather.fourth(0)
    chunk_forward(0, 3)
    lin.step(3)
    gather.second(1)
    chunk_forward(0, 0)
    chunk_forward(1, 1)
    lin.step(4)
    gather.third(1)
    chunk_forward(1, 2)
    gather.fourth(1)
    lin.arrive(4)
    attention.forward(8, split(lin_sum[...].reshape(RANK, WIDTH)), None)
    chunk_forward(1, 3)
    chunk_forward(1, 0)
    attention.settle()

    chunk_backward(1, 0)
    scatter.send4(1)
    att_ref[...] = attention.attended()
    chunk_backward(1, 3)
    scatter.send3(1)
    chunk_backward(0, 0)
    scatter.send4(0)
    g = attention.backward(8)
    for k in range(8):
        own_part[k] = g[k * 32 : k * 32 + 32]
    d_lin.step(0)
    chunk_backward(1, 2)
    scatter.send2(1)
    chunk_backward(0, 3)
    scatter.send3(0)
    d_lin.step(1)
    chunk_backward(1, 1)
    scatter.send1(1)
    d_lin.step(2)
    chunk_backward(0, 2)
    scatter.send2(0)
    d_lin.step(3)
    chunk_backward(0, 1)
    scatter.send_across()
    d_lin.step(4)
    scatter.send1(0)
    dq_ref[...] = attention.d_query()
    scatter.relay_total()
    d_lin.arrive(4)
    back = jnp.zeros((ROWS, WIDTH), F32)
    for piece in split(lin_total[...].reshape(RANK, WIDTH)):
        back = back + dot(proj_ref[...], piece)
    for tile in range(2):
        value = back[tile * TILE : tile * TILE + TILE] + scatter.total(0, tile)
        scatter.wait_cross(tile)
        out_ref[tile * TILE : tile * TILE + TILE] = value + scatter.z_in[tile].astype(F32)
    lin.finish()
    d_lin.finish()
    gather.finish()
    scatter.finish()


def finish_kernel(att_ref, dq_ref, grad_ref, wq_ref, wo_ref, upd_ref, ug_ref, out_ref):
    upd_ref[...] = dot(att_ref[...], wo_ref[...]).astype(BF16)
    ug_ref[...] = dot_t(dq_ref[...], wq_ref[...]).astype(BF16)
    out_ref[...] = grad_ref[...].astype(BF16)


def in_vmem(count):
    return [pl.BlockSpec(memory_space=pltpu.VMEM)] * count


def per_device(user_x, item_x, lin_proj, tile_lists, w_q, w_k, w_v, w_o, cotangent):
    shape = jax.ShapeDtypeStruct
    sums = pltpu.VMEM((8, 32, WIDTH), F32)
    attended, d_query, grad = pl.pallas_call(
        kernel,
        out_shape=[shape((ROWS, WIDTH), BF16)] * 2 + [shape((ROWS, WIDTH), F32)],
        in_specs=[pl.BlockSpec(memory_space=pltpu.SMEM)] + in_vmem(8),
        out_specs=in_vmem(3),
        scratch_shapes=[
            pltpu.VMEM((OWNERS, ROWS, WIDTH), BF16),
            sums, sums, sums, sums,
        ] + Gather.scratch + Scatter.scratch + Total.scratch + Total.scratch + Attention.scratch,
        compiler_params=pltpu.CompilerParams(
            collective_id=0, has_side_effects=True, vmem_limit_bytes=VMEM_BYTES
        ),
        name="attend_and_exchange",
    )(tile_lists, user_x, item_x, lin_proj, w_q, w_k, w_v, w_o, cotangent)
    return pl.pallas_call(
        finish_kernel,
        out_shape=[shape((ROWS, WIDTH), BF16)] * 3,
        in_specs=in_vmem(5),
        out_specs=in_vmem(3),
        compiler_params=pltpu.CompilerParams(vmem_limit_bytes=VMEM_BYTES),
        name="finish",
    )(attended, d_query, grad, w_q, w_o)


def solution(mesh):
    rows = P(("user", "item"), None)
    return jax.shard_map(
        per_device,
        mesh=mesh,
        in_specs=(rows, rows, rows, P("user", None), P(), P(), P(), P(), rows),
        out_specs=(rows, rows, rows),
        check_vma=False,
    )
```

```python
import functools

import jax
import jax.numpy as jnp
from jax import lax
from jax.experimental import pallas as pl
from jax.experimental.pallas import tpu as pltpu
from jax.sharding import PartitionSpec as P

F32, BF16 = jnp.float32, jnp.bfloat16
HEADS, HEAD, WIDTH, TILE, RANK = 8, 64, 512, 128, 256
ROWS = 256
OWNERS = 16
KEYS = OWNERS * TILE + RANK
CHUNK = 256
CHUNKS = KEYS // CHUNK
VMEM_BYTES = 60 * 1024 * 1024
MESH = pl.DeviceIdType.MESH
ORDER = ((0, 1), (0, 2), (0, 3), (1, 1), (0, 0), (1, 2), None, (1, 3), (1, 0))
LINFORMER = 6


def dot(a, b):
    return lax.dot_general(a, b, (((1,), (0,)), ((), ())), preferred_element_type=F32)


def dot_t(a, b):
    return lax.dot_general(a, b, (((1,), (1,)), ((), ())), preferred_element_type=F32)


def split(a):
    high = a.astype(BF16)
    return high, (a - high.astype(F32)).astype(BF16)


class Place:
    def __init__(self):
        self.user, self.item = lax.axis_index("user"), lax.axis_index("item")
        self.near = lax.rem(self.user, 8)
        self.z_lo = lax.div(self.user, 8)
        self.y = lax.rem(self.item, 8)
        self.z_hi = lax.div(self.item, 8)
        self.z = self.z_hi * 4 + self.z_lo
        self.member = (self.near, self.z, self.y)

    def peer(self, group, k):
        if group == 0:
            return (self.z_lo * 8 + k, self.item)
        if group == 1:
            return (lax.rem(k, 4) * 8 + self.near, lax.div(k, 4) * 8 + self.y)
        return (self.user, self.z_hi * 8 + k)

    def along_y(self, step):
        return lax.rem(self.y + step + 8, 8)

    def partner(self):
        return (self.user, lax.rem(self.item + 8, 16))


def greet(place):
    barrier = pltpu.get_barrier_semaphore()
    for group in range(3):
        for r in range(1, 8):
            k = lax.rem(place.member[group] + r, 8)
            pl.semaphore_signal(barrier, inc=1, device_id=place.peer(group, k), device_id_type=MESH)
    pl.semaphore_wait(barrier, 21)


class Total:
    scratch = [
        pltpu.VMEM((8, 32, WIDTH), F32),
        pltpu.VMEM((8, 8, 256), F32),
        pltpu.VMEM((8, 8, 256), F32),
        pltpu.VMEM((8, 256), F32),
        pltpu.VMEM((8, 8, 256), F32),
        pltpu.VMEM((8, 256), F32),
        pltpu.VMEM((8, 8, 256), F32),
        pltpu.VMEM((32, WIDTH), F32),
        pltpu.SemaphoreType.DMA((5, 8)),
        pltpu.SemaphoreType.DMA((5, 8)),
    ]

    def __init__(self, place, part, out, scratch):
        self.place, self.part, self.out = place, part, out
        (self.land1, self.s1, self.land2, self.s2, self.land3, self.s3, self.land4, self.s4) = scratch[:8]
        self.send_sem, self.recv_sem = scratch[8:]

    def copies(self, phase):
        group = (0, 1, 2, 1, 0)[phase]
        land = (self.land1, self.land2, self.land3, self.land4, self.out)[phase]
        me = self.place.member[group]
        for r in range(1, 8):
            k = lax.rem(me + r, 8)
            source = (self.part.at[k], self.s1.at[k], self.s2, self.s3, self.s4)[phase]
            yield pltpu.make_async_remote_copy(
                src_ref=source,
                dst_ref=land.at[me],
                send_sem=self.send_sem.at[phase, r],
                recv_sem=self.recv_sem.at[phase, r],
                device_id=self.place.peer(group, k),
                device_id_type=MESH,
            )

    def start(self, phase):
        for copy in self.copies(phase):
            copy.start()

    def arrive(self, phase):
        for copy in self.copies(phase):
            copy.wait_recv()

    def step(self, phase):
        near, z, y = self.place.member
        if phase == 0:
            self.start(0)
            self.land1[near] = self.part[near]
            return
        self.arrive(phase - 1)
        if phase == 1:
            total = self.land1[0]
            for k in range(1, 8):
                total = total + self.land1[k]
            for p in range(8):
                self.s1[p] = total[p // 2 * 8 : p // 2 * 8 + 8, p % 2 * 256 : p % 2 * 256 + 256]
            self.start(1)
            self.land2[z] = self.s1[z]
        elif phase == 2:
            total = self.land2[0]
            for k in range(1, 8):
                total = total + self.land2[k]
            self.s2[...] = total
            self.start(2)
            self.land3[y] = total
        elif phase == 3:
            total = self.land3[0]
            for k in range(1, 8):
                total = total + self.land3[k]
            self.s3[...] = total
            self.start(3)
            self.land4[z] = total
        elif phase == 4:
            for p in range(8):
                self.s4[p // 2 * 8 : p // 2 * 8 + 8, p % 2 * 256 : p % 2 * 256 + 256] = self.land4[p]
            self.start(4)
            self.out[near] = self.s4[...]

    def finish(self):
        for phase in range(5):
            for copy in self.copies(phase):
                copy.wait_send()


class Attention:
    scratch = [
        pltpu.VMEM((CHUNKS, 4, CHUNK, 128), BF16),
        pltpu.VMEM((CHUNKS, 4, CHUNK, 128), BF16),
        pltpu.VMEM((CHUNKS, HEADS, HEAD, CHUNK), BF16),
        pltpu.VMEM((HEADS, HEAD, CHUNK), BF16),
        pltpu.VMEM((HEADS, 128, ROWS), BF16),
        pltpu.VMEM((HEADS, 128, ROWS), BF16),
        pltpu.VMEM((4, 2 * ROWS, 128), BF16),
        pltpu.VMEM((4, 2 * ROWS, 128), BF16),
        pltpu.VMEM((HEADS, HEAD, ROWS), F32),
        pltpu.VMEM((CHUNKS, HEADS, CHUNK, ROWS), F32),
        pltpu.VMEM((CHUNK, 2 * WIDTH), F32),
        pltpu.VMEM((HEADS, HEAD, ROWS), F32),
        pltpu.VMEM((HEADS, HEAD, ROWS), F32),
        pltpu.VMEM((HEADS, 1, ROWS), F32),
        pltpu.VMEM((HEADS, 1, ROWS), F32),
        pltpu.VMEM((HEADS, 1, ROWS), F32),
        pltpu.VMEM((CHUNKS, HEADS, 1, ROWS), F32),
        pltpu.VMEM((WIDTH, WIDTH), BF16),
        pltpu.VMEM((WIDTH, WIDTH), BF16),
    ]

    def __init__(self, weights, scratch):
        self.wq, self.wk, self.wv, self.wo = weights
        (self.k_s, self.v_s, self.kt_s, self.vt_s, self.qt_m, self.at_m, self.q_m, self.a_m, self.at_s,
         self.e_s, self.dkv, self.o_t, self.dq_t, self.top, self.den, self.delta, self.tops,
         self.wk_t, self.wv_t) = scratch

    def prepare(self, user_ref, cot_ref):
        q = dot(user_ref[...], self.wq[...]).astype(BF16).astype(F32) * (HEAD**-0.5)
        a = dot_t(cot_ref[...], self.wo[...]).astype(BF16).astype(F32)
        qt, at = q.T, a.T
        self.at_s[...] = at.reshape(HEADS, HEAD, ROWS)
        low_lane = lax.broadcasted_iota(jnp.int32, (ROWS, 128), 1) < HEAD
        low_row = lax.broadcasted_iota(jnp.int32, (128, ROWS), 0) < HEAD
        for p in range(4):
            cut = slice(p * 128, p * 128 + 128)
            for hh in range(2):
                lane, row = (low_lane, low_row) if hh == 0 else (~low_lane, ~low_row)
                half = slice(hh * ROWS, hh * ROWS + ROWS)
                self.q_m[p, half] = jnp.where(lane, q[:, cut], 0.0).astype(BF16)
                self.a_m[p, half] = jnp.where(lane, a[:, cut], 0.0).astype(BF16)
                self.qt_m[2 * p + hh] = jnp.where(row, qt[cut], 0.0).astype(BF16)
                self.at_m[2 * p + hh] = jnp.where(row, at[cut], 0.0).astype(BF16)
        self.wk_t[...] = self.wk[...].astype(F32).T.astype(BF16)
        self.wv_t[...] = self.wv[...].astype(F32).T.astype(BF16)
        self.top[...] = jnp.full(self.top.shape, -1e30, F32)
        self.den[...] = jnp.zeros(self.den.shape, F32)
        self.o_t[...] = jnp.zeros(self.o_t.shape, F32)
        self.dq_t[...] = jnp.zeros(self.dq_t.shape, F32)

    def keys(self, c, pieces):
        k = sum(dot(piece, self.wk[...]) for piece in pieces).astype(BF16)
        for p in range(4):
            self.k_s[c, p] = k[:, p * 128 : p * 128 + 128]
        v = sum(dot(piece, self.wv[...]) for piece in pieces).astype(BF16)
        for p in range(4):
            self.v_s[c, p] = v[:, p * 128 : p * 128 + 128]
        kt = sum(dot_t(self.wk_t[...], piece) for piece in pieces).astype(BF16)
        self.kt_s[c] = kt.reshape(HEADS, HEAD, CHUNK)
        vt = sum(dot_t(self.wv_t[...], piece) for piece in pieces).astype(BF16)
        self.vt_s[...] = vt.reshape(HEADS, HEAD, CHUNK)

    def forward(self, c, live):
        keep = [live[0] != 0, live[1] != 0]

        def score(h):
            return dot(self.k_s[c, h // 2], self.qt_m[h])

        s = score(0)
        for h in range(HEADS):
            following = score(h + 1) if h + 1 < HEADS else None
            s = jnp.concatenate(
                [jnp.where(keep[0], s[:TILE], -1e30), jnp.where(keep[1], s[TILE:], -1e30)], axis=0
            )
            before = self.top[h]
            top = jnp.maximum(before, jnp.max(s, axis=0, keepdims=True))
            e = jnp.exp(s - top)
            scale = jnp.exp(before - top)
            self.top[h] = top
            self.tops[c, h] = top
            self.e_s[c, h] = e
            self.den[h] = self.den[h] * scale + jnp.sum(e, axis=0, keepdims=True)
            self.o_t[h] = self.o_t[h] * scale + dot(self.vt_s[h], e.astype(BF16))
            s = following

    def settle(self):
        for h in range(HEADS):
            inverse = 1.0 / self.den[h]
            o = self.o_t[h] * inverse
            self.o_t[h] = o
            self.den[h] = inverse
            self.delta[h] = jnp.sum(o * self.at_s[h], axis=0, keepdims=True)

    def backward(self, c):
        def pull(p):
            return [dot(self.v_s[c, p], self.at_m[2 * p + hh]) for hh in range(2)]

        dp = pull(0)
        for p in range(4):
            following = pull(p + 1) if p < 3 else None
            ds, pb = [], []
            for hh in range(2):
                h = 2 * p + hh
                prob = self.e_s[c, h] * (jnp.exp(self.tops[c, h] - self.top[h]) * self.den[h])
                pb.append(prob.astype(BF16))
                ds.append((prob * (dp[hh] - self.delta[h])).astype(BF16))
                self.dq_t[h] = self.dq_t[h] + dot(self.kt_s[c, h], ds[hh])
            self.dkv[:, p * 128 : p * 128 + 128] = dot(jnp.concatenate(ds, axis=1), self.q_m[p])
            self.dkv[:, WIDTH + p * 128 : WIDTH + p * 128 + 128] = dot(jnp.concatenate(pb, axis=1), self.a_m[p])
            dp = following

    def to_items(self, piece):
        return dot_t(piece[:, :WIDTH], self.wk[...]) + dot_t(piece[:, WIDTH:], self.wv[...])

    def attended(self):
        return self.o_t[...].reshape(WIDTH, ROWS).T.astype(BF16)

    def d_query(self):
        return (self.dq_t[...] * (HEAD**-0.5)).reshape(WIDTH, ROWS).T.astype(BF16)


def ring_peer(place, way, hops=1):
    return place.z_hi * 8 + place.along_y(hops if way == 0 else -hops)


class Ring:
    semaphores = [
        pltpu.SemaphoreType.DMA((2, 2, 8)),
        pltpu.SemaphoreType.DMA((2, 2, 8)),
        pltpu.SemaphoreType.DMA((4,)),
        pltpu.SemaphoreType.DMA((4,)),
        pltpu.VMEM((2, TILE, WIDTH), BF16),
    ]

    def __init__(self, place, sems):
        self.place = place
        self.send_sem, self.recv_sem, self.zs, self.zr, self.relay_buf = sems

    def column(self, chain):
        return (self.place.z_hi if chain == 0 else 1 - self.place.z_hi) * 8

    def copy(self, chain, way, number):
        source, target = self.ends(chain, way, number)
        return pltpu.make_async_remote_copy(
            src_ref=source, dst_ref=target,
            send_sem=self.send_sem.at[chain, way, number], recv_sem=self.recv_sem.at[chain, way, number],
            device_id=(self.place.user, ring_peer(self.place, way)), device_id_type=MESH,
        )

    def push(self, chain, way, number):
        self.copy(chain, way, number).start()

    def wait(self, chain, way, number):
        self.copy(chain, way, number).wait_recv()

    def leap(self, number):
        tile = number % 2
        z = lax.rem(self.place.z + (2 if tile == 0 else 6), 8)
        near, far = self.cross_ends(tile)
        source, target = (near, self.relay_buf.at[tile]) if number < 2 else (self.relay_buf.at[tile], far)
        return pltpu.make_async_remote_copy(
            src_ref=source, dst_ref=target, send_sem=self.zs.at[number], recv_sem=self.zr.at[number],
            device_id=self.place.peer(1, z), device_id_type=MESH,
        )

    def cross(self, tile):
        self.leap(tile).start()

    def relay(self):
        for tile in range(2):
            self.leap(tile).wait_recv()
            self.leap(2 + tile).start()

    def wait_cross(self, tile):
        self.leap(2 + tile).wait_recv()

    def finish(self):
        for number in range(4):
            self.leap(number).wait_send()
        for chain in range(2):
            for way in range(2):
                for number in range(7):
                    self.copy(chain, way, number).wait_send()


def tile_rows(tile):
    return pl.ds(tile * TILE, TILE)


class Gather(Ring):
    scratch = [
        pltpu.VMEM((2, 2, TILE, WIDTH), BF16),
        pltpu.VMEM((2, 2, TILE // 2, WIDTH), BF16),
        pltpu.VMEM((2, 2, TILE, WIDTH), BF16),
        pltpu.VMEM((2, 2, TILE // 2, WIDTH), BF16),
        pltpu.VMEM((2, 2, TILE // 2, WIDTH), BF16),
    ] + Ring.semaphores

    def __init__(self, place, lists, x_ref, all_ref, scratch):
        self.lists, self.x, self.all = lists, x_ref, all_ref
        self.out3, self.out4, self.in3, self.via3, self.in4 = scratch[:5]
        super().__init__(place, scratch[5:])

    def source(self, chain, way, hops):
        return self.column(chain) + self.place.along_y(-hops if way == 0 else hops)

    def block(self, chain, index, own):
        return self.x if own and chain == 0 else self.all.at[index]

    def cross_ends(self, tile):
        z = lax.rem(self.place.z + (6 if tile == 0 else 2), 8)
        index = lax.div(z, 4) * 8 + self.place.y
        return self.x.at[tile_rows(tile)], self.all.at[index, tile_rows(tile)]

    def ends(self, chain, way, number):
        if number < 2:
            index = self.source(chain, way, 0)
            rows = tile_rows(number)
            return self.block(chain, index, True).at[rows], self.all.at[index, rows]
        if number < 4:
            part = self.all.at[self.source(chain, way, 1), tile_rows(number - 2)]
            return part, part
        source, target = {4: (self.out4, self.via3), 5: (self.out3, self.in3), 6: (self.via3, self.in4)}[number]
        return source.at[chain, way], target.at[chain, way]

    def first(self, chain, tile):
        for way in range(2):
            self.push(chain, way, tile)

    def second(self, chain):
        for tile in range(2):
            for way in range(2):
                self.wait(chain, way, tile)
                self.push(chain, way, 2 + tile)

    def third(self, chain):
        for way in range(2):
            index = self.source(chain, way, 2)
            for tile in range(2):
                self.wait(chain, way, 2 + tile)
            far = self.lists[ring_peer(self.place, way, 2), index] == 1
            low = way * (TILE // 2)
            self.out4[chain, way] = jnp.where(
                far,
                self.all[index, TILE + low : TILE + low + TILE // 2],
                self.all[index, low : low + TILE // 2],
            )
            self.push(chain, way, 4)
            near = self.lists[ring_peer(self.place, way, 1), index] == 1
            self.out3[chain, way] = jnp.where(near, self.all[index, TILE:], self.all[index, :TILE])
            self.push(chain, way, 5)

    def fourth(self, chain):
        for way in range(2):
            self.wait(chain, way, 4)
            self.push(chain, way, 6)

    def tiles(self, chain, e):
        found, live = [], []
        for way in ((1, 0) if e else (None, 4)):
            hops = 4 if way == 4 else e
            index = self.source(chain, 0 if way in (None, 4) else way, hops)
            tile = self.lists[self.place.item, index]
            live.append((tile < 2).astype(jnp.int32))
            if way == 4:
                for way in range(2):
                    self.wait(chain, way, 6)
                    found.append(self.in4[chain, way])
            elif e == 3:
                self.wait(chain, way, 5)
                found.append(self.in3[chain, way])
            else:
                block = self.block(chain, index, e == 0)
                found.append(jnp.where(tile == 1, block[TILE:], block[:TILE]))
        return jnp.concatenate(found, axis=0), live


class Scatter(Ring):
    scratch = [
        pltpu.VMEM((2, 2, TILE // 2, WIDTH), BF16),
        pltpu.VMEM((2, 2, TILE // 2, WIDTH), BF16),
        pltpu.VMEM((2, 2, TILE // 2, WIDTH), BF16),
        pltpu.VMEM((2, 2, TILE, WIDTH), BF16),
        pltpu.VMEM((2, 2, TILE, WIDTH), BF16),
        pltpu.VMEM((2, 2, 2, TILE, WIDTH), BF16),
        pltpu.VMEM((2, 2, 2, TILE, WIDTH), BF16),
        pltpu.VMEM((2, 2, 2, TILE, WIDTH), BF16),
        pltpu.VMEM((2, 2, 2, TILE, WIDTH), BF16),
        pltpu.VMEM((2, TILE, WIDTH), BF16),
        pltpu.VMEM((2, TILE, WIDTH), BF16),
        pltpu.VMEM((CHUNKS, CHUNK, WIDTH), F32),
    ] + Ring.semaphores

    def __init__(self, place, lists, scratch):
        self.lists = lists
        (self.out4, self.via3, self.in4, self.out3, self.in3, self.out2, self.in2, self.out1, self.in1,
         self.z_out, self.z_in, self.grads) = scratch[:12]
        super().__init__(place, scratch[12:])

    def owner(self, chain, way, hops):
        return self.column(chain) + self.place.along_y(hops if way == 0 else -hops)

    def cross_ends(self, tile):
        return self.z_out.at[tile], self.z_in.at[tile]

    def ends(self, chain, way, number):
        if number < 3:
            source, target = ((self.out4, self.via3), (self.via3, self.in4), (self.out3, self.in3))[number]
            return source.at[chain, way], target.at[chain, way]
        source, target = (self.out2, self.in2) if number < 5 else (self.out1, self.in1)
        tile = (number - 3) % 2
        return source.at[chain, way, tile], target.at[chain, way, tile]

    def own(self, chain, way, e):
        return self.grads[ORDER.index((chain, e)), tile_rows(0 if way == 0 else 1)]

    def lists_here(self, index, tile):
        return self.lists[self.place.item, index] == tile

    def send4(self, chain):
        for way in range(2):
            low = TILE + way * (TILE // 2)
            self.out4[chain, way] = self.grads[ORDER.index((chain, 0)), low : low + TILE // 2].astype(BF16)
            self.push(chain, way, 0)

    def send3(self, chain):
        for way in range(2):
            self.out3[chain, way] = self.own(chain, way, 3).astype(BF16)
            self.wait(chain, way, 0)
            self.push(chain, way, 1)
            self.push(chain, way, 2)

    def send2(self, chain):
        for way in range(2):
            index = self.owner(chain, way, 2)
            one, two = ring_peer(self.place, way, -1), ring_peer(self.place, way, -2)
            self.wait(chain, way, 1)
            self.wait(chain, way, 2)
            half = slice(way * (TILE // 2), way * (TILE // 2) + TILE // 2)
            other = slice((1 - way) * (TILE // 2), (1 - way) * (TILE // 2) + TILE // 2)
            for tile in range(2):
                value = jnp.where(self.lists_here(index, tile), self.own(chain, way, 2), 0.0)
                value = value + jnp.where(
                    self.lists[one, index] == tile, self.in3[chain, way].astype(F32), 0.0
                )
                far = jnp.where(self.lists[two, index] == tile, self.in4[chain, way].astype(F32), 0.0)
                self.out2[chain, way, tile, half] = (value[half] + far).astype(BF16)
                self.out2[chain, way, tile, other] = value[other].astype(BF16)
                self.push(chain, way, 3 + tile)

    def send1(self, chain):
        for tile in range(2):
            for way in range(2):
                index = self.owner(chain, way, 1)
                self.wait(chain, way, 3 + tile)
                value = jnp.where(self.lists_here(index, tile), self.own(chain, way, 1), 0.0)
                value = value + self.in2[chain, way, tile].astype(F32)
                self.out1[chain, way, tile] = value.astype(BF16)
                self.push(chain, way, 5 + tile)

    def total(self, chain, tile):
        for way in range(2):
            self.wait(chain, way, 5 + tile)
        value = jnp.where(self.lists_here(self.owner(chain, 0, 0), tile), self.own(chain, 0, 0), 0.0)
        return value + self.in1[chain, 0, tile].astype(F32) + self.in1[chain, 1, tile].astype(F32)

    def send_across(self):
        for tile in range(2):
            self.z_out[tile] = self.total(1, tile).astype(BF16)
            self.cross(tile)


def take(scratch, count):
    taken = scratch[:count]
    del scratch[:count]
    return taken


def kernel(
    lists_ref, user_ref, x_ref, proj_ref, wq_ref, wk_ref, wv_ref, wo_ref, cot_ref,
    att_ref, dq_ref, out_ref, all_x, part, lin_sum, lin_total, own_part, listed, live, *scratch
):
    scratch = list(scratch)
    place = Place()
    gather = Gather(place, lists_ref, x_ref, all_x, take(scratch, len(Gather.scratch)))
    scatter = Scatter(place, lists_ref, take(scratch, len(Scatter.scratch)))
    lin = Total(place, part, lin_sum, take(scratch, len(Total.scratch)))
    d_lin = Total(place, own_part, lin_total, take(scratch, len(Total.scratch)))
    attention = Attention((wq_ref, wk_ref, wv_ref, wo_ref), scratch)

    greet(place)
    for tile in range(2):
        gather.first(0, tile)
        gather.cross(tile)
    total = lax.dot_general(
        proj_ref[...], x_ref[...], (((0,), (0,)), ((), ())), preferred_element_type=F32
    )
    for k in range(8):
        part[k] = total[k * 32 : k * 32 + 32]
    lin.step(0)
    attention.prepare(user_ref, cot_ref)

    def before(i):
        if i == 0:
            gather.second(0)
            gather.relay()
        elif i == 1:
            lin.step(1)
            gather.third(0)
            for tile in range(2):
                gather.wait_cross(tile)
                gather.first(1, tile)
        elif i == 2:
            gather.fourth(0)
            lin.step(2)
        elif i == 3:
            lin.step(3)
            gather.second(1)
        elif i == 4:
            lin.step(4)
        elif i == 5:
            gather.third(1)
        elif i == 6:
            gather.fourth(1)
            lin.arrive(4)

    def forward_step(step, carry):
        for i, chunk in enumerate(ORDER):

            @pl.when(step == i)
            def _():
                before(i)
                if chunk is None:
                    live[0], live[1] = jnp.int32(1), jnp.int32(1)
                    attention.keys(i, split(lin_sum[...].reshape(RANK, WIDTH)))
                else:
                    rows, alive = gather.tiles(*chunk)
                    listed[...] = rows
                    live[0], live[1] = alive

        @pl.when(step != LINFORMER)
        def _():
            attention.keys(step, (listed[...],))

        attention.forward(step, live)
        return carry

    lax.fori_loop(0, CHUNKS, forward_step, 0)
    attention.settle()
    att_ref[...] = attention.attended()

    def after(i):
        if i == 8:
            scatter.send4(1)
        elif i == 7:
            scatter.send3(1)
        elif i == 6:
            d_lin.step(0)
        elif i == 5:
            scatter.send2(1)
        elif i == 4:
            scatter.send4(0)
            d_lin.step(1)
        elif i == 3:
            scatter.send1(1)
        elif i == 2:
            scatter.send3(0)
            d_lin.step(2)
        elif i == 1:
            scatter.send2(0)
            d_lin.step(3)

    def backward_step(step, carry):
        c = CHUNKS - 1 - step
        attention.backward(c)
        scatter.grads[c] = attention.to_items(attention.dkv[...].astype(BF16))
        for i in range(CHUNKS - 1, 0, -1):

            @pl.when(c == i)
            def _():
                if i == LINFORMER:
                    g = scatter.grads[i] + attention.to_items(split(attention.dkv[...])[1])
                    for k in range(8):
                        own_part[k] = g[k * 32 : k * 32 + 32]
                after(i)

        return carry

    lax.fori_loop(0, CHUNKS, backward_step, 0)
    scatter.send_across()
    d_lin.step(4)
    scatter.send1(0)
    dq_ref[...] = attention.d_query()
    scatter.relay()
    d_lin.arrive(4)
    back = jnp.zeros((ROWS, WIDTH), F32)
    for piece in split(lin_total[...].reshape(RANK, WIDTH)):
        back = back + dot(proj_ref[...], piece)
    for tile in range(2):
        value = back[tile * TILE : tile * TILE + TILE] + scatter.total(0, tile)
        scatter.wait_cross(tile)
        out_ref[tile * TILE : tile * TILE + TILE] = value + scatter.z_in[tile].astype(F32)
    lin.finish()
    d_lin.finish()
    gather.finish()
    scatter.finish()


def finish_kernel(att_ref, dq_ref, grad_ref, wq_ref, wo_ref, upd_ref, ug_ref, out_ref):
    upd_ref[...] = dot(att_ref[...], wo_ref[...]).astype(BF16)
    ug_ref[...] = dot_t(dq_ref[...], wq_ref[...]).astype(BF16)
    out_ref[...] = grad_ref[...].astype(BF16)


def in_vmem(count):
    return [pl.BlockSpec(memory_space=pltpu.VMEM)] * count


def per_device(user_x, item_x, lin_proj, tile_lists, w_q, w_k, w_v, w_o, cotangent):
    shape = jax.ShapeDtypeStruct
    sums = pltpu.VMEM((8, 32, WIDTH), F32)
    attended, d_query, grad = pl.pallas_call(
        kernel,
        out_shape=[shape((ROWS, WIDTH), BF16)] * 2 + [shape((ROWS, WIDTH), F32)],
        in_specs=[pl.BlockSpec(memory_space=pltpu.SMEM)] + in_vmem(8),
        out_specs=in_vmem(3),
        scratch_shapes=[
            pltpu.VMEM((OWNERS, ROWS, WIDTH), BF16),
            sums, sums, sums, sums,
            pltpu.VMEM((CHUNK, WIDTH), BF16),
            pltpu.SMEM((2,), jnp.int32),
        ] + Gather.scratch + Scatter.scratch + Total.scratch + Total.scratch + Attention.scratch,
        compiler_params=pltpu.CompilerParams(
            collective_id=0, has_side_effects=True, vmem_limit_bytes=VMEM_BYTES
        ),
        name="attend_and_exchange",
    )(tile_lists, user_x, item_x, lin_proj, w_q, w_k, w_v, w_o, cotangent)
    return pl.pallas_call(
        finish_kernel,
        out_shape=[shape((ROWS, WIDTH), BF16)] * 3,
        in_specs=in_vmem(5),
        out_specs=in_vmem(3),
        compiler_params=pltpu.CompilerParams(vmem_limit_bytes=VMEM_BYTES),
        name="finish",
    )(attended, d_query, grad, w_q, w_o)


def solution(mesh):
    rows = P(("user", "item"), None)
    return jax.shard_map(
        per_device,
        mesh=mesh,
        in_specs=(rows, rows, rows, P("user", None), P(), P(), P(), P(), rows),
        out_specs=(rows, rows, rows),
        check_vma=False,
    )
```

```python
import functools

import jax
import jax.numpy as jnp
from jax import lax
from jax.experimental import pallas as pl
from jax.experimental.pallas import tpu as pltpu
from jax.sharding import PartitionSpec as P

F32, BF16 = jnp.float32, jnp.bfloat16
HEADS, HEAD, WIDTH, TILE, RANK = 8, 64, 512, 128, 256
ROWS = 256
OWNERS = 16
KEYS = OWNERS * TILE + RANK
CHUNK = 256
CHUNKS = KEYS // CHUNK
VMEM_BYTES = 60 * 1024 * 1024
MESH = pl.DeviceIdType.MESH
ORDER = ((0, 1), (0, 2), (1, 1), (0, 3), None, (1, 2), (0, 0), (1, 3), (1, 0))
LINFORMER = 4


def dot(a, b):
    return lax.dot_general(a, b, (((1,), (0,)), ((), ())), preferred_element_type=F32)


def dot_t(a, b):
    return lax.dot_general(a, b, (((1,), (1,)), ((), ())), preferred_element_type=F32)


def split(a):
    high = a.astype(BF16)
    return high, (a - high.astype(F32)).astype(BF16)


class Place:
    def __init__(self):
        self.user, self.item = lax.axis_index("user"), lax.axis_index("item")
        self.near = lax.rem(self.user, 8)
        self.z_lo = lax.div(self.user, 8)
        self.y = lax.rem(self.item, 8)
        self.z_hi = lax.div(self.item, 8)
        self.z = self.z_hi * 4 + self.z_lo
        self.member = (self.near, self.z, self.y)

    def peer(self, group, k):
        if group == 0:
            return (self.z_lo * 8 + k, self.item)
        if group == 1:
            return (lax.rem(k, 4) * 8 + self.near, lax.div(k, 4) * 8 + self.y)
        return (self.user, self.z_hi * 8 + k)

    def along_y(self, step):
        return lax.rem(self.y + step + 8, 8)

    def partner(self):
        return (self.user, lax.rem(self.item + 8, 16))


def greet(place):
    barrier = pltpu.get_barrier_semaphore()
    for group in range(3):
        for r in range(1, 8):
            k = lax.rem(place.member[group] + r, 8)
            pl.semaphore_signal(barrier, inc=1, device_id=place.peer(group, k), device_id_type=MESH)
    pl.semaphore_wait(barrier, 21)


class Total:
    scratch = [
        pltpu.VMEM((8, 32, WIDTH), BF16),
        pltpu.VMEM((8, 8, 256), F32),
        pltpu.VMEM((8, 8, 256), F32),
        pltpu.VMEM((8, 256), F32),
        pltpu.VMEM((8, 8, 256), F32),
        pltpu.VMEM((8, 256), F32),
        pltpu.VMEM((8, 8, 256), F32),
        pltpu.VMEM((32, WIDTH), BF16),
        pltpu.SemaphoreType.DMA((5, 8)),
        pltpu.SemaphoreType.DMA((5, 8)),
    ]

    def __init__(self, place, part, out, scratch):
        self.place, self.part, self.out = place, part, out
        (self.land1, self.s1, self.land2, self.s2, self.land3, self.s3, self.land4, self.s4) = scratch[:8]
        self.send_sem, self.recv_sem = scratch[8:]

    def copies(self, phase):
        group = (0, 1, 2, 1, 0)[phase]
        land = (self.land1, self.land2, self.land3, self.land4, self.out)[phase]
        me = self.place.member[group]
        for r in range(1, 8):
            k = lax.rem(me + r, 8)
            source = (self.part.at[k], self.s1.at[k], self.s2, self.s3, self.s4)[phase]
            yield pltpu.make_async_remote_copy(
                src_ref=source,
                dst_ref=land.at[me],
                send_sem=self.send_sem.at[phase, r],
                recv_sem=self.recv_sem.at[phase, r],
                device_id=self.place.peer(group, k),
                device_id_type=MESH,
            )

    def start(self, phase):
        for copy in self.copies(phase):
            copy.start()

    def arrive(self, phase):
        for copy in self.copies(phase):
            copy.wait_recv()

    def step(self, phase):
        near, z, y = self.place.member
        if phase == 0:
            self.start(0)
            self.land1[near] = self.part[near]
            return
        self.arrive(phase - 1)
        if phase == 1:
            total = self.land1[0].astype(F32)
            for k in range(1, 8):
                total = total + self.land1[k].astype(F32)
            for p in range(8):
                self.s1[p] = total[p // 2 * 8 : p // 2 * 8 + 8, p % 2 * 256 : p % 2 * 256 + 256]
            self.start(1)
            self.land2[z] = self.s1[z]
        elif phase == 2:
            total = self.land2[0]
            for k in range(1, 8):
                total = total + self.land2[k]
            self.s2[...] = total
            self.start(2)
            self.land3[y] = total
        elif phase == 3:
            total = self.land3[0]
            for k in range(1, 8):
                total = total + self.land3[k]
            self.s3[...] = total
            self.start(3)
            self.land4[z] = total
        elif phase == 4:
            bands = [jnp.concatenate([self.land4[2 * p], self.land4[2 * p + 1]], axis=1) for p in range(4)]
            self.s4[...] = jnp.concatenate(bands, axis=0).astype(BF16)
            self.start(4)
            self.out[near] = self.s4[...]

    def finish(self):
        for phase in range(5):
            for copy in self.copies(phase):
                copy.wait_send()


class Attention:
    scratch = [
        pltpu.VMEM((CHUNKS, 4, CHUNK, 128), BF16),
        pltpu.VMEM((CHUNKS, 4, CHUNK, 128), BF16),
        pltpu.VMEM((CHUNKS, HEADS, HEAD, CHUNK), BF16),
        pltpu.VMEM((HEADS, HEAD, CHUNK), BF16),
        pltpu.VMEM((HEADS, 128, ROWS), BF16),
        pltpu.VMEM((HEADS, 128, ROWS), BF16),
        pltpu.VMEM((4, 2 * ROWS, 128), BF16),
        pltpu.VMEM((4, 2 * ROWS, 128), BF16),
        pltpu.VMEM((HEADS, HEAD, ROWS), F32),
        pltpu.VMEM((CHUNKS, HEADS, CHUNK, ROWS), F32),
        pltpu.VMEM((CHUNK, 2 * WIDTH), F32),
        pltpu.VMEM((HEADS, HEAD, ROWS), F32),
        pltpu.VMEM((HEADS, HEAD, ROWS), F32),
        pltpu.VMEM((HEADS, 1, ROWS), F32),
        pltpu.VMEM((HEADS, 1, ROWS), F32),
        pltpu.VMEM((HEADS, 1, ROWS), F32),
        pltpu.VMEM((CHUNKS, HEADS, 1, ROWS), F32),
        pltpu.VMEM((WIDTH, WIDTH), BF16),
        pltpu.VMEM((WIDTH, WIDTH), BF16),
    ]

    def __init__(self, weights, scratch):
        self.wq, self.wk, self.wv, self.wo = weights
        (self.k_s, self.v_s, self.kt_s, self.vt_s, self.qt_m, self.at_m, self.q_m, self.a_m, self.at_s,
         self.e_s, self.dkv, self.o_t, self.dq_t, self.top, self.den, self.delta, self.tops,
         self.wk_t, self.wv_t) = scratch

    def prepare(self, user_ref, cot_ref):
        q = dot(user_ref[...], self.wq[...]).astype(BF16).astype(F32) * (HEAD**-0.5)
        a = dot_t(cot_ref[...], self.wo[...]).astype(BF16).astype(F32)
        qt, at = q.T, a.T
        self.at_s[...] = at.reshape(HEADS, HEAD, ROWS)
        low_lane = lax.broadcasted_iota(jnp.int32, (ROWS, 128), 1) < HEAD
        low_row = lax.broadcasted_iota(jnp.int32, (128, ROWS), 0) < HEAD
        for p in range(4):
            cut = slice(p * 128, p * 128 + 128)
            for hh in range(2):
                lane, row = (low_lane, low_row) if hh == 0 else (~low_lane, ~low_row)
                half = slice(hh * ROWS, hh * ROWS + ROWS)
                self.q_m[p, half] = jnp.where(lane, q[:, cut], 0.0).astype(BF16)
                self.a_m[p, half] = jnp.where(lane, a[:, cut], 0.0).astype(BF16)
                self.qt_m[2 * p + hh] = jnp.where(row, qt[cut], 0.0).astype(BF16)
                self.at_m[2 * p + hh] = jnp.where(row, at[cut], 0.0).astype(BF16)
        self.wk_t[...] = self.wk[...].astype(F32).T.astype(BF16)
        self.wv_t[...] = self.wv[...].astype(F32).T.astype(BF16)
        self.top[...] = jnp.full(self.top.shape, -1e30, F32)
        self.den[...] = jnp.zeros(self.den.shape, F32)
        self.o_t[...] = jnp.zeros(self.o_t.shape, F32)
        self.dq_t[...] = jnp.zeros(self.dq_t.shape, F32)

    def keys(self, c, pieces):
        k = sum(dot(piece, self.wk[...]) for piece in pieces).astype(BF16)
        for p in range(4):
            self.k_s[c, p] = k[:, p * 128 : p * 128 + 128]
        v = sum(dot(piece, self.wv[...]) for piece in pieces).astype(BF16)
        for p in range(4):
            self.v_s[c, p] = v[:, p * 128 : p * 128 + 128]
        kt = sum(dot_t(self.wk_t[...], piece) for piece in pieces).astype(BF16)
        self.kt_s[c] = kt.reshape(HEADS, HEAD, CHUNK)
        vt = sum(dot_t(self.wv_t[...], piece) for piece in pieces).astype(BF16)
        self.vt_s[...] = vt.reshape(HEADS, HEAD, CHUNK)

    def forward(self, c, live):
        keep = [live[0] != 0, live[1] != 0]

        def score(h):
            return dot(self.k_s[c, h // 2], self.qt_m[h])

        s = score(0)
        for h in range(HEADS):
            following = score(h + 1) if h + 1 < HEADS else None
            s = jnp.concatenate(
                [jnp.where(keep[0], s[:TILE], -1e30), jnp.where(keep[1], s[TILE:], -1e30)], axis=0
            )
            before = self.top[h]
            top = jnp.maximum(before, jnp.max(s, axis=0, keepdims=True))
            e = jnp.exp(s - top)
            scale = jnp.exp(before - top)
            self.top[h] = top
            self.tops[c, h] = top
            self.e_s[c, h] = e
            self.den[h] = self.den[h] * scale + jnp.sum(e, axis=0, keepdims=True)
            self.o_t[h] = self.o_t[h] * scale + dot(self.vt_s[h], e.astype(BF16))
            s = following

    def settle(self):
        for h in range(HEADS):
            inverse = 1.0 / self.den[h]
            o = self.o_t[h] * inverse
            self.o_t[h] = o
            self.den[h] = inverse
            self.delta[h] = jnp.sum(o * self.at_s[h], axis=0, keepdims=True)

    def backward(self, c):
        def pull(p):
            return [dot(self.v_s[c, p], self.at_m[2 * p + hh]) for hh in range(2)]

        dp = pull(0)
        for p in range(4):
            following = pull(p + 1) if p < 3 else None
            ds, pb = [], []
            for hh in range(2):
                h = 2 * p + hh
                prob = self.e_s[c, h] * (jnp.exp(self.tops[c, h] - self.top[h]) * self.den[h])
                pb.append(prob.astype(BF16))
                ds.append((prob * (dp[hh] - self.delta[h])).astype(BF16))
                self.dq_t[h] = self.dq_t[h] + dot(self.kt_s[c, h], ds[hh])
            self.dkv[:, p * 128 : p * 128 + 128] = dot(jnp.concatenate(ds, axis=1), self.q_m[p])
            self.dkv[:, WIDTH + p * 128 : WIDTH + p * 128 + 128] = dot(jnp.concatenate(pb, axis=1), self.a_m[p])
            dp = following

    def to_items(self, piece):
        return dot_t(piece[:, :WIDTH], self.wk[...]) + dot_t(piece[:, WIDTH:], self.wv[...])

    def updated(self):
        attended = self.o_t[...].reshape(WIDTH, ROWS).T.astype(BF16)
        return dot(attended, self.wo[...]).astype(BF16)

    def user_grad(self):
        d_query = (self.dq_t[...] * (HEAD**-0.5)).reshape(WIDTH, ROWS).T.astype(BF16)
        return dot_t(d_query, self.wq[...]).astype(BF16)


def ring_peer(place, way, hops=1):
    return place.z_hi * 8 + place.along_y(hops if way == 0 else -hops)


class Ring:
    semaphores = [
        pltpu.SemaphoreType.DMA((2, 2, 8)),
        pltpu.SemaphoreType.DMA((2, 2, 8)),
        pltpu.SemaphoreType.DMA((4,)),
        pltpu.SemaphoreType.DMA((4,)),
        pltpu.VMEM((2, TILE, WIDTH), BF16),
    ]

    def __init__(self, place, sems):
        self.place = place
        self.send_sem, self.recv_sem, self.zs, self.zr, self.relay_buf = sems

    def column(self, chain):
        return (self.place.z_hi if chain == 0 else 1 - self.place.z_hi) * 8

    def copy(self, chain, way, number):
        source, target = self.ends(chain, way, number)
        return pltpu.make_async_remote_copy(
            src_ref=source, dst_ref=target,
            send_sem=self.send_sem.at[chain, way, number], recv_sem=self.recv_sem.at[chain, way, number],
            device_id=(self.place.user, ring_peer(self.place, way)), device_id_type=MESH,
        )

    def push(self, chain, way, number):
        self.copy(chain, way, number).start()

    def wait(self, chain, way, number):
        self.copy(chain, way, number).wait_recv()

    def leap(self, number):
        tile = number % 2
        z = lax.rem(self.place.z + (2 if tile == 0 else 6), 8)
        near, far = self.cross_ends(tile)
        source, target = (near, self.relay_buf.at[tile]) if number < 2 else (self.relay_buf.at[tile], far)
        return pltpu.make_async_remote_copy(
            src_ref=source, dst_ref=target, send_sem=self.zs.at[number], recv_sem=self.zr.at[number],
            device_id=self.place.peer(1, z), device_id_type=MESH,
        )

    def cross(self, tile):
        self.leap(tile).start()

    def relay(self):
        for tile in range(2):
            self.leap(tile).wait_recv()
            self.leap(2 + tile).start()

    def wait_cross(self, tile):
        self.leap(2 + tile).wait_recv()

    def finish(self):
        for number in range(4):
            self.leap(number).wait_send()
        for chain in range(2):
            for way in range(2):
                for number in range(7):
                    self.copy(chain, way, number).wait_send()


def tile_rows(tile):
    return pl.ds(tile * TILE, TILE)


class Gather(Ring):
    scratch = [
        pltpu.VMEM((2, 2, TILE, WIDTH), BF16),
        pltpu.VMEM((2, 2, TILE // 2, WIDTH), BF16),
        pltpu.VMEM((2, 2, TILE, WIDTH), BF16),
        pltpu.VMEM((2, 2, TILE // 2, WIDTH), BF16),
        pltpu.VMEM((2, 2, TILE // 2, WIDTH), BF16),
    ] + Ring.semaphores

    def __init__(self, place, lists, x_ref, all_ref, scratch):
        self.lists, self.x, self.all = lists, x_ref, all_ref
        self.out3, self.out4, self.in3, self.via3, self.in4 = scratch[:5]
        super().__init__(place, scratch[5:])

    def source(self, chain, way, hops):
        return self.column(chain) + self.place.along_y(-hops if way == 0 else hops)

    def block(self, chain, index, own):
        return self.x if own and chain == 0 else self.all.at[index]

    def cross_ends(self, tile):
        z = lax.rem(self.place.z + (6 if tile == 0 else 2), 8)
        index = lax.div(z, 4) * 8 + self.place.y
        return self.x.at[tile_rows(tile)], self.all.at[index, tile_rows(tile)]

    def ends(self, chain, way, number):
        if number < 2:
            index = self.source(chain, way, 0)
            rows = tile_rows(number)
            return self.block(chain, index, True).at[rows], self.all.at[index, rows]
        if number < 4:
            part = self.all.at[self.source(chain, way, 1), tile_rows(number - 2)]
            return part, part
        source, target = {4: (self.out4, self.via3), 5: (self.out3, self.in3), 6: (self.via3, self.in4)}[number]
        return source.at[chain, way], target.at[chain, way]

    def first(self, chain, tile):
        for way in range(2):
            self.push(chain, way, tile)

    def second(self, chain):
        for tile in range(2):
            for way in range(2):
                self.wait(chain, way, tile)
                self.push(chain, way, 2 + tile)

    def third(self, chain):
        for way in range(2):
            index = self.source(chain, way, 2)
            for tile in range(2):
                self.wait(chain, way, 2 + tile)
            far = self.lists[ring_peer(self.place, way, 2), index] == 1
            low = way * (TILE // 2)
            self.out4[chain, way] = jnp.where(
                far,
                self.all[index, TILE + low : TILE + low + TILE // 2],
                self.all[index, low : low + TILE // 2],
            )
            self.push(chain, way, 4)
            near = self.lists[ring_peer(self.place, way, 1), index] == 1
            self.out3[chain, way] = jnp.where(near, self.all[index, TILE:], self.all[index, :TILE])
            self.push(chain, way, 5)

    def fourth(self, chain):
        for way in range(2):
            self.wait(chain, way, 4)
            self.push(chain, way, 6)

    def tiles(self, chain, e):
        found, live = [], []
        for way in ((1, 0) if e else (None, 4)):
            hops = 4 if way == 4 else e
            index = self.source(chain, 0 if way in (None, 4) else way, hops)
            tile = self.lists[self.place.item, index]
            live.append((tile < 2).astype(jnp.int32))
            if way == 4:
                for way in range(2):
                    self.wait(chain, way, 6)
                    found.append(self.in4[chain, way])
            elif e == 3:
                self.wait(chain, way, 5)
                found.append(self.in3[chain, way])
            else:
                block = self.block(chain, index, e == 0)
                found.append(jnp.where(tile == 1, block[TILE:], block[:TILE]))
        return jnp.concatenate(found, axis=0), live


class Scatter(Ring):
    scratch = [
        pltpu.VMEM((2, 2, TILE // 2, WIDTH), BF16),
        pltpu.VMEM((2, 2, TILE // 2, WIDTH), BF16),
        pltpu.VMEM((2, 2, TILE // 2, WIDTH), BF16),
        pltpu.VMEM((2, 2, TILE, WIDTH), BF16),
        pltpu.VMEM((2, 2, TILE, WIDTH), BF16),
        pltpu.VMEM((2, 2, 2, TILE, WIDTH), BF16),
        pltpu.VMEM((2, 2, 2, TILE, WIDTH), BF16),
        pltpu.VMEM((2, 2, 2, TILE, WIDTH), BF16),
        pltpu.VMEM((2, 2, 2, TILE, WIDTH), BF16),
        pltpu.VMEM((2, TILE, WIDTH), BF16),
        pltpu.VMEM((2, TILE, WIDTH), BF16),
        pltpu.VMEM((CHUNKS, CHUNK, WIDTH), F32),
    ] + Ring.semaphores

    def __init__(self, place, lists, scratch):
        self.lists = lists
        (self.out4, self.via3, self.in4, self.out3, self.in3, self.out2, self.in2, self.out1, self.in1,
         self.z_out, self.z_in, self.grads) = scratch[:12]
        super().__init__(place, scratch[12:])

    def owner(self, chain, way, hops):
        return self.column(chain) + self.place.along_y(hops if way == 0 else -hops)

    def cross_ends(self, tile):
        return self.z_out.at[tile], self.z_in.at[tile]

    def ends(self, chain, way, number):
        if number < 3:
            source, target = ((self.out4, self.via3), (self.via3, self.in4), (self.out3, self.in3))[number]
            return source.at[chain, way], target.at[chain, way]
        source, target = (self.out2, self.in2) if number < 5 else (self.out1, self.in1)
        tile = (number - 3) % 2
        return source.at[chain, way, tile], target.at[chain, way, tile]

    def own(self, chain, way, e):
        return self.grads[ORDER.index((chain, e)), tile_rows(0 if way == 0 else 1)]

    def lists_here(self, index, tile):
        return self.lists[self.place.item, index] == tile

    def send4(self, chain):
        for way in range(2):
            low = TILE + way * (TILE // 2)
            self.out4[chain, way] = self.grads[ORDER.index((chain, 0)), low : low + TILE // 2].astype(BF16)
            self.push(chain, way, 0)

    def send3(self, chain):
        for way in range(2):
            self.out3[chain, way] = self.own(chain, way, 3).astype(BF16)
            self.wait(chain, way, 0)
            self.push(chain, way, 1)
            self.push(chain, way, 2)

    def send2(self, chain):
        for way in range(2):
            index = self.owner(chain, way, 2)
            one, two = ring_peer(self.place, way, -1), ring_peer(self.place, way, -2)
            self.wait(chain, way, 1)
            self.wait(chain, way, 2)
            half = slice(way * (TILE // 2), way * (TILE // 2) + TILE // 2)
            other = slice((1 - way) * (TILE // 2), (1 - way) * (TILE // 2) + TILE // 2)
            for tile in range(2):
                value = jnp.where(self.lists_here(index, tile), self.own(chain, way, 2), 0.0)
                value = value + jnp.where(
                    self.lists[one, index] == tile, self.in3[chain, way].astype(F32), 0.0
                )
                far = jnp.where(self.lists[two, index] == tile, self.in4[chain, way].astype(F32), 0.0)
                self.out2[chain, way, tile, half] = (value[half] + far).astype(BF16)
                self.out2[chain, way, tile, other] = value[other].astype(BF16)
                self.push(chain, way, 3 + tile)

    def send1(self, chain):
        for tile in range(2):
            for way in range(2):
                index = self.owner(chain, way, 1)
                self.wait(chain, way, 3 + tile)
                value = jnp.where(self.lists_here(index, tile), self.own(chain, way, 1), 0.0)
                value = value + self.in2[chain, way, tile].astype(F32)
                self.out1[chain, way, tile] = value.astype(BF16)
                self.push(chain, way, 5 + tile)

    def total(self, chain, tile):
        for way in range(2):
            self.wait(chain, way, 5 + tile)
        value = jnp.where(self.lists_here(self.owner(chain, 0, 0), tile), self.own(chain, 0, 0), 0.0)
        return value + self.in1[chain, 0, tile].astype(F32) + self.in1[chain, 1, tile].astype(F32)

    def send_across(self):
        for tile in range(2):
            self.z_out[tile] = self.total(1, tile).astype(BF16)
            self.cross(tile)


def take(scratch, count):
    taken = scratch[:count]
    del scratch[:count]
    return taken


def kernel(
    lists_ref, user_ref, x_ref, proj_ref, wq_ref, wk_ref, wv_ref, wo_ref, cot_ref,
    upd_ref, ug_ref, out_ref, all_x, part, lin_sum, lin_total, own_part, listed, live, *scratch
):
    scratch = list(scratch)
    place = Place()
    gather = Gather(place, lists_ref, x_ref, all_x, take(scratch, len(Gather.scratch)))
    scatter = Scatter(place, lists_ref, take(scratch, len(Scatter.scratch)))
    lin = Total(place, part, lin_sum, take(scratch, len(Total.scratch)))
    d_lin = Total(place, own_part, lin_total, take(scratch, len(Total.scratch)))
    attention = Attention((wq_ref, wk_ref, wv_ref, wo_ref), scratch)

    greet(place)
    for tile in range(2):
        gather.first(0, tile)
        gather.cross(tile)
    total = lax.dot_general(
        proj_ref[...], x_ref[...], (((0,), (0,)), ((), ())), preferred_element_type=F32
    )
    for k in range(8):
        part[k] = total[k * 32 : k * 32 + 32].astype(BF16)
    lin.step(0)
    attention.prepare(user_ref, cot_ref)

    def before(i):
        if i == 0:
            gather.second(0)
            gather.relay()
        elif i == 1:
            lin.step(1)
            gather.third(0)
            for tile in range(2):
                gather.wait_cross(tile)
                gather.first(1, tile)
        elif i == 2:
            gather.fourth(0)
            lin.step(2)
            lin.step(3)
            gather.second(1)
        elif i == 3:
            lin.step(4)
        elif i == 4:
            lin.arrive(4)
        elif i == 5:
            gather.third(1)
        elif i == 6:
            gather.fourth(1)

    def forward_step(step, carry):
        for i, chunk in enumerate(ORDER):

            @pl.when(step == i)
            def _():
                before(i)
                if chunk is None:
                    live[0], live[1] = jnp.int32(1), jnp.int32(1)
                    attention.keys(i, (lin_sum[...].reshape(RANK, WIDTH),))
                else:
                    rows, alive = gather.tiles(*chunk)
                    listed[...] = rows
                    live[0], live[1] = alive

        @pl.when(step != LINFORMER)
        def _():
            attention.keys(step, (listed[...],))

        attention.forward(step, live)
        return carry

    lax.fori_loop(0, CHUNKS, forward_step, 0)
    attention.settle()

    def after(i):
        if i == 8:
            scatter.send4(1)
        elif i == 7:
            scatter.send3(1)
        elif i == 6:
            scatter.send4(0)
        elif i == 5:
            scatter.send2(1)
        elif i == 4:
            d_lin.step(0)
        elif i == 3:
            scatter.send3(0)
        elif i == 2:
            scatter.send1(1)
            d_lin.step(1)
        elif i == 1:
            scatter.send2(0)
            d_lin.step(2)

    def backward_step(step, carry):
        c = CHUNKS - 1 - step
        attention.backward(c)
        scatter.grads[c] = attention.to_items(attention.dkv[...].astype(BF16))
        for i in range(CHUNKS - 1, 0, -1):

            @pl.when(c == i)
            def _():
                if i == LINFORMER:
                    g = scatter.grads[i] + attention.to_items(split(attention.dkv[...])[1])
                    for k in range(8):
                        own_part[k] = g[k * 32 : k * 32 + 32].astype(BF16)
                after(i)

        return carry

    lax.fori_loop(0, CHUNKS, backward_step, 0)
    scatter.send_across()
    d_lin.step(3)
    upd_ref[...] = attention.updated()
    ug_ref[...] = attention.user_grad()
    scatter.send1(0)
    scatter.relay()
    d_lin.step(4)
    d_lin.arrive(4)
    back = dot(proj_ref[...], lin_total[...].reshape(RANK, WIDTH))
    for tile in range(2):
        value = back[tile * TILE : tile * TILE + TILE] + scatter.total(0, tile)
        scatter.wait_cross(tile)
        out_ref[tile * TILE : tile * TILE + TILE] = (value + scatter.z_in[tile].astype(F32)).astype(BF16)
    lin.finish()
    d_lin.finish()
    gather.finish()
    scatter.finish()


def finish_kernel(*refs):
    for k in range(3):
        refs[3 + k][...] = refs[k][...]


def in_vmem(count):
    return [pl.BlockSpec(memory_space=pltpu.VMEM)] * count


def per_device(user_x, item_x, lin_proj, tile_lists, w_q, w_k, w_v, w_o, cotangent):
    shape = jax.ShapeDtypeStruct
    sums = pltpu.VMEM((8, 32, WIDTH), BF16)
    results = pl.pallas_call(
        kernel,
        out_shape=[shape((ROWS, WIDTH), BF16)] * 3,
        in_specs=[pl.BlockSpec(memory_space=pltpu.SMEM)] + in_vmem(8),
        out_specs=in_vmem(3),
        scratch_shapes=[
            pltpu.VMEM((OWNERS, ROWS, WIDTH), BF16),
            sums, sums, sums, sums,
            pltpu.VMEM((CHUNK, WIDTH), BF16),
            pltpu.SMEM((2,), jnp.int32),
        ] + Gather.scratch + Scatter.scratch + Total.scratch + Total.scratch + Attention.scratch,
        compiler_params=pltpu.CompilerParams(
            collective_id=0, has_side_effects=True, vmem_limit_bytes=VMEM_BYTES
        ),
        name="attend_and_exchange",
    )(tile_lists, user_x, item_x, lin_proj, w_q, w_k, w_v, w_o, cotangent)
    return pl.pallas_call(
        finish_kernel,
        out_shape=[shape((ROWS, WIDTH), BF16)] * 3,
        in_specs=in_vmem(3),
        out_specs=in_vmem(3),
        compiler_params=pltpu.CompilerParams(vmem_limit_bytes=VMEM_BYTES),
        name="finish",
    )(*results)


def solution(mesh):
    rows = P(("user", "item"), None)
    return jax.shard_map(
        per_device,
        mesh=mesh,
        in_specs=(rows, rows, rows, P("user", None), P(), P(), P(), P(), rows),
        out_specs=(rows, rows, rows),
        check_vma=False,
    )
```

```python
import functools

import jax
import jax.numpy as jnp
from jax import lax
from jax.experimental import pallas as pl
from jax.experimental.pallas import tpu as pltpu
from jax.sharding import PartitionSpec as P

F32, BF16 = jnp.float32, jnp.bfloat16
HEADS, HEAD, WIDTH, TILE, RANK = 8, 64, 512, 128, 256
ROWS = 256
OWNERS = 16
KEYS = OWNERS * TILE + RANK
CHUNK = 256
CHUNKS = KEYS // CHUNK
VMEM_BYTES = 60 * 1024 * 1024
MESH = pl.DeviceIdType.MESH
ORDER = ((0, 1), (0, 2), (1, 1), (0, 3), None, (1, 2), (0, 0), (1, 3), (1, 0))
LINFORMER = 4
FORWARD = ((0, 1), (0, 2), (0, 3), (0, 0), (1, 1), None, (1, 2), (1, 3), (1, 0))
FORWARD_CODE = sum(ORDER.index(chunk) * CHUNKS**k for k, chunk in enumerate(FORWARD))


def dot(a, b):
    return lax.dot_general(a, b, (((1,), (0,)), ((), ())), preferred_element_type=F32)


def dot_t(a, b):
    return lax.dot_general(a, b, (((1,), (1,)), ((), ())), preferred_element_type=F32)


def split(a):
    high = a.astype(BF16)
    return high, (a - high.astype(F32)).astype(BF16)


class Place:
    def __init__(self):
        self.user, self.item = lax.axis_index("user"), lax.axis_index("item")
        self.near = lax.rem(self.user, 8)
        self.z_lo = lax.div(self.user, 8)
        self.y = lax.rem(self.item, 8)
        self.z_hi = lax.div(self.item, 8)
        self.z = self.z_hi * 4 + self.z_lo
        self.member = (self.near, self.z, self.y)

    def peer(self, group, k):
        if group == 0:
            return (self.z_lo * 8 + k, self.item)
        if group == 1:
            return (lax.rem(k, 4) * 8 + self.near, lax.div(k, 4) * 8 + self.y)
        return (self.user, self.z_hi * 8 + k)

    def along_y(self, step):
        return lax.rem(self.y + step + 8, 8)

    def partner(self):
        return (self.user, lax.rem(self.item + 8, 16))


def greet(place):
    barrier = pltpu.get_barrier_semaphore()
    for group in range(3):
        for r in range(1, 8):
            k = lax.rem(place.member[group] + r, 8)
            pl.semaphore_signal(barrier, inc=1, device_id=place.peer(group, k), device_id_type=MESH)
    pl.semaphore_wait(barrier, 21)


class Total:
    scratch = [
        pltpu.VMEM((8, 32, WIDTH), BF16),
        pltpu.VMEM((8, 8, 256), F32),
        pltpu.VMEM((8, 8, 256), F32),
        pltpu.VMEM((8, 256), F32),
        pltpu.VMEM((8, 8, 256), F32),
        pltpu.VMEM((8, 256), F32),
        pltpu.VMEM((8, 8, 256), F32),
        pltpu.VMEM((32, WIDTH), BF16),
        pltpu.SemaphoreType.DMA((5, 8)),
        pltpu.SemaphoreType.DMA((5, 8)),
    ]

    def __init__(self, place, part, out, scratch):
        self.place, self.part, self.out = place, part, out
        (self.land1, self.s1, self.land2, self.s2, self.land3, self.s3, self.land4, self.s4) = scratch[:8]
        self.send_sem, self.recv_sem = scratch[8:]

    def copies(self, phase):
        group = (0, 1, 2, 1, 0)[phase]
        land = (self.land1, self.land2, self.land3, self.land4, self.out)[phase]
        me = self.place.member[group]
        for r in range(1, 8):
            k = lax.rem(me + r, 8)
            source = (self.part.at[k], self.s1.at[k], self.s2, self.s3, self.s4)[phase]
            yield pltpu.make_async_remote_copy(
                src_ref=source,
                dst_ref=land.at[me],
                send_sem=self.send_sem.at[phase, r],
                recv_sem=self.recv_sem.at[phase, r],
                device_id=self.place.peer(group, k),
                device_id_type=MESH,
            )

    def start(self, phase):
        for copy in self.copies(phase):
            copy.start()

    def arrive(self, phase):
        for copy in self.copies(phase):
            copy.wait_recv()

    def step(self, phase):
        near, z, y = self.place.member
        if phase == 0:
            self.start(0)
            self.land1[near] = self.part[near]
            return
        self.arrive(phase - 1)
        if phase == 1:
            total = self.land1[0].astype(F32)
            for k in range(1, 8):
                total = total + self.land1[k].astype(F32)
            for p in range(8):
                self.s1[p] = total[p // 2 * 8 : p // 2 * 8 + 8, p % 2 * 256 : p % 2 * 256 + 256]
            self.start(1)
            self.land2[z] = self.s1[z]
        elif phase == 2:
            total = self.land2[0]
            for k in range(1, 8):
                total = total + self.land2[k]
            self.s2[...] = total
            self.start(2)
            self.land3[y] = total
        elif phase == 3:
            total = self.land3[0]
            for k in range(1, 8):
                total = total + self.land3[k]
            self.s3[...] = total
            self.start(3)
            self.land4[z] = total
        elif phase == 4:
            bands = [jnp.concatenate([self.land4[2 * p], self.land4[2 * p + 1]], axis=1) for p in range(4)]
            self.s4[...] = jnp.concatenate(bands, axis=0).astype(BF16)
            self.start(4)
            self.out[near] = self.s4[...]

    def finish(self):
        for phase in range(5):
            for copy in self.copies(phase):
                copy.wait_send()


class Attention:
    scratch = [
        pltpu.VMEM((CHUNKS, 4, CHUNK, 128), BF16),
        pltpu.VMEM((CHUNKS, 4, CHUNK, 128), BF16),
        pltpu.VMEM((CHUNKS, HEADS, HEAD, CHUNK), BF16),
        pltpu.VMEM((HEADS, HEAD, CHUNK), BF16),
        pltpu.VMEM((HEADS, 128, ROWS), BF16),
        pltpu.VMEM((HEADS, 128, ROWS), BF16),
        pltpu.VMEM((4, 2 * ROWS, 128), BF16),
        pltpu.VMEM((4, 2 * ROWS, 128), BF16),
        pltpu.VMEM((HEADS, HEAD, ROWS), F32),
        pltpu.VMEM((CHUNKS, HEADS, CHUNK, ROWS), F32),
        pltpu.VMEM((CHUNK, 2 * WIDTH), F32),
        pltpu.VMEM((HEADS, HEAD, ROWS), F32),
        pltpu.VMEM((HEADS, HEAD, ROWS), F32),
        pltpu.VMEM((HEADS, 1, ROWS), F32),
        pltpu.VMEM((HEADS, 1, ROWS), F32),
        pltpu.VMEM((HEADS, 1, ROWS), F32),
        pltpu.VMEM((CHUNKS, HEADS, 1, ROWS), F32),
        pltpu.VMEM((WIDTH, WIDTH), BF16),
        pltpu.VMEM((WIDTH, WIDTH), BF16),
    ]

    def __init__(self, weights, scratch):
        self.wq, self.wk, self.wv, self.wo = weights
        (self.k_s, self.v_s, self.kt_s, self.vt_s, self.qt_m, self.at_m, self.q_m, self.a_m, self.at_s,
         self.e_s, self.dkv, self.o_t, self.dq_t, self.top, self.den, self.delta, self.tops,
         self.wk_t, self.wv_t) = scratch

    def prepare(self, user_ref, cot_ref):
        q = dot(user_ref[...], self.wq[...]).astype(BF16).astype(F32) * (HEAD**-0.5)
        a = dot_t(cot_ref[...], self.wo[...]).astype(BF16).astype(F32)
        qt, at = q.T, a.T
        self.at_s[...] = at.reshape(HEADS, HEAD, ROWS)
        low_lane = lax.broadcasted_iota(jnp.int32, (ROWS, 128), 1) < HEAD
        low_row = lax.broadcasted_iota(jnp.int32, (128, ROWS), 0) < HEAD
        for p in range(4):
            cut = slice(p * 128, p * 128 + 128)
            for hh in range(2):
                lane, row = (low_lane, low_row) if hh == 0 else (~low_lane, ~low_row)
                half = slice(hh * ROWS, hh * ROWS + ROWS)
                self.q_m[p, half] = jnp.where(lane, q[:, cut], 0.0).astype(BF16)
                self.a_m[p, half] = jnp.where(lane, a[:, cut], 0.0).astype(BF16)
                self.qt_m[2 * p + hh] = jnp.where(row, qt[cut], 0.0).astype(BF16)
                self.at_m[2 * p + hh] = jnp.where(row, at[cut], 0.0).astype(BF16)
        self.wk_t[...] = self.wk[...].astype(F32).T.astype(BF16)
        self.wv_t[...] = self.wv[...].astype(F32).T.astype(BF16)
        self.top[...] = jnp.full(self.top.shape, -1e30, F32)
        self.den[...] = jnp.zeros(self.den.shape, F32)
        self.o_t[...] = jnp.zeros(self.o_t.shape, F32)
        self.dq_t[...] = jnp.zeros(self.dq_t.shape, F32)

    def keys(self, c, pieces):
        k = sum(dot(piece, self.wk[...]) for piece in pieces).astype(BF16)
        for p in range(4):
            self.k_s[c, p] = k[:, p * 128 : p * 128 + 128]
        v = sum(dot(piece, self.wv[...]) for piece in pieces).astype(BF16)
        for p in range(4):
            self.v_s[c, p] = v[:, p * 128 : p * 128 + 128]
        kt = sum(dot_t(self.wk_t[...], piece) for piece in pieces).astype(BF16)
        self.kt_s[c] = kt.reshape(HEADS, HEAD, CHUNK)
        vt = sum(dot_t(self.wv_t[...], piece) for piece in pieces).astype(BF16)
        self.vt_s[...] = vt.reshape(HEADS, HEAD, CHUNK)

    def forward(self, c, live):
        keep = [live[0] != 0, live[1] != 0]

        def score(h):
            return dot(self.k_s[c, h // 2], self.qt_m[h])

        s = score(0)
        for h in range(HEADS):
            following = score(h + 1) if h + 1 < HEADS else None
            s = jnp.concatenate(
                [jnp.where(keep[0], s[:TILE], -1e30), jnp.where(keep[1], s[TILE:], -1e30)], axis=0
            )
            before = self.top[h]
            top = jnp.maximum(before, jnp.max(s, axis=0, keepdims=True))
            e = jnp.exp(s - top)
            scale = jnp.exp(before - top)
            self.top[h] = top
            self.tops[c, h] = top
            self.e_s[c, h] = e
            self.den[h] = self.den[h] * scale + jnp.sum(e, axis=0, keepdims=True)
            self.o_t[h] = self.o_t[h] * scale + dot(self.vt_s[h], e.astype(BF16))
            s = following

    def settle(self):
        for h in range(HEADS):
            inverse = 1.0 / self.den[h]
            o = self.o_t[h] * inverse
            self.o_t[h] = o
            self.den[h] = inverse
            self.delta[h] = jnp.sum(o * self.at_s[h], axis=0, keepdims=True)

    def backward(self, c):
        def pull(p):
            return [dot(self.v_s[c, p], self.at_m[2 * p + hh]) for hh in range(2)]

        dp = pull(0)
        for p in range(4):
            following = pull(p + 1) if p < 3 else None
            ds, pb = [], []
            for hh in range(2):
                h = 2 * p + hh
                prob = self.e_s[c, h] * (jnp.exp(self.tops[c, h] - self.top[h]) * self.den[h])
                pb.append(prob.astype(BF16))
                ds.append((prob * (dp[hh] - self.delta[h])).astype(BF16))
                self.dq_t[h] = self.dq_t[h] + dot(self.kt_s[c, h], ds[hh])
            self.dkv[:, p * 128 : p * 128 + 128] = dot(jnp.concatenate(ds, axis=1), self.q_m[p])
            self.dkv[:, WIDTH + p * 128 : WIDTH + p * 128 + 128] = dot(jnp.concatenate(pb, axis=1), self.a_m[p])
            dp = following

    def to_items(self, piece):
        return dot_t(piece[:, :WIDTH], self.wk[...]) + dot_t(piece[:, WIDTH:], self.wv[...])

    def updated(self):
        attended = self.o_t[...].reshape(WIDTH, ROWS).T.astype(BF16)
        return dot(attended, self.wo[...]).astype(BF16)

    def user_grad(self):
        d_query = (self.dq_t[...] * (HEAD**-0.5)).reshape(WIDTH, ROWS).T.astype(BF16)
        return dot_t(d_query, self.wq[...]).astype(BF16)


def ring_peer(place, way, hops=1):
    return place.z_hi * 8 + place.along_y(hops if way == 0 else -hops)


class Ring:
    semaphores = [
        pltpu.SemaphoreType.DMA((2, 2, 8)),
        pltpu.SemaphoreType.DMA((2, 2, 8)),
        pltpu.SemaphoreType.DMA((4,)),
        pltpu.SemaphoreType.DMA((4,)),
        pltpu.VMEM((2, TILE, WIDTH), BF16),
    ]

    def __init__(self, place, sems):
        self.place = place
        self.send_sem, self.recv_sem, self.zs, self.zr, self.relay_buf = sems

    def column(self, chain):
        return (self.place.z_hi if chain == 0 else 1 - self.place.z_hi) * 8

    def copy(self, chain, way, number):
        source, target = self.ends(chain, way, number)
        return pltpu.make_async_remote_copy(
            src_ref=source, dst_ref=target,
            send_sem=self.send_sem.at[chain, way, number], recv_sem=self.recv_sem.at[chain, way, number],
            device_id=(self.place.user, ring_peer(self.place, way)), device_id_type=MESH,
        )

    def push(self, chain, way, number):
        self.copy(chain, way, number).start()

    def wait(self, chain, way, number):
        self.copy(chain, way, number).wait_recv()

    def leap(self, number):
        tile = number % 2
        z = lax.rem(self.place.z + (2 if tile == 0 else 6), 8)
        near, far = self.cross_ends(tile)
        source, target = (near, self.relay_buf.at[tile]) if number < 2 else (self.relay_buf.at[tile], far)
        return pltpu.make_async_remote_copy(
            src_ref=source, dst_ref=target, send_sem=self.zs.at[number], recv_sem=self.zr.at[number],
            device_id=self.place.peer(1, z), device_id_type=MESH,
        )

    def cross(self, tile):
        self.leap(tile).start()

    def relay(self):
        for tile in range(2):
            self.leap(tile).wait_recv()
            self.leap(2 + tile).start()

    def wait_cross(self, tile):
        self.leap(2 + tile).wait_recv()

    def finish(self):
        for number in range(4):
            self.leap(number).wait_send()
        for chain in range(2):
            for way in range(2):
                for number in range(7):
                    self.copy(chain, way, number).wait_send()


def tile_rows(tile):
    return pl.ds(tile * TILE, TILE)


class Gather(Ring):
    scratch = [
        pltpu.VMEM((2, 2, TILE, WIDTH), BF16),
        pltpu.VMEM((2, 2, TILE // 2, WIDTH), BF16),
        pltpu.VMEM((2, 2, TILE, WIDTH), BF16),
        pltpu.VMEM((2, 2, TILE // 2, WIDTH), BF16),
        pltpu.VMEM((2, 2, TILE // 2, WIDTH), BF16),
    ] + Ring.semaphores

    def __init__(self, place, lists, x_ref, all_ref, scratch):
        self.lists, self.x, self.all = lists, x_ref, all_ref
        self.out3, self.out4, self.in3, self.via3, self.in4 = scratch[:5]
        super().__init__(place, scratch[5:])

    def source(self, chain, way, hops):
        return self.column(chain) + self.place.along_y(-hops if way == 0 else hops)

    def block(self, chain, index, own):
        return self.x if own and chain == 0 else self.all.at[index]

    def cross_ends(self, tile):
        z = lax.rem(self.place.z + (6 if tile == 0 else 2), 8)
        index = lax.div(z, 4) * 8 + self.place.y
        return self.x.at[tile_rows(tile)], self.all.at[index, tile_rows(tile)]

    def ends(self, chain, way, number):
        if number < 2:
            index = self.source(chain, way, 0)
            rows = tile_rows(number)
            return self.block(chain, index, True).at[rows], self.all.at[index, rows]
        if number < 4:
            part = self.all.at[self.source(chain, way, 1), tile_rows(number - 2)]
            return part, part
        source, target = {4: (self.out4, self.via3), 5: (self.out3, self.in3), 6: (self.via3, self.in4)}[number]
        return source.at[chain, way], target.at[chain, way]

    def first(self, chain, tile):
        for way in range(2):
            self.push(chain, way, tile)

    def second(self, chain):
        for tile in range(2):
            for way in range(2):
                self.wait(chain, way, tile)
                self.push(chain, way, 2 + tile)

    def third(self, chain):
        for way in range(2):
            index = self.source(chain, way, 2)
            for tile in range(2):
                self.wait(chain, way, 2 + tile)
            far = self.lists[ring_peer(self.place, way, 2), index] == 1
            low = way * (TILE // 2)
            self.out4[chain, way] = jnp.where(
                far,
                self.all[index, TILE + low : TILE + low + TILE // 2],
                self.all[index, low : low + TILE // 2],
            )
            self.push(chain, way, 4)
            near = self.lists[ring_peer(self.place, way, 1), index] == 1
            self.out3[chain, way] = jnp.where(near, self.all[index, TILE:], self.all[index, :TILE])
            self.push(chain, way, 5)

    def fourth(self, chain):
        for way in range(2):
            self.wait(chain, way, 4)
            self.push(chain, way, 6)

    def tiles(self, chain, e):
        found, live = [], []
        for way in ((1, 0) if e else (None, 4)):
            hops = 4 if way == 4 else e
            index = self.source(chain, 0 if way in (None, 4) else way, hops)
            tile = self.lists[self.place.item, index]
            live.append((tile < 2).astype(jnp.int32))
            if way == 4:
                for way in range(2):
                    self.wait(chain, way, 6)
                    found.append(self.in4[chain, way])
            elif e == 3:
                self.wait(chain, way, 5)
                found.append(self.in3[chain, way])
            else:
                block = self.block(chain, index, e == 0)
                found.append(jnp.where(tile == 1, block[TILE:], block[:TILE]))
        return jnp.concatenate(found, axis=0), live


class Scatter(Ring):
    scratch = [
        pltpu.VMEM((2, 2, TILE // 2, WIDTH), BF16),
        pltpu.VMEM((2, 2, TILE // 2, WIDTH), BF16),
        pltpu.VMEM((2, 2, TILE // 2, WIDTH), BF16),
        pltpu.VMEM((2, 2, TILE, WIDTH), BF16),
        pltpu.VMEM((2, 2, TILE, WIDTH), BF16),
        pltpu.VMEM((2, 2, 2, TILE, WIDTH), BF16),
        pltpu.VMEM((2, 2, 2, TILE, WIDTH), BF16),
        pltpu.VMEM((2, 2, 2, TILE, WIDTH), BF16),
        pltpu.VMEM((2, 2, 2, TILE, WIDTH), BF16),
        pltpu.VMEM((2, TILE, WIDTH), BF16),
        pltpu.VMEM((2, TILE, WIDTH), BF16),
        pltpu.VMEM((CHUNKS, CHUNK, WIDTH), F32),
    ] + Ring.semaphores

    def __init__(self, place, lists, scratch):
        self.lists = lists
        (self.out4, self.via3, self.in4, self.out3, self.in3, self.out2, self.in2, self.out1, self.in1,
         self.z_out, self.z_in, self.grads) = scratch[:12]
        super().__init__(place, scratch[12:])

    def owner(self, chain, way, hops):
        return self.column(chain) + self.place.along_y(hops if way == 0 else -hops)

    def cross_ends(self, tile):
        return self.z_out.at[tile], self.z_in.at[tile]

    def ends(self, chain, way, number):
        if number < 3:
            source, target = ((self.out4, self.via3), (self.via3, self.in4), (self.out3, self.in3))[number]
            return source.at[chain, way], target.at[chain, way]
        source, target = (self.out2, self.in2) if number < 5 else (self.out1, self.in1)
        tile = (number - 3) % 2
        return source.at[chain, way, tile], target.at[chain, way, tile]

    def own(self, chain, way, e):
        return self.grads[ORDER.index((chain, e)), tile_rows(0 if way == 0 else 1)]

    def lists_here(self, index, tile):
        return self.lists[self.place.item, index] == tile

    def send4(self, chain):
        for way in range(2):
            low = TILE + way * (TILE // 2)
            self.out4[chain, way] = self.grads[ORDER.index((chain, 0)), low : low + TILE // 2].astype(BF16)
            self.push(chain, way, 0)

    def send3(self, chain):
        for way in range(2):
            self.out3[chain, way] = self.own(chain, way, 3).astype(BF16)
            self.wait(chain, way, 0)
            self.push(chain, way, 1)
            self.push(chain, way, 2)

    def send2(self, chain):
        for way in range(2):
            index = self.owner(chain, way, 2)
            one, two = ring_peer(self.place, way, -1), ring_peer(self.place, way, -2)
            self.wait(chain, way, 1)
            self.wait(chain, way, 2)
            half = slice(way * (TILE // 2), way * (TILE // 2) + TILE // 2)
            other = slice((1 - way) * (TILE // 2), (1 - way) * (TILE // 2) + TILE // 2)
            for tile in range(2):
                value = jnp.where(self.lists_here(index, tile), self.own(chain, way, 2), 0.0)
                value = value + jnp.where(
                    self.lists[one, index] == tile, self.in3[chain, way].astype(F32), 0.0
                )
                far = jnp.where(self.lists[two, index] == tile, self.in4[chain, way].astype(F32), 0.0)
                self.out2[chain, way, tile, half] = (value[half] + far).astype(BF16)
                self.out2[chain, way, tile, other] = value[other].astype(BF16)
                self.push(chain, way, 3 + tile)

    def send1(self, chain):
        for tile in range(2):
            for way in range(2):
                index = self.owner(chain, way, 1)
                self.wait(chain, way, 3 + tile)
                value = jnp.where(self.lists_here(index, tile), self.own(chain, way, 1), 0.0)
                value = value + self.in2[chain, way, tile].astype(F32)
                self.out1[chain, way, tile] = value.astype(BF16)
                self.push(chain, way, 5 + tile)

    def total(self, chain, tile):
        for way in range(2):
            self.wait(chain, way, 5 + tile)
        value = jnp.where(self.lists_here(self.owner(chain, 0, 0), tile), self.own(chain, 0, 0), 0.0)
        return value + self.in1[chain, 0, tile].astype(F32) + self.in1[chain, 1, tile].astype(F32)

    def send_across(self):
        for tile in range(2):
            self.z_out[tile] = self.total(1, tile).astype(BF16)
            self.cross(tile)


def take(scratch, count):
    taken = scratch[:count]
    del scratch[:count]
    return taken


def kernel(
    lists_ref, x_ref, proj_ref, user_hbm, cot_hbm, wq_hbm, wk_hbm, wv_hbm, wo_hbm, upd_hbm, ug_hbm, out_ref,
    user_ref, cot_ref, wq_ref, wk_ref, wv_ref, wo_ref, upd_ref, ug_ref, local_sem, all_x, part, lin_sum, lin_total, own_part, listed, live, *scratch
):
    scratch = list(scratch)
    place = Place()
    gather = Gather(place, lists_ref, x_ref, all_x, take(scratch, len(Gather.scratch)))
    scatter = Scatter(place, lists_ref, take(scratch, len(Scatter.scratch)))
    lin = Total(place, part, lin_sum, take(scratch, len(Total.scratch)))
    d_lin = Total(place, own_part, lin_total, take(scratch, len(Total.scratch)))
    attention = Attention((wq_ref, wk_ref, wv_ref, wo_ref), scratch)

    arriving = [
        pltpu.make_async_copy(source, target, local_sem.at[k])
        for k, (source, target) in enumerate(
            (
                (user_hbm, user_ref), (wq_hbm, wq_ref), (cot_hbm, cot_ref), (wo_hbm, wo_ref),
                (wk_hbm, wk_ref), (wv_hbm, wv_ref),
            )
        )
    ]
    for copy in arriving:
        copy.start()
    greet(place)
    for tile in range(2):
        gather.first(0, tile)
        gather.cross(tile)
    total = lax.dot_general(
        proj_ref[...], x_ref[...], (((0,), (0,)), ((), ())), preferred_element_type=F32
    )
    for k in range(8):
        part[k] = total[k * 32 : k * 32 + 32].astype(BF16)
    lin.step(0)
    for copy in arriving:
        copy.wait()
    attention.prepare(user_ref, cot_ref)

    def before(i):
        if i == 0:
            gather.second(0)
            gather.relay()
        elif i == 1:
            lin.step(1)
            gather.third(0)
            for tile in range(2):
                gather.wait_cross(tile)
                gather.first(1, tile)
        elif i == 2:
            gather.fourth(0)
            lin.step(2)
        elif i == 3:
            lin.step(3)
        elif i == 4:
            gather.second(1)
            lin.step(4)
        elif i == 5:
            lin.arrive(4)
        elif i == 6:
            gather.third(1)
        elif i == 7:
            gather.fourth(1)

    def forward_step(step, code):
        c = lax.rem(code, CHUNKS)
        for i, chunk in enumerate(FORWARD):

            @pl.when(step == i)
            def _():
                before(i)
                if chunk is None:
                    live[0], live[1] = jnp.int32(1), jnp.int32(1)
                    listed[...] = lin_sum[...].reshape(RANK, WIDTH)
                else:
                    rows, alive = gather.tiles(*chunk)
                    listed[...] = rows
                    live[0], live[1] = alive

        attention.keys(c, (listed[...],))
        attention.forward(c, live)
        return lax.div(code, CHUNKS)

    lax.fori_loop(0, CHUNKS, forward_step, jnp.int32(FORWARD_CODE))
    attention.settle()

    def after(i):
        if i == 8:
            scatter.send4(1)
        elif i == 7:
            scatter.send3(1)
        elif i == 6:
            scatter.send4(0)
        elif i == 5:
            scatter.send2(1)
        elif i == 4:
            d_lin.step(0)
        elif i == 3:
            scatter.send3(0)
        elif i == 2:
            scatter.send1(1)
            d_lin.step(1)
        elif i == 1:
            scatter.send2(0)
            d_lin.step(2)

    def backward_step(step, carry):
        c = CHUNKS - 1 - step
        attention.backward(c)
        scatter.grads[c] = attention.to_items(attention.dkv[...].astype(BF16))
        for i in range(CHUNKS - 1, 0, -1):

            @pl.when(c == i)
            def _():
                if i == LINFORMER:
                    g = scatter.grads[i] + attention.to_items(split(attention.dkv[...])[1])
                    for k in range(8):
                        own_part[k] = g[k * 32 : k * 32 + 32].astype(BF16)
                after(i)

        return carry

    lax.fori_loop(0, CHUNKS, backward_step, 0)
    scatter.send_across()
    d_lin.step(3)
    upd_ref[...] = attention.updated()
    ug_ref[...] = attention.user_grad()
    leaving = [
        pltpu.make_async_copy(upd_ref, upd_hbm, local_sem.at[6]),
        pltpu.make_async_copy(ug_ref, ug_hbm, local_sem.at[7]),
    ]
    for copy in leaving:
        copy.start()
    scatter.send1(0)
    scatter.relay()
    d_lin.step(4)
    d_lin.arrive(4)
    back = dot(proj_ref[...], lin_total[...].reshape(RANK, WIDTH))
    for tile in range(2):
        value = back[tile * TILE : tile * TILE + TILE] + scatter.total(0, tile)
        scatter.wait_cross(tile)
        out_ref[tile * TILE : tile * TILE + TILE] = (value + scatter.z_in[tile].astype(F32)).astype(BF16)
    for copy in leaving:
        copy.wait()
    lin.finish()
    d_lin.finish()
    gather.finish()
    scatter.finish()


def finish_kernel(*refs):
    for k in range(3):
        refs[3 + k][...] = refs[k][...]


def in_vmem(count):
    return [pl.BlockSpec(memory_space=pltpu.VMEM)] * count


def anywhere(count):
    return [pl.BlockSpec(memory_space=pl.ANY)] * count


def per_device(user_x, item_x, lin_proj, tile_lists, w_q, w_k, w_v, w_o, cotangent):
    shape = jax.ShapeDtypeStruct
    sums = pltpu.VMEM((8, 32, WIDTH), BF16)
    users, weights = pltpu.VMEM((ROWS, WIDTH), BF16), pltpu.VMEM((WIDTH, WIDTH), BF16)
    results = pl.pallas_call(
        kernel,
        out_shape=[shape((ROWS, WIDTH), BF16)] * 3,
        in_specs=[pl.BlockSpec(memory_space=pltpu.SMEM)] + in_vmem(2) + anywhere(6),
        out_specs=anywhere(2) + in_vmem(1),
        scratch_shapes=[
            users, users, weights, weights, weights, weights, users, users,
            pltpu.SemaphoreType.DMA((8,)),
            pltpu.VMEM((OWNERS, ROWS, WIDTH), BF16),
            sums, sums, sums, sums,
            pltpu.VMEM((CHUNK, WIDTH), BF16),
            pltpu.SMEM((2,), jnp.int32),
        ] + Gather.scratch + Scatter.scratch + Total.scratch + Total.scratch + Attention.scratch,
        compiler_params=pltpu.CompilerParams(
            collective_id=0, has_side_effects=True, vmem_limit_bytes=VMEM_BYTES
        ),
        name="attend_and_exchange",
    )(tile_lists, item_x, lin_proj, user_x, cotangent, w_q, w_k, w_v, w_o)
    return pl.pallas_call(
        finish_kernel,
        out_shape=[shape((ROWS, WIDTH), BF16)] * 3,
        in_specs=in_vmem(3),
        out_specs=in_vmem(3),
        compiler_params=pltpu.CompilerParams(vmem_limit_bytes=VMEM_BYTES),
        name="finish",
    )(*results)


def solution(mesh):
    rows = P(("user", "item"), None)
    return jax.shard_map(
        per_device,
        mesh=mesh,
        in_specs=(rows, rows, rows, P("user", None), P(), P(), P(), P(), rows),
        out_specs=(rows, rows, rows),
        check_vma=False,
    )
```

```python
import functools

import jax
import jax.numpy as jnp
from jax import lax
from jax.experimental import pallas as pl
from jax.experimental.pallas import tpu as pltpu
from jax.sharding import PartitionSpec as P

F32, BF16 = jnp.float32, jnp.bfloat16
HEADS, HEAD, WIDTH, TILE, RANK = 8, 64, 512, 128, 256
ROWS = 256
OWNERS = 16
KEYS = OWNERS * TILE + RANK
CHUNK = 256
CHUNKS = KEYS // CHUNK
VMEM_BYTES = 60 * 1024 * 1024
MESH = pl.DeviceIdType.MESH
ORDER = ((0, 1), (0, 2), (1, 1), (0, 3), None, (1, 2), (0, 0), (1, 3), (1, 0))
LINFORMER = 4
FORWARD = ((0, 1), (0, 2), (0, 3), (0, 0), (1, 1), None, (1, 2), (1, 3), (1, 0))
FORWARD_CODE = sum(ORDER.index(chunk) * CHUNKS**k for k, chunk in enumerate(FORWARD))


def dot(a, b):
    return lax.dot_general(a, b, (((1,), (0,)), ((), ())), preferred_element_type=F32)


def dot_t(a, b):
    return lax.dot_general(a, b, (((1,), (1,)), ((), ())), preferred_element_type=F32)


def split(a):
    high = a.astype(BF16)
    return high, (a - high.astype(F32)).astype(BF16)


class Place:
    def __init__(self):
        self.user, self.item = lax.axis_index("user"), lax.axis_index("item")
        self.near = lax.rem(self.user, 8)
        self.z_lo = lax.div(self.user, 8)
        self.y = lax.rem(self.item, 8)
        self.z_hi = lax.div(self.item, 8)
        self.z = self.z_hi * 4 + self.z_lo
        self.member = (self.near, self.z, self.y)

    def peer(self, group, k):
        if group == 0:
            return (self.z_lo * 8 + k, self.item)
        if group == 1:
            return (lax.rem(k, 4) * 8 + self.near, lax.div(k, 4) * 8 + self.y)
        return (self.user, self.z_hi * 8 + k)

    def along_y(self, step):
        return lax.rem(self.y + step + 8, 8)

    def partner(self):
        return (self.user, lax.rem(self.item + 8, 16))


def greet(place):
    barrier = pltpu.get_barrier_semaphore()
    for group in range(3):
        for r in range(1, 8):
            k = lax.rem(place.member[group] + r, 8)
            pl.semaphore_signal(barrier, inc=1, device_id=place.peer(group, k), device_id_type=MESH)
    pl.semaphore_wait(barrier, 21)


class Total:
    scratch = [
        pltpu.VMEM((8, 32, WIDTH), BF16),
        pltpu.VMEM((8, 8, 256), F32),
        pltpu.VMEM((8, 8, 256), F32),
        pltpu.VMEM((8, 256), F32),
        pltpu.VMEM((8, 8, 256), F32),
        pltpu.VMEM((8, 256), F32),
        pltpu.VMEM((8, 8, 256), F32),
        pltpu.VMEM((32, WIDTH), BF16),
        pltpu.SemaphoreType.DMA((5, 8)),
        pltpu.SemaphoreType.DMA((5, 8)),
    ]

    def __init__(self, place, part, out, scratch):
        self.place, self.part, self.out = place, part, out
        (self.land1, self.s1, self.land2, self.s2, self.land3, self.s3, self.land4, self.s4) = scratch[:8]
        self.send_sem, self.recv_sem = scratch[8:]

    def copies(self, phase):
        group = (0, 1, 2, 1, 0)[phase]
        land = (self.land1, self.land2, self.land3, self.land4, self.out)[phase]
        me = self.place.member[group]
        for r in range(1, 8):
            k = lax.rem(me + r, 8)
            source = (self.part.at[k], self.s1.at[k], self.s2, self.s3, self.s4)[phase]
            yield pltpu.make_async_remote_copy(
                src_ref=source,
                dst_ref=land.at[me],
                send_sem=self.send_sem.at[phase, r],
                recv_sem=self.recv_sem.at[phase, r],
                device_id=self.place.peer(group, k),
                device_id_type=MESH,
            )

    def start(self, phase):
        for copy in self.copies(phase):
            copy.start()

    def arrive(self, phase):
        for copy in self.copies(phase):
            copy.wait_recv()

    def step(self, phase):
        near, z, y = self.place.member
        if phase == 0:
            self.start(0)
            self.land1[near] = self.part[near]
            return
        self.arrive(phase - 1)
        if phase == 1:
            total = self.land1[0].astype(F32)
            for k in range(1, 8):
                total = total + self.land1[k].astype(F32)
            for p in range(8):
                self.s1[p] = total[p // 2 * 8 : p // 2 * 8 + 8, p % 2 * 256 : p % 2 * 256 + 256]
            self.start(1)
            self.land2[z] = self.s1[z]
        elif phase == 2:
            total = self.land2[0]
            for k in range(1, 8):
                total = total + self.land2[k]
            self.s2[...] = total
            self.start(2)
            self.land3[y] = total
        elif phase == 3:
            total = self.land3[0]
            for k in range(1, 8):
                total = total + self.land3[k]
            self.s3[...] = total
            self.start(3)
            self.land4[z] = total
        elif phase == 4:
            bands = [jnp.concatenate([self.land4[2 * p], self.land4[2 * p + 1]], axis=1) for p in range(4)]
            self.s4[...] = jnp.concatenate(bands, axis=0).astype(BF16)
            self.start(4)
            self.out[near] = self.s4[...]

    def finish(self, phases):
        for phase in phases:
            for copy in self.copies(phase):
                copy.wait_send()


class Attention:
    scratch = [
        pltpu.VMEM((CHUNKS, 4, CHUNK, 128), BF16),
        pltpu.VMEM((CHUNKS, 4, CHUNK, 128), BF16),
        pltpu.VMEM((CHUNKS, HEADS, HEAD, CHUNK), BF16),
        pltpu.VMEM((HEADS, HEAD, CHUNK), BF16),
        pltpu.VMEM((HEADS, 128, ROWS), BF16),
        pltpu.VMEM((HEADS, 128, ROWS), BF16),
        pltpu.VMEM((4, 2 * ROWS, 128), BF16),
        pltpu.VMEM((4, 2 * ROWS, 128), BF16),
        pltpu.VMEM((HEADS, HEAD, ROWS), F32),
        pltpu.VMEM((CHUNKS, HEADS, CHUNK, ROWS), F32),
        pltpu.VMEM((CHUNK, 2 * WIDTH), F32),
        pltpu.VMEM((HEADS, HEAD, ROWS), F32),
        pltpu.VMEM((HEADS, HEAD, ROWS), F32),
        pltpu.VMEM((HEADS, 1, ROWS), F32),
        pltpu.VMEM((HEADS, 1, ROWS), F32),
        pltpu.VMEM((HEADS, 1, ROWS), F32),
        pltpu.VMEM((CHUNKS, HEADS, 1, ROWS), F32),
        pltpu.VMEM((WIDTH, WIDTH), BF16),
        pltpu.VMEM((WIDTH, WIDTH), BF16),
    ]

    def __init__(self, weights, scratch):
        self.wq, self.wk, self.wv, self.wo = weights
        (self.k_s, self.v_s, self.kt_s, self.vt_s, self.qt_m, self.at_m, self.q_m, self.a_m, self.at_s,
         self.e_s, self.dkv, self.o_t, self.dq_t, self.top, self.den, self.delta, self.tops,
         self.wk_t, self.wv_t) = scratch

    def prepare(self, user_ref, cot_ref):
        q = dot(user_ref[...], self.wq[...]).astype(BF16).astype(F32) * (HEAD**-0.5)
        a = dot_t(cot_ref[...], self.wo[...]).astype(BF16).astype(F32)
        qt, at = q.T, a.T
        self.at_s[...] = at.reshape(HEADS, HEAD, ROWS)
        low_lane = lax.broadcasted_iota(jnp.int32, (ROWS, 128), 1) < HEAD
        low_row = lax.broadcasted_iota(jnp.int32, (128, ROWS), 0) < HEAD
        for p in range(4):
            cut = slice(p * 128, p * 128 + 128)
            for hh in range(2):
                lane, row = (low_lane, low_row) if hh == 0 else (~low_lane, ~low_row)
                half = slice(hh * ROWS, hh * ROWS + ROWS)
                self.q_m[p, half] = jnp.where(lane, q[:, cut], 0.0).astype(BF16)
                self.a_m[p, half] = jnp.where(lane, a[:, cut], 0.0).astype(BF16)
                self.qt_m[2 * p + hh] = jnp.where(row, qt[cut], 0.0).astype(BF16)
                self.at_m[2 * p + hh] = jnp.where(row, at[cut], 0.0).astype(BF16)
        self.wk_t[...] = self.wk[...].astype(F32).T.astype(BF16)
        self.wv_t[...] = self.wv[...].astype(F32).T.astype(BF16)
        self.top[...] = jnp.full(self.top.shape, -1e30, F32)
        self.den[...] = jnp.zeros(self.den.shape, F32)
        self.o_t[...] = jnp.zeros(self.o_t.shape, F32)
        self.dq_t[...] = jnp.zeros(self.dq_t.shape, F32)

    def keys(self, c, pieces):
        k = sum(dot(piece, self.wk[...]) for piece in pieces).astype(BF16)
        for p in range(4):
            self.k_s[c, p] = k[:, p * 128 : p * 128 + 128]
        v = sum(dot(piece, self.wv[...]) for piece in pieces).astype(BF16)
        for p in range(4):
            self.v_s[c, p] = v[:, p * 128 : p * 128 + 128]
        kt = sum(dot_t(self.wk_t[...], piece) for piece in pieces).astype(BF16)
        self.kt_s[c] = kt.reshape(HEADS, HEAD, CHUNK)
        vt = sum(dot_t(self.wv_t[...], piece) for piece in pieces).astype(BF16)
        self.vt_s[...] = vt.reshape(HEADS, HEAD, CHUNK)

    def forward(self, c, live):
        keep = [live[0] != 0, live[1] != 0]

        def score(h):
            return dot(self.k_s[c, h // 2], self.qt_m[h])

        s = score(0)
        for h in range(HEADS):
            following = score(h + 1) if h + 1 < HEADS else None
            s = jnp.concatenate(
                [jnp.where(keep[0], s[:TILE], -1e30), jnp.where(keep[1], s[TILE:], -1e30)], axis=0
            )
            before = self.top[h]
            top = jnp.maximum(before, jnp.max(s, axis=0, keepdims=True))
            e = jnp.exp(s - top)
            scale = jnp.exp(before - top)
            self.top[h] = top
            self.tops[c, h] = top
            self.e_s[c, h] = e
            self.den[h] = self.den[h] * scale + jnp.sum(e, axis=0, keepdims=True)
            self.o_t[h] = self.o_t[h] * scale + dot(self.vt_s[h], e.astype(BF16))
            s = following

    def settle(self):
        for h in range(HEADS):
            inverse = 1.0 / self.den[h]
            o = self.o_t[h] * inverse
            self.o_t[h] = o
            self.den[h] = inverse
            self.delta[h] = jnp.sum(o * self.at_s[h], axis=0, keepdims=True)

    def backward(self, c):
        def pull(p):
            return [dot(self.v_s[c, p], self.at_m[2 * p + hh]) for hh in range(2)]

        dp = pull(0)
        for p in range(4):
            following = pull(p + 1) if p < 3 else None
            ds, pb = [], []
            for hh in range(2):
                h = 2 * p + hh
                prob = self.e_s[c, h] * (jnp.exp(self.tops[c, h] - self.top[h]) * self.den[h])
                pb.append(prob.astype(BF16))
                ds.append((prob * (dp[hh] - self.delta[h])).astype(BF16))
                self.dq_t[h] = self.dq_t[h] + dot(self.kt_s[c, h], ds[hh])
            self.dkv[:, p * 128 : p * 128 + 128] = dot(jnp.concatenate(ds, axis=1), self.q_m[p])
            self.dkv[:, WIDTH + p * 128 : WIDTH + p * 128 + 128] = dot(jnp.concatenate(pb, axis=1), self.a_m[p])
            dp = following

    def to_items(self, piece):
        return dot_t(piece[:, :WIDTH], self.wk[...]) + dot_t(piece[:, WIDTH:], self.wv[...])

    def updated(self):
        attended = self.o_t[...].reshape(WIDTH, ROWS).T.astype(BF16)
        return dot(attended, self.wo[...]).astype(BF16)

    def user_grad(self):
        d_query = (self.dq_t[...] * (HEAD**-0.5)).reshape(WIDTH, ROWS).T.astype(BF16)
        return dot_t(d_query, self.wq[...]).astype(BF16)


def ring_peer(place, way, hops=1):
    return place.z_hi * 8 + place.along_y(hops if way == 0 else -hops)


class Ring:
    semaphores = [
        pltpu.SemaphoreType.DMA((2, 2, 8)),
        pltpu.SemaphoreType.DMA((2, 2, 8)),
        pltpu.SemaphoreType.DMA((4,)),
        pltpu.SemaphoreType.DMA((4,)),
        pltpu.VMEM((2, TILE, WIDTH), BF16),
    ]

    def __init__(self, place, sems):
        self.place = place
        self.send_sem, self.recv_sem, self.zs, self.zr, self.relay_buf = sems

    def column(self, chain):
        return (self.place.z_hi if chain == 0 else 1 - self.place.z_hi) * 8

    def copy(self, chain, way, number):
        source, target = self.ends(chain, way, number)
        return pltpu.make_async_remote_copy(
            src_ref=source, dst_ref=target,
            send_sem=self.send_sem.at[chain, way, number], recv_sem=self.recv_sem.at[chain, way, number],
            device_id=(self.place.user, ring_peer(self.place, way, 2 if number == self.double else 1)),
            device_id_type=MESH,
        )

    def push(self, chain, way, number):
        self.copy(chain, way, number).start()

    def wait(self, chain, way, number):
        self.copy(chain, way, number).wait_recv()

    def leap(self, number):
        tile = number % 2
        z = lax.rem(self.place.z + (2 if tile == 0 else 6), 8)
        near, far = self.cross_ends(tile)
        source, target = (near, self.relay_buf.at[tile]) if number < 2 else (self.relay_buf.at[tile], far)
        return pltpu.make_async_remote_copy(
            src_ref=source, dst_ref=target, send_sem=self.zs.at[number], recv_sem=self.zr.at[number],
            device_id=self.place.peer(1, z), device_id_type=MESH,
        )

    def cross(self, tile):
        self.leap(tile).start()

    def relay(self):
        for tile in range(2):
            self.leap(tile).wait_recv()
            self.leap(2 + tile).start()

    def wait_cross(self, tile):
        self.leap(2 + tile).wait_recv()

    def finish(self, numbers):
        for chain in range(2):
            for way in range(2):
                for number in numbers:
                    self.copy(chain, way, number).wait_send()

    def finish_cross(self):
        for number in range(4):
            self.leap(number).wait_send()


def tile_rows(tile):
    return pl.ds(tile * TILE, TILE)


class Gather(Ring):
    scratch = [
        pltpu.VMEM((2, 2, TILE, WIDTH), BF16),
        pltpu.VMEM((2, 2, TILE // 2, WIDTH), BF16),
        pltpu.VMEM((2, 2, TILE, WIDTH), BF16),
        pltpu.VMEM((2, 2, TILE // 2, WIDTH), BF16),
    ] + Ring.semaphores
    double = 4

    def __init__(self, place, lists, x_ref, all_ref, scratch):
        self.lists, self.x, self.all = lists, x_ref, all_ref
        self.out3, self.out4, self.in3, self.in4 = scratch[:4]
        super().__init__(place, scratch[4:])

    def source(self, chain, way, hops):
        return self.column(chain) + self.place.along_y(-hops if way == 0 else hops)

    def block(self, chain, index, own):
        return self.x if own and chain == 0 else self.all.at[index]

    def cross_ends(self, tile):
        z = lax.rem(self.place.z + (6 if tile == 0 else 2), 8)
        index = lax.div(z, 4) * 8 + self.place.y
        return self.x.at[tile_rows(tile)], self.all.at[index, tile_rows(tile)]

    def ends(self, chain, way, number):
        if number < 2:
            index = self.source(chain, way, 0)
            rows = tile_rows(number)
            return self.block(chain, index, True).at[rows], self.all.at[index, rows]
        if number < 4:
            part = self.all.at[self.source(chain, way, 1), tile_rows(number - 2)]
            return part, part
        source, target = (self.out4, self.in4) if number == 4 else (self.out3, self.in3)
        return source.at[chain, way], target.at[chain, way]

    def first(self, chain, tile):
        for way in range(2):
            self.push(chain, way, tile)

    def second(self, chain):
        for tile in range(2):
            for way in range(2):
                self.wait(chain, way, tile)
                self.push(chain, way, 2 + tile)

    def third(self, chain):
        for way in range(2):
            index = self.source(chain, way, 2)
            for tile in range(2):
                self.wait(chain, way, 2 + tile)
            far = self.lists[ring_peer(self.place, way, 2), index] == 1
            low = way * (TILE // 2)
            self.out4[chain, way] = jnp.where(
                far,
                self.all[index, TILE + low : TILE + low + TILE // 2],
                self.all[index, low : low + TILE // 2],
            )
            self.push(chain, way, 4)
            near = self.lists[ring_peer(self.place, way, 1), index] == 1
            self.out3[chain, way] = jnp.where(near, self.all[index, TILE:], self.all[index, :TILE])
            self.push(chain, way, 5)

    def tiles(self, chain, e):
        found, live = [], []
        for way in ((1, 0) if e else (None, 4)):
            hops = 4 if way == 4 else e
            index = self.source(chain, 0 if way in (None, 4) else way, hops)
            tile = self.lists[self.place.item, index]
            live.append((tile < 2).astype(jnp.int32))
            if way == 4:
                for way in range(2):
                    self.wait(chain, way, 4)
                    found.append(self.in4[chain, way])
            elif e == 3:
                self.wait(chain, way, 5)
                found.append(self.in3[chain, way])
            else:
                block = self.block(chain, index, e == 0)
                found.append(jnp.where(tile == 1, block[TILE:], block[:TILE]))
        return jnp.concatenate(found, axis=0), live


class Scatter(Ring):
    scratch = [
        pltpu.VMEM((2, 2, TILE // 2, WIDTH), BF16),
        pltpu.VMEM((2, 2, TILE // 2, WIDTH), BF16),
        pltpu.VMEM((2, 2, TILE, WIDTH), BF16),
        pltpu.VMEM((2, 2, TILE, WIDTH), BF16),
        pltpu.VMEM((2, 2, 2, TILE, WIDTH), BF16),
        pltpu.VMEM((2, 2, 2, TILE, WIDTH), BF16),
        pltpu.VMEM((2, 2, 2, TILE, WIDTH), BF16),
        pltpu.VMEM((2, 2, 2, TILE, WIDTH), BF16),
        pltpu.VMEM((2, TILE, WIDTH), BF16),
        pltpu.VMEM((2, TILE, WIDTH), BF16),
        pltpu.VMEM((CHUNKS, CHUNK, WIDTH), F32),
    ] + Ring.semaphores
    double = 0

    def __init__(self, place, lists, scratch):
        self.lists = lists
        (self.out4, self.in4, self.out3, self.in3, self.out2, self.in2, self.out1, self.in1,
         self.z_out, self.z_in, self.grads) = scratch[:11]
        super().__init__(place, scratch[11:])

    def owner(self, chain, way, hops):
        return self.column(chain) + self.place.along_y(hops if way == 0 else -hops)

    def cross_ends(self, tile):
        return self.z_out.at[tile], self.z_in.at[tile]

    def ends(self, chain, way, number):
        if number < 3:
            source, target = (self.out4, self.in4) if number == 0 else (self.out3, self.in3)
            return source.at[chain, way], target.at[chain, way]
        source, target = (self.out2, self.in2) if number < 5 else (self.out1, self.in1)
        tile = (number - 3) % 2
        return source.at[chain, way, tile], target.at[chain, way, tile]

    def own(self, chain, way, e):
        return self.grads[ORDER.index((chain, e)), tile_rows(0 if way == 0 else 1)]

    def lists_here(self, index, tile):
        return self.lists[self.place.item, index] == tile

    def send4(self, chain):
        for way in range(2):
            low = TILE + way * (TILE // 2)
            self.out4[chain, way] = self.grads[ORDER.index((chain, 0)), low : low + TILE // 2].astype(BF16)
            self.push(chain, way, 0)

    def send3(self, chain):
        for way in range(2):
            self.out3[chain, way] = self.own(chain, way, 3).astype(BF16)
            self.push(chain, way, 2)

    def send2(self, chain):
        for way in range(2):
            index = self.owner(chain, way, 2)
            one, two = ring_peer(self.place, way, -1), ring_peer(self.place, way, -2)
            self.wait(chain, way, 0)
            self.wait(chain, way, 2)
            half = slice(way * (TILE // 2), way * (TILE // 2) + TILE // 2)
            other = slice((1 - way) * (TILE // 2), (1 - way) * (TILE // 2) + TILE // 2)
            for tile in range(2):
                value = jnp.where(self.lists_here(index, tile), self.own(chain, way, 2), 0.0)
                value = value + jnp.where(
                    self.lists[one, index] == tile, self.in3[chain, way].astype(F32), 0.0
                )
                far = jnp.where(self.lists[two, index] == tile, self.in4[chain, way].astype(F32), 0.0)
                self.out2[chain, way, tile, half] = (value[half] + far).astype(BF16)
                self.out2[chain, way, tile, other] = value[other].astype(BF16)
                self.push(chain, way, 3 + tile)

    def send1(self, chain):
        for tile in range(2):
            for way in range(2):
                index = self.owner(chain, way, 1)
                self.wait(chain, way, 3 + tile)
                value = jnp.where(self.lists_here(index, tile), self.own(chain, way, 1), 0.0)
                value = value + self.in2[chain, way, tile].astype(F32)
                self.out1[chain, way, tile] = value.astype(BF16)
                self.push(chain, way, 5 + tile)

    def total(self, chain, tile):
        for way in range(2):
            self.wait(chain, way, 5 + tile)
        value = jnp.where(self.lists_here(self.owner(chain, 0, 0), tile), self.own(chain, 0, 0), 0.0)
        return value + self.in1[chain, 0, tile].astype(F32) + self.in1[chain, 1, tile].astype(F32)

    def send_across(self):
        for tile in range(2):
            self.z_out[tile] = self.total(1, tile).astype(BF16)
            self.cross(tile)


def take(scratch, count):
    taken = scratch[:count]
    del scratch[:count]
    return taken


def kernel(
    lists_ref, x_ref, proj_ref, user_hbm, cot_hbm, wq_hbm, wk_hbm, wv_hbm, wo_hbm, upd_hbm, ug_hbm, out_ref,
    user_ref, cot_ref, wq_ref, wk_ref, wv_ref, wo_ref, upd_ref, ug_ref, local_sem, all_x, part, lin_sum, lin_total, own_part, listed, live, *scratch
):
    scratch = list(scratch)
    place = Place()
    gather = Gather(place, lists_ref, x_ref, all_x, take(scratch, len(Gather.scratch)))
    scatter = Scatter(place, lists_ref, take(scratch, len(Scatter.scratch)))
    lin = Total(place, part, lin_sum, take(scratch, len(Total.scratch)))
    d_lin = Total(place, own_part, lin_total, take(scratch, len(Total.scratch)))
    attention = Attention((wq_ref, wk_ref, wv_ref, wo_ref), scratch)

    arriving = [
        pltpu.make_async_copy(source, target, local_sem.at[k])
        for k, (source, target) in enumerate(
            (
                (user_hbm, user_ref), (wq_hbm, wq_ref), (cot_hbm, cot_ref), (wo_hbm, wo_ref),
                (wk_hbm, wk_ref), (wv_hbm, wv_ref),
            )
        )
    ]
    for copy in arriving:
        copy.start()
    greet(place)
    for tile in range(2):
        gather.first(0, tile)
        gather.cross(tile)
    total = lax.dot_general(
        proj_ref[...], x_ref[...], (((0,), (0,)), ((), ())), preferred_element_type=F32
    )
    for k in range(8):
        part[k] = total[k * 32 : k * 32 + 32].astype(BF16)
    lin.step(0)
    for copy in arriving:
        copy.wait()
    attention.prepare(user_ref, cot_ref)

    def before(i):
        if i == 0:
            gather.second(0)
            gather.relay()
        elif i == 1:
            lin.step(1)
            gather.third(0)
            for tile in range(2):
                gather.wait_cross(tile)
                gather.first(1, tile)
        elif i == 2:
            lin.step(2)
        elif i == 3:
            lin.step(3)
        elif i == 4:
            gather.second(1)
            lin.step(4)
        elif i == 5:
            lin.arrive(4)
        elif i == 6:
            gather.third(1)

    def forward_step(step, code):
        c = lax.rem(code, CHUNKS)
        for i, chunk in enumerate(FORWARD):

            @pl.when(step == i)
            def _():
                before(i)
                if chunk is None:
                    live[0], live[1] = jnp.int32(1), jnp.int32(1)
                    listed[...] = lin_sum[...].reshape(RANK, WIDTH)
                else:
                    rows, alive = gather.tiles(*chunk)
                    listed[...] = rows
                    live[0], live[1] = alive

        attention.keys(c, (listed[...],))
        attention.forward(c, live)
        return lax.div(code, CHUNKS)

    lax.fori_loop(0, CHUNKS, forward_step, jnp.int32(FORWARD_CODE))
    attention.settle()

    def after(i):
        if i == 8:
            scatter.send4(1)
        elif i == 7:
            scatter.send3(1)
        elif i == 6:
            scatter.send4(0)
        elif i == 5:
            scatter.send2(1)
        elif i == 4:
            d_lin.step(0)
        elif i == 3:
            scatter.send3(0)
        elif i == 2:
            scatter.send1(1)
            d_lin.step(1)
        elif i == 1:
            scatter.send2(0)
            d_lin.step(2)

    def backward_step(step, carry):
        c = CHUNKS - 1 - step
        attention.backward(c)
        scatter.grads[c] = attention.to_items(attention.dkv[...].astype(BF16))
        for i in range(CHUNKS - 1, 0, -1):

            @pl.when(c == i)
            def _():
                if i == LINFORMER:
                    g = scatter.grads[i] + attention.to_items(split(attention.dkv[...])[1])
                    for k in range(8):
                        own_part[k] = g[k * 32 : k * 32 + 32].astype(BF16)
                after(i)

        return carry

    lax.fori_loop(0, CHUNKS, backward_step, 0)
    lin.finish(range(5))
    gather.finish(range(6))
    gather.finish_cross()
    scatter.send_across()
    d_lin.step(3)
    upd_ref[...] = attention.updated()
    ug_ref[...] = attention.user_grad()
    leaving = [
        pltpu.make_async_copy(upd_ref, upd_hbm, local_sem.at[6]),
        pltpu.make_async_copy(ug_ref, ug_hbm, local_sem.at[7]),
    ]
    for copy in leaving:
        copy.start()
    scatter.send1(0)
    scatter.relay()
    d_lin.step(4)
    d_lin.finish(range(4))
    scatter.finish((0, 2, 3, 4))
    for copy in leaving:
        copy.wait()
    d_lin.arrive(4)
    back = dot(proj_ref[...], lin_total[...].reshape(RANK, WIDTH))
    for tile in range(2):
        value = back[tile * TILE : tile * TILE + TILE] + scatter.total(0, tile)
        scatter.wait_cross(tile)
        out_ref[tile * TILE : tile * TILE + TILE] = (value + scatter.z_in[tile].astype(F32)).astype(BF16)
    d_lin.finish((4,))
    scatter.finish((5, 6))
    scatter.finish_cross()


def finish_kernel(*refs):
    for k in range(3):
        refs[3 + k][...] = refs[k][...]


def in_vmem(count):
    return [pl.BlockSpec(memory_space=pltpu.VMEM)] * count


def anywhere(count):
    return [pl.BlockSpec(memory_space=pl.ANY)] * count


def per_device(user_x, item_x, lin_proj, tile_lists, w_q, w_k, w_v, w_o, cotangent):
    shape = jax.ShapeDtypeStruct
    sums = pltpu.VMEM((8, 32, WIDTH), BF16)
    users, weights = pltpu.VMEM((ROWS, WIDTH), BF16), pltpu.VMEM((WIDTH, WIDTH), BF16)
    results = pl.pallas_call(
        kernel,
        out_shape=[shape((ROWS, WIDTH), BF16)] * 3,
        in_specs=[pl.BlockSpec(memory_space=pltpu.SMEM)] + in_vmem(2) + anywhere(6),
        out_specs=anywhere(2) + in_vmem(1),
        scratch_shapes=[
            users, users, weights, weights, weights, weights, users, users,
            pltpu.SemaphoreType.DMA((8,)),
            pltpu.VMEM((OWNERS, ROWS, WIDTH), BF16),
            sums, sums, sums, sums,
            pltpu.VMEM((CHUNK, WIDTH), BF16),
            pltpu.SMEM((2,), jnp.int32),
        ] + Gather.scratch + Scatter.scratch + Total.scratch + Total.scratch + Attention.scratch,
        compiler_params=pltpu.CompilerParams(
            collective_id=0, has_side_effects=True, vmem_limit_bytes=VMEM_BYTES
        ),
        name="attend_and_exchange",
    )(tile_lists, item_x, lin_proj, user_x, cotangent, w_q, w_k, w_v, w_o)
    return pl.pallas_call(
        finish_kernel,
        out_shape=[shape((ROWS, WIDTH), BF16)] * 3,
        in_specs=in_vmem(3),
        out_specs=in_vmem(3),
        compiler_params=pltpu.CompilerParams(vmem_limit_bytes=VMEM_BYTES),
        name="finish",
    )(*results)


def solution(mesh):
    rows = P(("user", "item"), None)
    return jax.shard_map(
        per_device,
        mesh=mesh,
        in_specs=(rows, rows, rows, P("user", None), P(), P(), P(), P(), rows),
        out_specs=(rows, rows, rows),
        check_vma=False,
    )
```
